256 devices in a mesh: dp: 32 (over x, y, core), fsdp: 8 (over z).
Axes of the slice: x: 4, y: 4, z: 8, core: 2. Of those that a mesh axis runs over, the one named last changes fastest.
Arguments:
- events: bfloat16 [98304, 1024], P(('dp', 'fsdp')), may hold values from -6 to 6
- gain_in: float32 [1024], replicated, may hold values from 0.1 to 1.9
- gain_out: float32 [1024], replicated, may hold values from 0.1 to 1.9
- w_proj: bfloat16 [1024, 4096], P('fsdp'), may hold values from -0.1875 to 0.1875
- w_out: bfloat16 [1024, 1024], P('fsdp'), may hold values from -0.1875 to 0.1875
- target: int32 [8192], P(('dp', 'fsdp')), may hold values from 0 to 31, as said below
- segment: int32 [8192], P(('dp', 'fsdp')), may hold values from 0 to 3, as said below
- history: int32 [1024], P(('dp', 'fsdp')), may hold values from 1 to 348, as said below
- owners: int32 [1024], P(('dp', 'fsdp')), may hold values from 0 to 31, as said below
- pooled_cot: float32 [1024, 1024], P(('dp', 'fsdp')), may hold values from -6 to 6
Outputs:
- pooled: float32 [1024, 1024], P(('dp', 'fsdp'))
- grad_proj: float32 [1024, 4096], P('fsdp', 'dp')
- grad_out: float32 [1024, 1024], P('fsdp', 'dp')
The draws below stay inside these ranges and needn't reach their ends.
Inputs may be any that keep to these rules, and one draw needn't show every extreme that they name: target[i, j, b] = (i + s) mod 32, where s depends only on j and b and, for fixed j, takes each value 0 to 31 once over b. Along one device's 32 slots the segment never falls and takes every value. A user's history is more than 12 times (its slots - 1) and at most 12 times its slots. owners[i, j, u] = (i + s) mod 32, where s depends only on j and u and differs between the users of one device.
All inputs are finite; a program needn't handle non-finite values.
Results may differ from the reference program's by a relative error of at most 0.03.
Values may be sent and summed in bfloat16 or wider, within the bound.
A program may use at most 128 MiB of HBM per device.

```python
import math
import jax
import jax.numpy as jnp
from jax import lax

D = 1024
HEADS = 8
ROWS_DEV = 384
USERS_DEV = 4
TILE = 12
EVENTS = 98304
USERS = 1024
N_DP = 32
N_FSDP = 8
DEVICES = 256


def rotation_table(key, per_device):
    keys = jax.random.split(key, N_FSDP)
    orders = jax.vmap(lambda single: jax.random.permutation(single, N_DP))(keys)
    offsets = orders[:, :per_device].astype(jnp.int32)
    base = jnp.arange(N_DP, dtype=jnp.int32)
    return ((base[:, None, None] + offsets[None, :, :]) % N_DP).astype(jnp.int32).reshape(-1)


def user_segments(key):
    gaps = max(N_DP - 1, 0)
    gap_ids = jnp.arange(gaps, dtype=jnp.int32)[None, :]
    scores = jax.random.randint(key, (DEVICES, gaps), 0, 2 ** 20) * N_DP + gap_ids
    first_row = jnp.arange(DEVICES, dtype=jnp.int32)[:, None] == 0
    scores = jnp.where(first_row, gap_ids, scores).astype(jnp.int32)
    ranks = jnp.argsort(jnp.argsort(scores, axis=1), axis=1)
    cuts = (ranks < USERS_DEV - 1).astype(jnp.int32)
    leading = jnp.zeros((DEVICES, 1), jnp.int32)
    return jnp.concatenate([leading, jnp.cumsum(cuts, axis=1)], axis=1).astype(jnp.int32)


def draw_target(key, part):
    key = jax.random.fold_in(key, 11)
    return rotation_table(key, N_DP)


def draw_owners(key, part):
    key = jax.random.fold_in(key, 23)
    return rotation_table(key, USERS_DEV)


def draw_segment(key, part):
    segments = user_segments(key)
    return segments.reshape(-1)


def draw_history(key, part):
    segments = user_segments(key)
    key = jax.random.fold_in(key, 37)
    counts = jnp.sum((segments[:, :, None] == jnp.arange(USERS_DEV, dtype=jnp.int32)[None, None, :]).astype(jnp.int32), axis=1)
    trimmed = jax.random.randint(key, (DEVICES, USERS_DEV), 0, TILE)
    trimmed = trimmed.at[0, USERS_DEV - 1].set(0)
    return (TILE * counts - trimmed).astype(jnp.int32).reshape(-1)


def shard_levels(stream_key, shape, cuts, least, largest):
    loudness = 1.0
    for dim, shards_of in cuts:
        heights = jax.random.uniform(jax.random.fold_in(jax.random.fold_in(stream_key, 6), dim), (shards_of,), jnp.float32, least / len(cuts), largest / len(cuts))
        loudness = loudness * jnp.repeat(jnp.exp(heights), shape[dim] // shards_of).reshape((-1,) + (1,) * (len(shape) - 1 - dim))
    return loudness


def centred(own_key, dims, scale, most, cuts=(), kind=jnp.bfloat16):
    gain = shard_levels(own_key, dims, cuts, -0.22, 0.18) if cuts else 1.0
    entries = jax.random.normal(own_key, dims, jnp.float32) * scale * gain
    return jnp.minimum(jnp.maximum(entries, -most), most).astype(kind)


def setup_inputs(seed: int = 0) -> dict:
    arg_keys = jax.random.split(jax.random.key(seed), 11)
    events = centred(arg_keys[0], (EVENTS, D), 1.0, 6.0, ((0, 256),))
    gain_in = jnp.clip(1.0 + 0.18 * jax.random.normal(arg_keys[1], (D,), jnp.float32), 0.1, 1.9)
    gain_out = jnp.clip(1.0 + 0.18 * jax.random.normal(arg_keys[2], (D,), jnp.float32), 0.1, 1.9)
    w_proj = centred(arg_keys[3], (D, 4 * D), D ** -0.5, 0.1875, ((0, 8),))
    w_out = centred(arg_keys[4], (D, D), D ** -0.5, 0.1875, ((0, 8),))
    target = draw_target(jax.random.fold_in(arg_keys[10], 71), 0)
    segment = draw_segment(jax.random.fold_in(arg_keys[10], 71), 0)
    history = draw_history(jax.random.fold_in(arg_keys[10], 71), 0)
    owners = draw_owners(jax.random.fold_in(arg_keys[10], 71), 0)
    pooled_cot = centred(arg_keys[9], (USERS, D), 1.0, 6.0, ((0, 256),), jnp.float32)
    return {"events": events, "gain_in": gain_in, "gain_out": gain_out, "w_proj": w_proj, "w_out": w_out, "target": target, "segment": segment, "history": history, "owners": owners, "pooled_cot": pooled_cot}


def user_layout(segment, history, row_count):
    blocks = segment.shape[0]
    block_rows = row_count // blocks
    user_ids = jnp.arange(history.shape[0], dtype=jnp.int32)
    same_user = segment[:, None] == segment[None, :]
    earlier = jnp.arange(blocks, dtype=jnp.int32)[None, :] < jnp.arange(blocks, dtype=jnp.int32)[:, None]
    before = lax.optimization_barrier(jnp.sum((same_user & earlier).astype(jnp.int32), axis=1))
    offsets = jnp.arange(block_rows, dtype=jnp.int32)
    position = (before[:, None] * block_rows + offsets[None, :]).reshape(row_count)
    row_user = jnp.broadcast_to(segment[:, None], (blocks, block_rows)).reshape(row_count)
    member = row_user[:, None] == user_ids[None, :]
    limit = lax.optimization_barrier(jnp.sum(jnp.where(member, history[None, :], 0), axis=1))
    valid = position < limit
    return (row_user, position, valid, member)

def layer_pooled(arrived, proj_weight, out_weight, gain_in, gain_out, segment, history):
    row_count, features = arrived.shape
    head_size = features // HEADS
    row_user, position, valid, member = user_layout(segment, history, row_count)
    inputs = arrived.astype(jnp.float32)
    normed = (inputs * lax.rsqrt(lax.optimization_barrier(jnp.mean(inputs * inputs, axis=-1, keepdims=True)) + 1e-06) * gain_in).astype(jnp.bfloat16)
    activated = jax.nn.silu(jnp.dot(normed, proj_weight, preferred_element_type=jnp.float32)).astype(jnp.bfloat16)
    gate_part, value_part, query_part, key_part = jnp.split(activated, 4, axis=1)
    queries = query_part.reshape(row_count, HEADS, head_size).astype(jnp.float32)
    key_rows = key_part.reshape(row_count, HEADS, head_size).astype(jnp.float32)
    values = value_part.reshape(row_count, HEADS, head_size).astype(jnp.float32)
    scores = jnp.einsum('qhd,khd->hqk', queries, key_rows) / math.sqrt(head_size)
    allowed = (row_user[:, None] == row_user[None, :]) & (position[None, :] <= position[:, None]) & valid[None, :]
    attend = jnp.where(allowed[None], jax.nn.silu(scores), 0.0).astype(jnp.bfloat16)
    mixed = jnp.einsum('hqk,khd->qhd', attend.astype(jnp.float32), values).reshape(row_count, features)
    normed_mix = mixed * lax.rsqrt(lax.optimization_barrier(jnp.mean(mixed * mixed, axis=-1, keepdims=True)) + 1e-06) * gain_out
    gated = (normed_mix * gate_part.astype(jnp.float32)).astype(jnp.bfloat16)
    output = jnp.dot(gated, out_weight, preferred_element_type=jnp.float32) + inputs
    member_valid = (member & valid[:, None]).astype(jnp.float32)
    totals = jnp.dot(member_valid.T, output, precision=lax.Precision.HIGHEST)
    return totals / history.astype(jnp.float32)[:, None]

def reference(events, gain_in, gain_out, w_proj, w_out, target, segment, history, owners, pooled_cot):
    source_blocks = events.reshape(N_DP, N_FSDP, N_DP, TILE * D)
    routing = target.reshape(N_DP, N_FSDP, N_DP)
    dp_ids = jnp.arange(N_DP, dtype=jnp.int32)
    landing = (routing[:, None, :, :] == dp_ids[None, :, None, None]).astype(jnp.int32)
    source = lax.optimization_barrier(jnp.sum(landing * dp_ids[:, None, None, None], axis=0)).astype(jnp.int32)
    fsdp_ids = jnp.broadcast_to(jnp.arange(N_FSDP, dtype=jnp.int32)[None, :, None], source.shape)
    slot_ids = jnp.broadcast_to(jnp.arange(N_DP, dtype=jnp.int32)[None, None, :], source.shape)
    arrived = source_blocks[source, fsdp_ids, slot_ids].reshape(DEVICES, ROWS_DEV, D)
    segments = segment.reshape(DEVICES, N_DP)
    histories = history.reshape(DEVICES, USERS_DEV)
    owner_grid = owners.reshape(N_DP, N_FSDP, USERS_DEV)
    column_ids = jnp.broadcast_to(jnp.arange(N_FSDP, dtype=jnp.int32)[None, :, None], owner_grid.shape)
    user_ids = jnp.broadcast_to(jnp.arange(USERS_DEV, dtype=jnp.int32)[None, None, :], owner_grid.shape)
    slot_index = ((owner_grid * N_FSDP + column_ids) * USERS_DEV + user_ids).reshape(DEVICES, USERS_DEV).astype(jnp.int32)
    cot_rows = pooled_cot[slot_index]

    def device_step(totals, piece_in):
        rows_in, seg_dev, hist_dev, cot_dev = piece_in

        def local_fn(proj_weight, out_weight):
            return layer_pooled(rows_in, proj_weight, out_weight, gain_in, gain_out, seg_dev, hist_dev)
        user_mean, pullback = jax.vjp(local_fn, w_proj, w_out)
        grad_first, grad_second = pullback(cot_dev)
        return ((totals[0] + grad_first.astype(jnp.float32), totals[1] + grad_second.astype(jnp.float32)), user_mean)
    starting = (jnp.zeros((D, 4 * D), jnp.float32), jnp.zeros((D, D), jnp.float32))
    (grad_proj, grad_out), means = lax.scan(device_step, starting, (arrived, segments, histories, cot_rows))
    pooled = jnp.zeros((DEVICES * USERS_DEV, D), jnp.float32).at[slot_index.reshape(-1)].set(means.reshape(-1, D))
    return (pooled, grad_proj, grad_out)
```

```python
import math

import jax
import jax.numpy as jnp
from jax import lax
from jax.experimental import pallas as pl
from jax.experimental.pallas import tpu as pltpu
from jax.sharding import PartitionSpec as P

MESH = pl.DeviceIdType.MESH
BF16, F32, I32 = jnp.bfloat16, jnp.float32, jnp.int32

N_DP, N_Z = 32, 8
HEADS, HEAD = 8, 128
TILE = 12
BLOCK = 16
ROWS = 384
FEATURES = 1024
COLUMNS = 5120
PIECE = COLUMNS // 8
STRIPE = 160
Z_ROWS = 48


def dot(a, b, dims=((1,), (0,))):
    return lax.dot_general(a, b, (dims, ((), ())), preferred_element_type=F32)


def position():
    i, z = lax.axis_index("dp"), lax.axis_index("fsdp")
    return i, i // 8, (i // 2) % 4, i % 2, z


def send(src, dst, send_sem, recv_sem, device):
    copy = pltpu.make_async_remote_copy(
        src_ref=src,
        dst_ref=dst,
        send_sem=send_sem,
        recv_sem=recv_sem,
        device_id=device,
        device_id_type=MESH,
    )
    copy.start()
    return copy


def await_bytes(ref, sem):
    pltpu.make_async_copy(ref, ref, sem).wait()


def greet(i, z):
    barrier = pltpu.get_barrier_semaphore()

    def greet_dp(k, carry):
        pl.semaphore_signal(barrier, inc=1, device_id=((i + k) % N_DP, z), device_id_type=MESH)
        return carry

    def greet_z(k, carry):
        pl.semaphore_signal(barrier, inc=1, device_id=(i, (z + k) % N_Z), device_id_type=MESH)
        return carry

    lax.fori_loop(1, N_DP, greet_dp, 0)
    lax.fori_loop(1, N_Z, greet_z, 0)
    return barrier


def gather_kernel(
    target_ref,
    owners_ref,
    events_ref,
    cot_ref,
    proj_ref,
    out_ref,
    arrived_ref,
    cot_mine_ref,
    weights,
    outgoing,
    incoming,
    padded_cot,
    local_sem,
    tile_send,
    tile_recv,
    piece_send,
    piece_recv,
    ring_send,
    ring_recv,
    plane_send,
    plane_recv,
    twin_send,
    twin_recv,
):
    i, x, y, c, z = position()
    twin = (i + 1 - 2 * c, z)
    mine = pl.ds(64 * c, 64)
    load = [
        pltpu.make_async_copy(
            proj_ref.at[mine], weights.at[z, mine, pl.ds(0, 4096)], local_sem.at[0]
        ),
        pltpu.make_async_copy(
            out_ref.at[mine], weights.at[z, mine, pl.ds(4096, 1024)], local_sem.at[1]
        ),
    ]
    for copy in load:
        copy.start()

    lane = lax.broadcasted_iota(I32, (1, ROWS), 1)
    lane_slot, lane_row = lane // TILE, lane % TILE
    goes = jnp.zeros((1, ROWS), I32)
    comes = jnp.zeros((1, ROWS), I32)
    for b in range(N_DP):
        there = target_ref[b]
        goes = jnp.where(lane_slot == b, there, goes)
        comes = jnp.where(lane_slot == b, (2 * i - there + 2 * N_DP) % N_DP, comes)
    block_row = lax.broadcasted_iota(I32, (BLOCK * N_DP, ROWS), 0)
    place = (block_row == BLOCK * goes + lane_row).astype(BF16)
    user_lane = lax.broadcasted_iota(I32, (1, 128), 1)
    user_row = lax.broadcasted_iota(I32, (BLOCK, 1), 0)
    cot_goes = jnp.full((1, 128), -1, I32)
    cot_comes = jnp.full((BLOCK, 1), -1, I32)
    for u in range(4):
        owner = owners_ref[u]
        back = (2 * i - owner + 2 * N_DP) % N_DP
        cot_goes = jnp.where(user_lane == u, BLOCK * back + TILE + u, cot_goes)
        cot_comes = jnp.where(user_row == u, BLOCK * owner + TILE + u, cot_comes)
    cot_row = lax.broadcasted_iota(I32, (BLOCK * N_DP, 128), 0)
    cot_place = (cot_row == cot_goes).astype(BF16)
    padded_cot[...] = jnp.zeros_like(padded_cot)
    padded_cot[0:4, :] = cot_ref[...]
    for copy in load:
        copy.wait()
    barrier = greet(i, z)
    packed = dot(place, events_ref[...]) + dot(cot_place, padded_cot[...].astype(BF16))
    outgoing[...] = packed.astype(BF16).reshape(N_DP, BLOCK, FEATURES)

    pl.semaphore_wait(barrier, N_DP - 1 + N_Z - 1)

    sends = []

    def to_twin(ref):
        send(ref, ref, twin_send, twin_recv, twin)

    ring_row, plane_row = 64 * c, 64 * c + 32
    half_of_z = z // 4
    p = (1 - half_of_z) * (4 * x + y) + half_of_z * (4 * y + x)
    piece = weights.at[z, pl.ds(plane_row + 16 * (p // 8), 16), pl.ds(PIECE * (p % 8), PIECE)]

    def send_piece(k, carry):
        send(piece, piece, piece_send, piece_recv, (i, (z + k) % N_Z))
        return carry

    lax.fori_loop(1, N_Z, send_piece, 0)

    def ring_part(step, way):
        shard = (z - way * step + 2 * N_Z) % N_Z
        if step < 4:
            return weights.at[shard, pl.ds(ring_row, 32)]
        return weights.at[shard, pl.ds(ring_row + (0 if way > 0 else 16), 16)]

    def ring_step(step):
        for d, way in ((0, 1), (1, -1)):
            shard = (z - way * (step - 1) + 2 * N_Z) % N_Z
            if step < 4:
                part = weights.at[shard, pl.ds(ring_row, 32)]
            else:
                part = weights.at[shard, pl.ds(ring_row + (0 if way > 0 else 16), 16)]
            sends.append(
                send(
                    part,
                    part,
                    ring_send.at[step - 1, d],
                    ring_recv.at[step - 1, d],
                    (i, (z + way + N_Z) % N_Z),
                )
            )

    def ring_arrive(step):
        for d, way in ((0, 1), (1, -1)):
            await_bytes(ring_part(step, way), ring_recv.at[step - 1, d])

    def ring_to_twin(step):
        for d, way in ((0, 1), (1, -1)):
            to_twin(ring_part(step, way))

    ring_step(1)

    def send_tile(k, carry):
        there = (i + k) % N_DP
        send(outgoing.at[there], incoming.at[i], tile_send, tile_recv, (there, z))
        return carry

    lax.fori_loop(1, N_DP, send_tile, 0)
    incoming[i] = outgoing[i]
    to_twin(ring_part(0, 1))

    def plane_chunk(half, phase, place_on_axis, part):
        fast, slow = ((y, x), (x, y))[half]
        shards = pl.ds(4 * half + (2 if part == 1 else 0), 4 if part is None else 2)
        if phase == 0:
            row = plane_row + 16 * (slow // 2)
            column = PIECE * (4 * (slow % 2) + place_on_axis)
            return weights.at[shards, pl.ds(row, 16), pl.ds(column, PIECE)]
        row = plane_row + 16 * (place_on_axis // 2)
        column = 4 * PIECE * (place_on_axis % 2)
        return weights.at[shards, pl.ds(row, 16), pl.ds(column, 4 * PIECE)]

    def plane_axis(half, phase):
        along_y = (half == 0) == (phase == 0)
        here = y if along_y else x
        neighbours = []
        for way in (1, -1):
            there = (here + way + 4) % 4
            neighbours.append(8 * x + 2 * there + c if along_y else 8 * there + 2 * y + c)
        return here, neighbours

    def plane_step(phase, step):
        for half in range(2):
            here, neighbours = plane_axis(half, phase)
            for d, way in ((0, 1), (1, -1)):
                origin = (here - way * (step - 1) + 4) % 4
                part = plane_chunk(half, phase, origin, None if step == 1 else d)
                sends.append(
                    send(
                        part,
                        part,
                        plane_send.at[phase, step - 1, half, d],
                        plane_recv.at[phase, step - 1, half, d],
                        (neighbours[d], z),
                    )
                )

    def plane_arrive(phase, step):
        for half in range(2):
            here, _ = plane_axis(half, phase)
            for d, way in ((0, 1), (1, -1)):
                origin = (here - way * step + 4) % 4
                part = plane_chunk(half, phase, origin, None if step == 1 else d)
                await_bytes(part, plane_recv.at[phase, step - 1, half, d])

    def plane_to_twin(step):
        for half in range(2):
            here, _ = plane_axis(half, 1)
            if step == 0:
                to_twin(plane_chunk(half, 1, here, None))
                continue
            for d, way in ((0, 1), (1, -1)):
                origin = (here - way * step + 4) % 4
                to_twin(plane_chunk(half, 1, origin, None if step == 1 else d))

    pieces = weights.at[pl.ds(0, N_Z - 1), pl.ds(0, 16), pl.ds(0, PIECE)]
    await_bytes(pieces, piece_recv)
    plane_step(0, 1)
    plane_arrive(0, 1)
    plane_step(0, 2)
    plane_arrive(0, 2)
    plane_step(1, 1)
    plane_to_twin(0)
    ring_arrive(1)
    ring_step(2)
    ring_to_twin(1)

    await_bytes(incoming.at[pl.ds(0, N_DP - 1)], tile_recv)
    every = incoming[...].reshape(BLOCK * N_DP, FEATURES)
    fetch = (block_row == BLOCK * comes + lane_row).astype(BF16)
    arrived_ref[...] = dot(fetch, every, ((0,), (0,))).astype(BF16)
    cot_lane = lax.broadcasted_iota(I32, (BLOCK, BLOCK * N_DP), 1)
    cot_mine_ref[...] = dot((cot_lane == cot_comes).astype(BF16), every)

    ring_arrive(2)
    ring_step(3)
    ring_to_twin(2)
    plane_arrive(1, 1)
    plane_step(1, 2)
    plane_to_twin(1)
    ring_arrive(3)
    ring_step(4)
    ring_to_twin(3)
    plane_arrive(1, 2)
    plane_to_twin(2)
    ring_arrive(4)
    ring_to_twin(4)

    for copy in sends:
        copy.wait_send()
    await_bytes(pieces, piece_send)
    await_bytes(outgoing.at[pl.ds(0, N_DP - 1)], tile_send)
    await_bytes(weights.at[:, mine], twin_send)
    await_bytes(weights.at[:, pl.ds(64 * (1 - c), 64)], twin_recv)


def gather(target, owners, events, cot, w_proj, w_out):
    any_space, vmem = pl.BlockSpec(memory_space=pl.ANY), pl.BlockSpec(memory_space=pltpu.VMEM)
    smem = pl.BlockSpec(memory_space=pltpu.SMEM)
    dma = pltpu.SemaphoreType.DMA
    return pl.pallas_call(
        gather_kernel,
        out_shape=(
            jax.ShapeDtypeStruct((ROWS, FEATURES), BF16),
            jax.ShapeDtypeStruct((BLOCK, FEATURES), F32),
            jax.ShapeDtypeStruct((N_Z, 128, COLUMNS), BF16),
        ),
        in_specs=[smem, smem, vmem, vmem, any_space, any_space],
        out_specs=(vmem, vmem, any_space),
        scratch_shapes=[
            pltpu.VMEM((N_DP, BLOCK, FEATURES), BF16),
            pltpu.VMEM((N_DP, BLOCK, FEATURES), BF16),
            pltpu.VMEM((128, FEATURES), F32),
            dma((2,)),
            dma,
            dma,
            dma,
            dma,
            dma((4, 2)),
            dma((4, 2)),
            dma((2, 2, 2, 2)),
            dma((2, 2, 2, 2)),
            dma,
            dma,
        ],
        compiler_params=pltpu.CompilerParams(
            collective_id=0, has_side_effects=True, vmem_limit_bytes=60 * 2**20
        ),
        name="gather",
    )(target, owners, events, cot, w_proj, w_out)


def layer_kernel(
    segment_ref,
    history_ref,
    arrived_ref,
    cot_ref,
    gain_in_ref,
    gain_out_ref,
    w_gate,
    w_value,
    w_query,
    w_key,
    w_out_ref,
    grads_ref,
    mean_ref,
    normed,
    normed_t,
    act,
    act_slope,
    attend,
    attend_slope,
    mixed,
    mixed_cot,
    gate_cot,
    users,
    mask,
    grad_out_t,
    gated_cot,
):
    step = pl.program_id(0)
    scale = 1.0 / math.sqrt(HEAD)

    def spans():
        starts, ends = [], []
        for u in range(4):
            start = jnp.int32(0)
            for b in range(N_DP):
                start = start + jnp.where(segment_ref[b] < u, TILE, 0)
            starts.append(start)
            ends.append(start + history_ref[u])
        return starts, ends

    @pl.when(step == 0)
    def _():
        inputs = arrived_ref[...].astype(F32)
        power = jnp.mean(inputs * inputs, axis=-1, keepdims=True)
        rows = (inputs * lax.rsqrt(power + 1e-06) * gain_in_ref[...]).astype(BF16)
        normed[...] = rows
        normed_t[...] = rows.T
        starts, ends = spans()
        event = lax.broadcasted_iota(I32, (ROWS, 128), 0)
        lane = lax.broadcasted_iota(I32, (ROWS, 128), 1)
        owned = jnp.zeros((ROWS, 128), jnp.bool_)
        valid = jnp.zeros((ROWS, 128), jnp.bool_)
        for u in range(4):
            stop = starts[u + 1] if u < 3 else ROWS
            mine = (lane == u) & (event >= starts[u])
            owned = owned | (mine & (event < stop))
            valid = valid | (mine & (event < ends[u]))
        owned = owned.astype(F32).astype(BF16)
        valid = valid.astype(F32).astype(BF16)
        users[...] = valid
        same = dot(owned, valid, ((1,), (1,)))
        query = lax.broadcasted_iota(I32, (ROWS, ROWS), 0)
        key = lax.broadcasted_iota(I32, (ROWS, ROWS), 1)
        mask[...] = jnp.where(key <= query, same, 0.0)

    @pl.when(step < HEADS)
    def _():
        h = step
        weight = jnp.concatenate([w_gate[...], w_value[...], w_query[...], w_key[...]], axis=1)
        pre = dot(normed[...], weight)
        sig = 0.5 * jnp.tanh(0.5 * pre) + 0.5
        silu = pre * sig
        act_slope[h] = sig + silu * (1.0 - sig)
        act[h] = silu.astype(BF16)
        value = act[h, :, 128:256]
        query = act[h, :, 256:384]
        key = act[h, :, 384:512]
        scores = dot(query, key, ((1,), (1,))) * scale
        sig = 0.5 * jnp.tanh(0.5 * scores) + 0.5
        silu = scores * sig
        attend_slope[h] = (sig + silu * (1.0 - sig)) * (mask[...] * scale)
        attend[h] = (silu * mask[...]).astype(BF16)
        mixed[h] = dot(attend[h], value)

    @pl.when(step == HEADS)
    def _():
        starts, ends = spans()
        total = jnp.zeros((ROWS, 1), F32)
        for h in range(HEADS):
            total = total + jnp.sum(mixed[h] * mixed[h], axis=-1, keepdims=True)
        norm = lax.rsqrt(total * (1.0 / FEATURES) + 1e-06)
        row = lax.broadcasted_iota(I32, (8, 1), 0)
        length = jnp.ones((8, 1), F32)
        for u in range(4):
            length = jnp.where(row == u, history_ref[u].astype(F32), length)
        inverse = 1.0 / length
        event = lax.broadcasted_iota(I32, (BLOCK, ROWS), 1)
        user = lax.broadcasted_iota(I32, (BLOCK, ROWS), 0)
        valid_t = jnp.zeros((BLOCK, ROWS), jnp.bool_)
        for u in range(4):
            valid_t = valid_t | ((user == u) & (event >= starts[u]) & (event < ends[u]))
        valid_t = valid_t.astype(F32).astype(BF16)

        w_out = w_out_ref[...]
        cot = cot_ref[...]
        back = dot(cot.astype(BF16), w_out, ((1,), (1,)))[0:8] * inverse
        gated_cot[...] = jnp.zeros_like(gated_cot)
        gated_cot[0:8, :] = back
        pooled = []
        slope_total = jnp.zeros((ROWS, 1), F32)
        for h in range(HEADS):
            columns = slice(HEAD * h, HEAD * (h + 1))
            gain = gain_out_ref[:, columns]
            gate = act[h, :, 0:128].astype(F32)
            plain = mixed[h] * norm * gain
            gated = (plain * gate).astype(BF16)
            pooled.append(dot(valid_t, gated)[0:8])
            cot_rows = dot(users[...], gated_cot[:, columns].astype(BF16))
            gate_cot[h] = cot_rows * plain
            slope = cot_rows * gate * gain
            slope_total = slope_total + jnp.sum(slope * mixed[h], axis=-1, keepdims=True)
        shared = norm * norm * norm * slope_total * (1.0 / FEATURES)
        for h in range(HEADS):
            columns = slice(HEAD * h, HEAD * (h + 1))
            gain = gain_out_ref[:, columns]
            gate = act[h, :, 0:128].astype(F32)
            cot_rows = dot(users[...], gated_cot[:, columns].astype(BF16))
            slope = cot_rows * gate * gain
            mixed_cot[h] = (norm * slope - shared * mixed[h]).astype(BF16)

        pooled = jnp.concatenate(pooled, axis=1)
        high = pooled.astype(BF16).astype(F32)
        low = pooled - high
        both = jnp.concatenate([high, low], axis=0).astype(BF16)
        product = dot(both, w_out)
        summed = dot(valid_t, arrived_ref[...])[0:8]
        mean = (product[0:8] + product[8:16] + summed) * inverse
        mean_ref[...] = jnp.concatenate(
            [mean[0:4, 256 * k : 256 * (k + 1)] for k in range(4)], axis=0
        ).astype(BF16)

        share = cot[0:8] * inverse
        share_high = share.astype(BF16).astype(F32)
        share_low = share - share_high
        left = jnp.concatenate([share_high, share_low, share_high], axis=0).astype(BF16)
        right = jnp.concatenate([high, high, low], axis=0).astype(BF16)
        grad_out_t[...] = (
            dot(left, right, ((0,), (0,))).astype(BF16).reshape(N_DP, 32, FEATURES)
        )

    @pl.when(step >= HEADS)
    def _():
        h = step - HEADS
        value = act[h, :, 128:256]
        query = act[h, :, 256:384]
        key = act[h, :, 384:512]
        cot = mixed_cot[h]
        score_cot = (dot(cot, value, ((1,), (1,))) * attend_slope[h]).astype(BF16)
        value_cot = dot(attend[h], cot, ((0,), (0,)))
        query_cot = dot(score_cot, key)
        key_cot = dot(score_cot, query, ((0,), (0,)))
        act_cot = jnp.concatenate([gate_cot[h], value_cot, query_cot, key_cot], axis=1)
        pre_cot = (act_cot * act_slope[h]).astype(BF16)
        grad = dot(normed_t[...], pre_cot).astype(BF16)
        for part in range(4):
            columns = grad[:, 128 * part : 128 * (part + 1)]
            grads_ref[part, 0, :, 0:128, :] = columns.reshape(N_Z, 128, 128)
            for z in range(N_Z):
                grads_ref[part, 0, z, 128:STRIPE, :] = grad_out_t[
                    HEADS * part + h, :, 128 * z : 128 * (z + 1)
                ]


def layer(segment, history, arrived, cot, gain_in, gain_out, weights):
    smem = pl.BlockSpec(memory_space=pltpu.SMEM)

    def whole(shape):
        return pl.BlockSpec(shape, lambda s: (0,) * len(shape))

    def head_weight(part):
        return pl.BlockSpec(
            (FEATURES, 128), lambda s: (0, HEADS * part + jnp.minimum(s, HEADS - 1))
        )

    return pl.pallas_call(
        layer_kernel,
        grid=(2 * HEADS,),
        out_shape=(
            jax.ShapeDtypeStruct((4, HEADS, N_Z, STRIPE, 128), BF16),
            jax.ShapeDtypeStruct((16, 256), BF16),
        ),
        in_specs=[
            smem,
            smem,
            whole((ROWS, FEATURES)),
            whole((BLOCK, FEATURES)),
            whole((1, FEATURES)),
            whole((1, FEATURES)),
            head_weight(0),
            head_weight(1),
            head_weight(2),
            head_weight(3),
            pl.BlockSpec((FEATURES, FEATURES), lambda s: (0, 4)),
        ],
        out_specs=(
            pl.BlockSpec(
                (4, 1, N_Z, STRIPE, 128), lambda s: (0, jnp.maximum(s - HEADS, 0), 0, 0, 0)
            ),
            whole((16, 256)),
        ),
        scratch_shapes=[
            pltpu.VMEM((ROWS, FEATURES), BF16),
            pltpu.VMEM((FEATURES, ROWS), BF16),
            pltpu.VMEM((HEADS, ROWS, 512), BF16),
            pltpu.VMEM((HEADS, ROWS, 512), F32),
            pltpu.VMEM((HEADS, ROWS, ROWS), BF16),
            pltpu.VMEM((HEADS, ROWS, ROWS), F32),
            pltpu.VMEM((HEADS, ROWS, HEAD), F32),
            pltpu.VMEM((HEADS, ROWS, HEAD), BF16),
            pltpu.VMEM((HEADS, ROWS, HEAD), F32),
            pltpu.VMEM((ROWS, 128), BF16),
            pltpu.VMEM((ROWS, ROWS), F32),
            pltpu.VMEM((N_DP, 32, FEATURES), BF16),
            pltpu.VMEM((128, FEATURES), F32),
        ],
        compiler_params=pltpu.CompilerParams(
            dimension_semantics=("arbitrary",), vmem_limit_bytes=60 * 2**20
        ),
        name="layer",
    )(
        segment,
        history,
        arrived,
        cot,
        gain_in,
        gain_out,
        weights,
        weights,
        weights,
        weights,
        weights,
    )


def scatter_kernel(
    owners_ref,
    mean_ref,
    grads,
    pooled_ref,
    proj_ref,
    out_ref,
    held,
    other,
    means,
    z_in,
    plane_in_0,
    plane_in_1,
    last_z,
    last_plane,
    load_sem,
    twin_send,
    twin_recv,
    mean_send,
    mean_recv,
    ring_send,
    ring_recv,
    plane_send,
    plane_recv,
    last_send,
    last_recv,
):
    i, x, y, c, z = position()
    twin = (i + 1 - 2 * c, z)
    barrier = greet(i, z)
    top, rest = pl.ds(0, Z_ROWS), pl.ds(Z_ROWS, STRIPE - Z_ROWS)

    def ring_block(ref, place):
        return ref.at[:, :, place, top]

    def plane_block(ref, half, place):
        shards = pl.ds(4 * half, 4)
        if half == 0:
            return ref.at[place, :, shards, rest]
        return ref.at[:, place, shards, rest]

    parts = []
    for away in range(4, -1, -1):
        for way in (1, -1) if 0 < away < 4 else (1,):
            parts.append(("z", 0, away * way))
    for away in range(2, -1, -1):
        for way in (1, -1) if away == 1 else (1,):
            for half in range(2):
                parts.append(("p", half, away * way))

    def part_of(ref, part):
        kind, half, offset = part
        if kind == "z":
            return ring_block(ref, (z + offset + N_Z) % N_Z)
        return plane_block(ref, half, ((x, y)[half] + offset + 4) % 4)

    order = [q for q in parts if q[2] in (4,) and q[0] == "z"]
    order += [q for q in parts if q[0] == "p" and q[2] == 2]
    order += [q for q in parts if q[0] == "z" and abs(q[2]) == 3]
    order += [q for q in parts if q[0] == "p" and abs(q[2]) == 1]
    order += [q for q in parts if q[0] == "z" and abs(q[2]) == 2]
    order += [q for q in parts if q[0] == "z" and abs(q[2]) == 1]
    order += [q for q in parts if q[2] == 0]

    loads = {}
    for n, part in enumerate(order):
        loads[part] = pltpu.make_async_copy(
            part_of(grads.at[:, :, c], part), part_of(held, part), load_sem.at[n]
        )
        loads[part].start()
    pl.semaphore_wait(barrier, N_DP - 1 + N_Z - 1)
    twins = {}
    for n, part in enumerate(order):
        twins[part] = send(
            part_of(grads.at[:, :, 1 - c], part),
            part_of(other, part),
            twin_send.at[n],
            twin_recv.at[n],
            twin,
        )

    def send_mean(k, carry):
        send(mean_ref, means.at[i], mean_send, mean_recv, ((i + k) % N_DP, z))
        return carry

    lax.fori_loop(1, N_DP, send_mean, 0)
    means[i] = mean_ref[...]

    ready = set()

    def ready_part(part):
        if part in ready:
            return
        ready.add(part)
        loads[part].wait()
        twins[part].wait_recv()
        mine, theirs = part_of(held, part), part_of(other, part)
        mine[...] = mine[...] + theirs[...]

    sends = []

    def ring_step(step):
        for d, way in ((0, 1), (1, -1)):
            away = way * (5 - step)
            ready_part(("z", 0, 4 if step == 1 else away))
            chunk = ring_block(held, (z + away + N_Z) % N_Z)
            landing = z_in.at[d, step - 1]
            if step == 1:
                chunk = held.at[pl.ds(2 * d, 2), :, (z + away + N_Z) % N_Z, top]
                landing = z_in.at[d, 0, pl.ds(2 * d, 2)]
            sends.append(
                send(
                    chunk,
                    landing,
                    ring_send.at[step - 1, d],
                    ring_recv.at[step - 1, d],
                    (i, (z + way + N_Z) % N_Z),
                )
            )

    def ring_arrive(step):
        for d, way in ((0, 1), (1, -1)):
            away = way * (4 - step)
            ready_part(("z", 0, away))
            landing = z_in.at[d, step - 1]
            chunk = ring_block(held, (z + away + N_Z) % N_Z)
            if step == 1:
                landing = z_in.at[d, 0, pl.ds(2 * d, 2)]
                chunk = held.at[pl.ds(2 * d, 2), :, (z + away + N_Z) % N_Z, top]
            await_bytes(landing, ring_recv.at[step - 1, d])
            chunk[...] = chunk[...] + landing[...]

    def plane_axis(half, phase):
        along_x = (half == 0) == (phase == 0)
        here = x if along_x else y
        neighbours = []
        for way in (1, -1):
            there = (here + way + 4) % 4
            neighbours.append(8 * there + 2 * y + c if along_x else 8 * x + 2 * there + c)
        return here, neighbours

    def plane_chunk(half, phase, place, part):
        if phase == 0:
            shards = pl.ds(4 * half, 4)
            among = pl.ds(0, 4) if part is None else pl.ds(2 * part, 2)
            if half == 0:
                return held.at[place, among, shards, rest]
            return held.at[among, place, shards, rest]
        shards = pl.ds(4 * half, 4) if part is None else pl.ds(4 * half + 2 * part, 2)
        if half == 0:
            return held.at[x, place, shards, rest]
        return held.at[place, y, shards, rest]

    def plane_landing(half, phase, step, d):
        buffer = (plane_in_0, plane_in_1)[phase].at[half, step - 1, d]
        if step == 1:
            return buffer.at[pl.ds(2 * d, 2)]
        return buffer

    def plane_step(phase, step):
        for half in range(2):
            here, neighbours = plane_axis(half, phase)
            for d, way in ((0, 1), (1, -1)):
                away = way * (3 - step)
                if phase == 0:
                    ready_part(("p", half, 2 if step == 1 else away))
                chunk = plane_chunk(half, phase, (here + away + 4) % 4, d if step == 1 else None)
                sends.append(
                    send(
                        chunk,
                        plane_landing(half, phase, step, d),
                        plane_send.at[phase, step - 1, half, d],
                        plane_recv.at[phase, step - 1, half, d],
                        (neighbours[d], z),
                    )
                )

    def plane_arrive(phase, step):
        for half in range(2):
            here, _ = plane_axis(half, phase)
            for d, way in ((0, 1), (1, -1)):
                away = way * (2 - step)
                if phase == 0:
                    ready_part(("p", half, away))
                landing = plane_landing(half, phase, step, d)
                await_bytes(landing, plane_recv.at[phase, step - 1, half, d])
                chunk = plane_chunk(half, phase, (here + away + 4) % 4, d if step == 1 else None)
                chunk[...] = chunk[...] + landing[...]

    ring_step(1)
    plane_step(0, 1)
    ring_arrive(1)
    ring_step(2)
    plane_arrive(0, 1)
    plane_step(0, 2)
    ring_arrive(2)
    ring_step(3)

    await_bytes(means.at[pl.ds(0, N_DP - 1)], mean_recv)
    every = means[...].reshape(16 * N_DP, 256)
    lane = lax.broadcasted_iota(I32, (16, 16 * N_DP), 1)
    row = lax.broadcasted_iota(I32, (16, 1), 0)
    for k in range(4):
        wanted = jnp.full((16, 1), -1, I32)
        for u in range(4):
            source = (2 * i - owners_ref[u] + 2 * N_DP) % N_DP
            wanted = jnp.where(row == u, 16 * source + 4 * k + u, wanted)
        chosen = dot((lane == wanted).astype(BF16), every)
        pooled_ref[:, 256 * k : 256 * (k + 1)] = chosen[0:4]

    ring_arrive(3)
    ring_step(4)
    plane_arrive(0, 2)
    plane_step(1, 1)
    ring_arrive(4)

    def send_plane(k, carry):
        there = (i // 2 + k) % 16
        block = held.at[there // 4, there % 4, z, top]
        send(block, last_plane.at[i // 2], last_send.at[0], last_recv.at[0], (2 * there + c, z))
        return carry

    lax.fori_loop(1, 16, send_plane, 0)
    last_plane[i // 2] = held[x, y, z, 0:Z_ROWS]

    plane_arrive(1, 1)
    plane_step(1, 2)
    plane_arrive(1, 2)

    def send_z(k, carry):
        there = (z + k) % N_Z
        block = held.at[x, y, there, rest]
        send(block, last_z.at[z], last_send.at[1], last_recv.at[1], (i, there))
        return carry

    lax.fori_loop(1, N_Z, send_z, 0)
    last_z[z] = held[x, y, z, Z_ROWS:STRIPE]

    await_bytes(last_plane.at[pl.ds(0, 15)], last_recv.at[0])
    proj_ref[0:Z_ROWS, :] = jnp.sum(last_plane[...].astype(F32), axis=0)
    await_bytes(last_z.at[pl.ds(0, N_Z - 1)], last_recv.at[1])
    total = jnp.sum(last_z[...].astype(F32), axis=0)
    proj_ref[Z_ROWS:128, :] = total[0 : 128 - Z_ROWS]
    out_ref[...] = total[128 - Z_ROWS :]

    for part in order:
        twins[part].wait_send()
    for copy in sends:
        copy.wait_send()
    await_bytes(means.at[pl.ds(0, N_DP - 1)], mean_send)
    await_bytes(last_plane.at[pl.ds(0, 15)], last_send.at[0])
    await_bytes(last_z.at[pl.ds(0, N_Z - 1)], last_send.at[1])


def scatter(owners, mean, grads):
    any_space, vmem = pl.BlockSpec(memory_space=pl.ANY), pl.BlockSpec(memory_space=pltpu.VMEM)
    smem = pl.BlockSpec(memory_space=pltpu.SMEM)
    dma = pltpu.SemaphoreType.DMA
    low = STRIPE - Z_ROWS
    return pl.pallas_call(
        scatter_kernel,
        out_shape=(
            jax.ShapeDtypeStruct((4, FEATURES), F32),
            jax.ShapeDtypeStruct((128, 128), F32),
            jax.ShapeDtypeStruct((32, 128), F32),
        ),
        in_specs=[smem, vmem, any_space],
        out_specs=(vmem, vmem, vmem),
        scratch_shapes=[
            pltpu.VMEM((4, 4, N_Z, STRIPE, 128), BF16),
            pltpu.VMEM((4, 4, N_Z, STRIPE, 128), BF16),
            pltpu.VMEM((N_DP, 16, 256), BF16),
            pltpu.VMEM((2, 4, 4, 4, Z_ROWS, 128), BF16),
            pltpu.VMEM((2, 2, 2, 4, 4, low, 128), BF16),
            pltpu.VMEM((2, 2, 2, 4, low, 128), BF16),
            pltpu.VMEM((N_Z, low, 128), BF16),
            pltpu.VMEM((16, Z_ROWS, 128), BF16),
            dma((16,)),
            dma((16,)),
            dma((16,)),
            dma,
            dma,
            dma((4, 2)),
            dma((4, 2)),
            dma((2, 2, 2, 2)),
            dma((2, 2, 2, 2)),
            dma((2,)),
            dma((2,)),
        ],
        compiler_params=pltpu.CompilerParams(
            collective_id=1, has_side_effects=True, vmem_limit_bytes=60 * 2**20
        ),
        name="scatter",
    )(owners, mean, grads)


def body(events, gain_in, gain_out, w_proj, w_out, target, segment, history, owners, pooled_cot):
    arrived, cot, weights = gather(target, owners, events, pooled_cot, w_proj, w_out)
    grads, mean = layer(
        segment,
        history,
        arrived,
        cot,
        gain_in.reshape(1, FEATURES),
        gain_out.reshape(1, FEATURES),
        weights.reshape(FEATURES, COLUMNS),
    )
    pooled, grad_proj, grad_out_t = scatter(
        owners, mean, grads.reshape(4, 4, 2, N_Z, STRIPE, 128)
    )
    return (pooled, grad_proj, grad_out_t.T)


def solution(mesh):
    in_specs = (
        P(("dp", "fsdp"), None),
        P(),
        P(),
        P("fsdp", None),
        P("fsdp", None),
        P(("dp", "fsdp")),
        P(("dp", "fsdp")),
        P(("dp", "fsdp")),
        P(("dp", "fsdp")),
        P(("dp", "fsdp"), None),
    )
    out_specs = (P(("dp", "fsdp"), None), P("fsdp", "dp"), P("fsdp", "dp"))
    return jax.shard_map(body, mesh=mesh, in_specs=in_specs, out_specs=out_specs, check_vma=False)
```

```python
import math

import jax
import jax.numpy as jnp
from jax import lax
from jax.experimental import pallas as pl
from jax.experimental.pallas import tpu as pltpu
from jax.sharding import PartitionSpec as P

MESH = pl.DeviceIdType.MESH
BF16, F32, I32 = jnp.bfloat16, jnp.float32, jnp.int32

N_DP, N_Z = 32, 8
HEADS, HEAD = 8, 128
TILE = 12
BLOCK = 16
ROWS = 384
FEATURES = 1024
B_ROWS = 80
A_ROWS = 48
STRIPE = 160


def dot(a, b, dims=((1,), (0,)), precision=None):
    return lax.dot_general(
        a, b, (dims, ((), ())), precision=precision, preferred_element_type=F32
    )


def sigmoid(v):
    return 0.5 * jnp.tanh(0.5 * v) + 0.5


def send(src, dst, send_sem, recv_sem, device):
    copy = pltpu.make_async_remote_copy(
        src_ref=src,
        dst_ref=dst,
        send_sem=send_sem,
        recv_sem=recv_sem,
        device_id=device,
        device_id_type=MESH,
    )
    copy.start()
    return copy


def await_bytes(ref, sem):
    pltpu.make_async_copy(ref, ref, sem).wait()


def kernel(
    target_ref,
    owners_ref,
    segment_ref,
    history_ref,
    gain_in_ref,
    gain_out_ref,
    cot_ref,
    events_hbm,
    proj_hbm,
    out_hbm,
    pooled_ref,
    proj_ref,
    out_ref,
    events,
    w_out,
    outgoing,
    incoming,
    padded_cot,
    weights,
    arrived_sum,
    normed,
    normed_t,
    act,
    act_slope,
    attend,
    attend_slope,
    mixed,
    mixed_cot,
    gate_cot,
    users,
    users_t,
    mask,
    share,
    share_all,
    back,
    back_all,
    pool,
    pool_all,
    part,
    part_all,
    mean,
    mean_all,
    give,
    other,
    held,
    grad_out_t,
    other_out,
    z_in,
    plane_in_0,
    plane_in_1,
    last_z,
    last_plane,
    load_sem,
    tile_send,
    tile_recv,
    piece_send,
    piece_recv,
    ring_send,
    ring_recv,
    plane_send,
    plane_recv,
    twin_send,
    twin_recv,
    small_send,
    small_recv,
    give_send,
    give_recv,
    sum_z_send,
    sum_z_recv,
    sum_plane_send,
    sum_plane_recv,
    last_send,
    last_recv,
):
    i, z = lax.axis_index("dp"), lax.axis_index("fsdp")
    x, y, c = i // 8, (i // 2) % 4, i % 2
    twin = (i + 1 - 2 * c, z)
    mine = pl.ds(64 * c, 64)
    scale = 1.0 / math.sqrt(HEAD)

    load_events = pltpu.make_async_copy(events_hbm, events, load_sem.at[0])
    load_events.start()
    for n in range(4 * HEADS):
        pltpu.make_async_copy(
            proj_hbm.at[mine, pl.ds(128 * n, 128)],
            weights.at[n % HEADS, z, mine, pl.ds(128 * (n // HEADS), 128)],
            load_sem.at[1],
        ).start()
    load_out = pltpu.make_async_copy(out_hbm, w_out, load_sem.at[2])
    load_out.start()

    lane = lax.broadcasted_iota(I32, (1, ROWS), 1)
    lane_slot, lane_row = lane // TILE, lane % TILE
    goes = jnp.zeros((1, ROWS), I32)
    comes = jnp.zeros((1, ROWS), I32)
    for b in range(N_DP):
        there = target_ref[b]
        goes = jnp.where(lane_slot == b, there, goes)
        comes = jnp.where(lane_slot == b, (2 * i - there + 2 * N_DP) % N_DP, comes)
    block_row = lax.broadcasted_iota(I32, (BLOCK * N_DP, ROWS), 0)
    place = (block_row == BLOCK * goes + lane_row).astype(BF16)
    user_lane = lax.broadcasted_iota(I32, (1, 128), 1)
    user_row = lax.broadcasted_iota(I32, (BLOCK, 1), 0)
    cot_goes = jnp.full((1, 128), -1, I32)
    cot_comes = jnp.full((BLOCK, 1), -1, I32)
    inverse = jnp.ones((BLOCK, 1), F32)
    for u in range(4):
        owner = owners_ref[u]
        origin = (2 * i - owner + 2 * N_DP) % N_DP
        cot_goes = jnp.where(user_lane == u, BLOCK * origin + TILE + u, cot_goes)
        cot_comes = jnp.where(user_row == u, BLOCK * owner + TILE + u, cot_comes)
        inverse = jnp.where(user_row % 4 == u, history_ref[u].astype(F32), inverse)
    inverse = 1.0 / inverse
    cot_row = lax.broadcasted_iota(I32, (BLOCK * N_DP, 128), 0)
    cot_place = (cot_row == cot_goes).astype(BF16)
    padded_cot[...] = jnp.zeros_like(padded_cot)
    padded_cot[0:4, :] = cot_ref[...]

    await_bytes(weights.at[:, z, mine], load_sem.at[1])
    barrier = pltpu.get_barrier_semaphore()

    def greet_dp(k, carry):
        pl.semaphore_signal(barrier, inc=1, device_id=((i + k) % N_DP, z), device_id_type=MESH)
        return carry

    def greet_z(k, carry):
        pl.semaphore_signal(barrier, inc=1, device_id=(i, (z + k) % N_Z), device_id_type=MESH)
        return carry

    lax.fori_loop(1, N_DP, greet_dp, 0)
    lax.fori_loop(1, N_Z, greet_z, 0)

    load_events.wait()
    load_out.wait()
    packed = dot(place, events[...]) + dot(cot_place, padded_cot[...].astype(BF16))
    outgoing[...] = packed.astype(BF16).reshape(N_DP, BLOCK, FEATURES)
    pl.semaphore_wait(barrier, N_DP - 1 + N_Z - 1)

    sends = []

    def to_twin(ref):
        send(ref, ref, twin_send, twin_recv, twin)

    def along_z(make):
        def step(k, carry):
            make((z + k) % N_Z)
            return carry

        lax.fori_loop(1, N_Z, step, 0)

    ring_row, plane_row = 64 * c, 64 * c + 32
    half_of_z = z // 4
    p = (1 - half_of_z) * (4 * x + y) + half_of_z * (4 * y + x)
    piece = weights.at[p % 8, z, pl.ds(plane_row + 16 * (p // 8), 16)]
    along_z(lambda there: send(piece, piece, piece_send, piece_recv, (i, there)))

    def ring_part(step, way, group):
        shard = (z - way * step + 2 * N_Z) % N_Z
        rows = pl.ds(ring_row, 32) if step < 4 else pl.ds(ring_row + (0 if way > 0 else 16), 16)
        return weights.at[pl.ds(4 * group, 4), shard, rows]

    def ring_step(step, group):
        for d, way in ((0, 1), (1, -1)):
            shard = (z - way * (step - 1) + 2 * N_Z) % N_Z
            rows = (
                pl.ds(ring_row, 32) if step < 4 else pl.ds(ring_row + (0 if way > 0 else 16), 16)
            )
            ref = weights.at[pl.ds(4 * group, 4), shard, rows]
            sends.append(
                send(
                    ref,
                    ref,
                    ring_send.at[step - 1, group, d],
                    ring_recv.at[step - 1, group, d],
                    (i, (z + way + N_Z) % N_Z),
                )
            )

    def ring_arrive(step, group):
        for d, way in ((0, 1), (1, -1)):
            await_bytes(ring_part(step, way, group), ring_recv.at[step - 1, group, d])

    def ring_to_twin(step, group):
        for way in (1, -1):
            to_twin(ring_part(step, way, group))

    def ring_advance(step, group):
        ring_arrive(step, group)
        if step < 4:
            ring_step(step + 1, group)
        ring_to_twin(step, group)

    ring_step(1, 0)
    ring_step(1, 1)

    def send_tile(k, carry):
        there = (i + k) % N_DP
        send(outgoing.at[there], incoming.at[i], tile_send, tile_recv, (there, z))
        return carry

    lax.fori_loop(1, N_DP, send_tile, 0)
    incoming[i] = outgoing[i]
    for group in range(2):
        to_twin(ring_part(0, 1, group))

    def plane_chunk(half, phase, spot, only):
        slow = (x, y)[half]
        shards = pl.ds(4 * half + (2 if only == 1 else 0), 4 if only is None else 2)
        if phase == 0:
            return weights.at[
                4 * (slow % 2) + spot, shards, pl.ds(plane_row + 16 * (slow // 2), 16)
            ]
        return weights.at[
            pl.ds(4 * (spot % 2), 4), shards, pl.ds(plane_row + 16 * (spot // 2), 16)
        ]

    def plane_axis(along_y):
        here = y if along_y else x
        neighbours = []
        for way in (1, -1):
            there = (here + way + 4) % 4
            neighbours.append(8 * x + 2 * there + c if along_y else 8 * there + 2 * y + c)
        return here, neighbours

    def plane_step(phase, step):
        for half in range(2):
            here, neighbours = plane_axis((half == 0) == (phase == 0))
            for d, way in ((0, 1), (1, -1)):
                origin = (here - way * (step - 1) + 4) % 4
                ref = plane_chunk(half, phase, origin, None if step == 1 else d)
                sends.append(
                    send(
                        ref,
                        ref,
                        plane_send.at[phase, step - 1, half, d],
                        plane_recv.at[phase, step - 1, half, d],
                        (neighbours[d], z),
                    )
                )

    def plane_arrive(phase, step):
        for half in range(2):
            here, _ = plane_axis((half == 0) == (phase == 0))
            for d, way in ((0, 1), (1, -1)):
                origin = (here - way * step + 4) % 4
                ref = plane_chunk(half, phase, origin, None if step == 1 else d)
                await_bytes(ref, plane_recv.at[phase, step - 1, half, d])

    def plane_to_twin(step):
        for half in range(2):
            here, _ = plane_axis(half == 1)
            if step == 0:
                to_twin(plane_chunk(half, 1, here, None))
                continue
            for d, way in ((0, 1), (1, -1)):
                origin = (here - way * step + 4) % 4
                to_twin(plane_chunk(half, 1, origin, None if step == 1 else d))

    pieces = weights.at[0, pl.ds(0, N_Z - 1), pl.ds(0, 16)]
    await_bytes(pieces, piece_recv)
    plane_step(0, 1)
    ring_advance(1, 0)
    plane_arrive(0, 1)
    plane_step(0, 2)
    ring_advance(1, 1)
    plane_arrive(0, 2)
    plane_step(1, 1)
    plane_to_twin(0)
    ring_advance(2, 0)

    await_bytes(incoming.at[pl.ds(0, N_DP - 1)], tile_recv)
    every = incoming[...].reshape(BLOCK * N_DP, FEATURES)
    fetch = (block_row == BLOCK * comes + lane_row).astype(BF16)
    arrived = dot(fetch, every, ((0,), (0,)))
    cot_lane = lax.broadcasted_iota(I32, (BLOCK, BLOCK * N_DP), 1)
    cot_mine = dot((cot_lane == cot_comes).astype(BF16), every)

    def pack(rows):
        return jnp.concatenate([rows[0:4, 256 * k : 256 * (k + 1)] for k in range(4)], axis=0)

    share[...] = (pack(cot_mine) * inverse).astype(BF16)
    share_all[z] = share[...]
    along_z(
        lambda there: send(share, share_all.at[z], small_send.at[0], small_recv.at[0], (i, there))
    )
    ring_advance(2, 1)

    power = jnp.mean(arrived * arrived, axis=-1, keepdims=True)
    rows = (arrived * lax.rsqrt(power + 1e-06) * gain_in_ref[...]).astype(BF16)
    normed[...] = rows
    normed_t[...] = rows.T

    starts, ends = [], []
    for u in range(4):
        start = jnp.int32(0)
        for b in range(N_DP):
            start = start + jnp.where(segment_ref[b] < u, TILE, 0)
        starts.append(start)
        ends.append(start + history_ref[u])

    def members(event, user, stops):
        found = jnp.zeros(event.shape, jnp.bool_)
        for u in range(4):
            found = found | ((user == u) & (event >= starts[u]) & (event < stops[u]))
        return found.astype(F32).astype(BF16)

    event = lax.broadcasted_iota(I32, (ROWS, 128), 0)
    user = lax.broadcasted_iota(I32, (ROWS, 128), 1)
    owned = members(event, user, starts[1:] + [ROWS])
    valid = members(event, user, ends)
    users[...] = valid
    users_t[...] = members(
        lax.broadcasted_iota(I32, (BLOCK, ROWS), 1),
        lax.broadcasted_iota(I32, (BLOCK, ROWS), 0),
        ends,
    )
    same = dot(owned, valid, ((1,), (1,)))
    query_row = lax.broadcasted_iota(I32, (ROWS, ROWS), 0)
    key_row = lax.broadcasted_iota(I32, (ROWS, ROWS), 1)
    mask[...] = jnp.where(key_row <= query_row, same, 0.0)
    arrived_sum[...] = pack(dot(users_t[...], arrived.astype(BF16)))

    plane_arrive(1, 1)
    plane_step(1, 2)
    plane_to_twin(1)
    ring_advance(3, 0)

    await_bytes(share_all.at[pl.ds(0, N_Z - 1)], small_recv.at[0])
    shares = share_all[...].reshape(16 * N_Z, 256)
    quarter = (lax.broadcasted_iota(I32, (16 * N_Z, 1), 0) % 16) // 4
    partial = jnp.zeros((16 * N_Z, 128), F32)
    for k in range(4):
        product = dot(shares, w_out[:, 256 * k : 256 * (k + 1)], ((1,), (1,)))
        partial = partial + jnp.where(quarter == k, product, 0.0)
    fold_row = lax.broadcasted_iota(I32, (16 * N_Z, 16 * N_Z), 0)
    fold_column = lax.broadcasted_iota(I32, (16 * N_Z, 16 * N_Z), 1)
    fold = (fold_row // 16 == fold_column // 16) & (fold_row % 4 == fold_column % 4)
    folded = dot(fold.astype(F32), partial, precision=lax.Precision.HIGHEST)
    back[...] = folded.astype(BF16).reshape(N_Z, 16, 128)
    back_all[z] = back[z]
    along_z(
        lambda there: send(
            back.at[there], back_all.at[z], small_send.at[1], small_recv.at[1], (i, there)
        )
    )

    ring_advance(3, 1)
    ring_advance(4, 0)
    plane_arrive(1, 2)
    plane_to_twin(2)
    ring_advance(4, 1)
    await_bytes(weights.at[:, :, pl.ds(64 * (1 - c), 64)], twin_recv)

    def forward(h, carry):
        pre = dot(normed[...], weights[h].reshape(FEATURES, 4 * HEAD))
        sig = sigmoid(pre)
        silu = pre * sig
        act_slope[h] = sig + silu * (1.0 - sig)
        act[h] = silu.astype(BF16)
        value = act[h, :, 128:256]
        query = act[h, :, 256:384]
        key = act[h, :, 384:512]
        scores = dot(query, key, ((1,), (1,))) * scale
        sig = sigmoid(scores)
        silu = scores * sig
        attend_slope[h] = (sig + silu * (1.0 - sig)) * (mask[...] * scale)
        attend[h] = (silu * mask[...]).astype(BF16)
        mixed[h] = dot(attend[h], value)
        return carry

    lax.fori_loop(0, HEADS, forward, 0)

    await_bytes(back_all.at[pl.ds(0, N_Z - 1)], small_recv.at[1])
    total = jnp.zeros((ROWS, 1), F32)
    for h in range(HEADS):
        total = total + jnp.sum(mixed[h] * mixed[h], axis=-1, keepdims=True)
    norm = lax.rsqrt(total * (1.0 / FEATURES) + 1e-06)
    slope_total = jnp.zeros((ROWS, 1), F32)
    for h in range(HEADS):
        gain = gain_out_ref[:, HEAD * h : HEAD * (h + 1)]
        gate = act[h, :, 0:128].astype(F32)
        plain = mixed[h] * norm * gain
        pool[h] = dot(users_t[...], (plain * gate).astype(BF16))[0:8]
        cot_rows = dot(users[:, 0:16], back_all[h])
        gate_cot[h] = cot_rows * plain
        slope_total = slope_total + jnp.sum(cot_rows * gate * gain * mixed[h], axis=-1, keepdims=True)
    pool_all[z] = pool[z]
    along_z(
        lambda there: send(
            pool.at[there], pool_all.at[z], small_send.at[2], small_recv.at[2], (i, there)
        )
    )
    shared = norm * norm * norm * slope_total * (1.0 / FEATURES)
    for h in range(HEADS):
        gain = gain_out_ref[:, HEAD * h : HEAD * (h + 1)]
        gate = act[h, :, 0:128].astype(F32)
        cot_rows = dot(users[:, 0:16], back_all[h])
        mixed_cot[h] = (norm * (cot_rows * gate * gain) - shared * mixed[h]).astype(BF16)

    def backward(h):
        value = act[h, :, 128:256]
        query = act[h, :, 256:384]
        key = act[h, :, 384:512]
        cot = mixed_cot[h]
        score_cot = (dot(cot, value, ((1,), (1,))) * attend_slope[h]).astype(BF16)
        value_cot = dot(attend[h], cot, ((0,), (0,)))
        query_cot = dot(score_cot, key)
        key_cot = dot(score_cot, query, ((0,), (0,)))
        act_cot = jnp.concatenate([gate_cot[h], value_cot, query_cot, key_cot], axis=1)
        pre_cot = (act_cot * act_slope[h]).astype(BF16)
        return dot(normed_t[...], pre_cot)

    def backward_other(k, carry):
        spot = (y + 2 + 3 * k) % 4
        grad = backward(2 * spot + 1 - c).astype(BF16)
        for b in range(4):
            give[b, spot] = grad[:, 128 * b : 128 * (b + 1)].reshape(N_Z, 128, 128)
        send(give.at[:, spot], other.at[:, spot], give_send.at[k], give_recv.at[k], twin)
        return carry

    lax.fori_loop(0, 4, backward_other, 0)

    await_bytes(pool_all.at[pl.ds(0, N_Z - 1)], small_recv.at[2])
    pooled = pool_all[...]
    flat = pooled.reshape(8 * N_Z, 128)
    high = flat.astype(BF16).astype(F32)
    both = dot(jnp.concatenate([high, flat - high], axis=0).astype(BF16), w_out[...])
    products = (both[0 : 8 * N_Z] + both[8 * N_Z :]).reshape(N_Z, 8, FEATURES)
    part[...] = jnp.concatenate(
        [products[:, 0:4, 256 * k : 256 * (k + 1)] for k in range(4)], axis=1
    ).astype(BF16)
    part_all[z] = part[z]
    along_z(
        lambda there: send(
            part.at[there], part_all.at[z], small_send.at[3], small_recv.at[3], (i, there)
        )
    )
    spread = jnp.concatenate([pooled[:, 0:4]] * 4, axis=1).reshape(16 * N_Z, 128)
    for k in range(4):
        block = dot(
            share_all[...].reshape(16 * N_Z, 256),
            jnp.where(quarter == k, spread, 0.0).astype(BF16),
            ((0,), (0,)),
        )
        grad_out_t[4 * k : 4 * (k + 1)] = block.astype(BF16).reshape(4, 2, 32, 128)
    copy_out = send(grad_out_t.at[:, 1 - c], other_out, give_send.at[4], give_recv.at[4], twin)

    def backward_mine(k, carry):
        spot = (y + 2 + 3 * k) % 4
        grad = backward(2 * spot + c)
        await_bytes(other.at[:, spot], give_recv.at[k])
        for b in range(4):
            held[b, spot, :, 0:128, :] = (
                grad[:, 128 * b : 128 * (b + 1)].reshape(N_Z, 128, 128)
                + other[b, spot].astype(F32)
            ).astype(BF16)
        return carry

    lax.fori_loop(0, 4, backward_mine, 0)

    first_rows, z_rows = pl.ds(0, B_ROWS), pl.ds(B_ROWS, A_ROWS)
    last_rows = pl.ds(B_ROWS, STRIPE - B_ROWS)

    def sum_z_chunk(away, d, half):
        if half:
            return held.at[pl.ds(2 * d, 2), :, (z + away + N_Z) % N_Z, z_rows]
        return held.at[:, :, (z + away + N_Z) % N_Z, z_rows]

    def sum_z_landing(step, d):
        if step == 1:
            return z_in.at[d, 0, pl.ds(2 * d, 2)]
        return z_in.at[d, step - 1]

    def sum_z_step(step):
        for d, way in ((0, 1), (1, -1)):
            sends.append(
                send(
                    sum_z_chunk(way * (5 - step), d, step == 1),
                    sum_z_landing(step, d),
                    sum_z_send.at[step - 1, d],
                    sum_z_recv.at[step - 1, d],
                    (i, (z + way + N_Z) % N_Z),
                )
            )

    def sum_z_arrive(step):
        for d, way in ((0, 1), (1, -1)):
            landing = sum_z_landing(step, d)
            await_bytes(landing, sum_z_recv.at[step - 1, d])
            chunk = sum_z_chunk(way * (4 - step), d, step == 1)
            chunk[...] = chunk[...] + landing[...]

    def sum_plane_chunk(half, phase, spot, d):
        if phase == 0:
            shards = pl.ds(4 * half, 4)
            among = pl.ds(0, 4) if d is None else pl.ds(2 * d, 2)
            if half == 0:
                return held.at[spot, among, shards, first_rows]
            return held.at[among, spot, shards, first_rows]
        shards = pl.ds(4 * half, 4) if d is None else pl.ds(4 * half + 2 * d, 2)
        if half == 0:
            return held.at[x, spot, shards, first_rows]
        return held.at[spot, y, shards, first_rows]

    def sum_plane_landing(half, phase, step, d):
        buffer = (plane_in_0, plane_in_1)[phase].at[half, step - 1, d]
        return buffer.at[pl.ds(2 * d, 2)] if step == 1 else buffer

    def sum_plane_step(phase, step):
        for half in range(2):
            here, neighbours = plane_axis((half == 1) == (phase == 0))
            for d, way in ((0, 1), (1, -1)):
                spot = (here + way * (3 - step) + 4) % 4
                sends.append(
                    send(
                        sum_plane_chunk(half, phase, spot, d if step == 1 else None),
                        sum_plane_landing(half, phase, step, d),
                        sum_plane_send.at[phase, step - 1, half, d],
                        sum_plane_recv.at[phase, step - 1, half, d],
                        (neighbours[d], z),
                    )
                )

    def sum_plane_arrive(phase, step):
        for half in range(2):
            here, _ = plane_axis((half == 1) == (phase == 0))
            for d, way in ((0, 1), (1, -1)):
                landing = sum_plane_landing(half, phase, step, d)
                await_bytes(landing, sum_plane_recv.at[phase, step - 1, half, d])
                spot = (here + way * (2 - step) + 4) % 4
                chunk = sum_plane_chunk(half, phase, spot, d if step == 1 else None)
                chunk[...] = chunk[...] + landing[...]

    sum_z_step(1)
    sum_plane_step(0, 1)

    await_bytes(part_all.at[pl.ds(0, N_Z - 1)], small_recv.at[3])
    mean[...] = (
        (jnp.sum(part_all[...].astype(F32), axis=0) + arrived_sum[...]) * inverse
    ).astype(BF16)
    mean_all[i] = mean[...]

    def send_mean(k, carry):
        send(mean, mean_all.at[i], small_send.at[4], small_recv.at[4], ((i + k) % N_DP, z))
        return carry

    lax.fori_loop(1, N_DP, send_mean, 0)
    await_bytes(other_out, give_recv.at[4])
    held[:, :, z, 128:STRIPE, :] = (grad_out_t[:, c] + other_out[...]).reshape(4, 4, 32, 128)

    sum_z_arrive(1)
    sum_z_step(2)
    sum_plane_arrive(0, 1)
    sum_plane_step(0, 2)
    sum_z_arrive(2)
    sum_z_step(3)
    sum_z_arrive(3)
    sum_z_step(4)
    sum_plane_arrive(0, 2)
    sum_plane_step(1, 1)
    sum_z_arrive(4)

    def send_plane(k, carry):
        there = (i // 2 + k) % 16
        block = held.at[there // 4, there % 4, z, last_rows]
        send(block, last_plane.at[i // 2], last_send.at[0], last_recv.at[0], (2 * there + c, z))
        return carry

    lax.fori_loop(1, 16, send_plane, 0)
    last_plane[i // 2] = held[x, y, z, B_ROWS:STRIPE]

    sum_plane_arrive(1, 1)
    sum_plane_step(1, 2)

    await_bytes(mean_all.at[pl.ds(0, N_DP - 1)], small_recv.at[4])
    means = mean_all[...].reshape(16 * N_DP, 256)
    mean_lane = lax.broadcasted_iota(I32, (16, 16 * N_DP), 1)
    for k in range(4):
        wanted = jnp.full((16, 1), -1, I32)
        for u in range(4):
            source = (2 * i - owners_ref[u] + 2 * N_DP) % N_DP
            wanted = jnp.where(user_row == u, 16 * source + 4 * k + u, wanted)
        chosen = dot((mean_lane == wanted).astype(BF16), means)
        pooled_ref[:, 256 * k : 256 * (k + 1)] = chosen[0:4]

    sum_plane_arrive(1, 2)

    along_z(
        lambda there: send(
            held.at[x, y, there, first_rows],
            last_z.at[z],
            last_send.at[1],
            last_recv.at[1],
            (i, there),
        )
    )
    last_z[z] = held[x, y, z, 0:B_ROWS]

    await_bytes(last_plane.at[pl.ds(0, 15)], last_recv.at[0])
    rest = jnp.sum(last_plane[...].astype(F32), axis=0)
    proj_ref[B_ROWS:128, :] = rest[0:A_ROWS]
    out_ref[...] = rest[A_ROWS:]
    await_bytes(last_z.at[pl.ds(0, N_Z - 1)], last_recv.at[1])
    proj_ref[0:B_ROWS, :] = jnp.sum(last_z[...].astype(F32), axis=0)

    for copy in sends:
        copy.wait_send()
    copy_out.wait_send()
    for k in range(4):
        await_bytes(give.at[:, 0], give_send.at[k])
    await_bytes(pieces, piece_send)
    await_bytes(outgoing.at[pl.ds(0, N_DP - 1)], tile_send)
    await_bytes(weights.at[:, :, mine], twin_send)
    await_bytes(share_all.at[pl.ds(0, N_Z - 1)], small_send.at[0])
    await_bytes(back.at[pl.ds(0, N_Z - 1)], small_send.at[1])
    await_bytes(pool.at[pl.ds(0, N_Z - 1)], small_send.at[2])
    await_bytes(part.at[pl.ds(0, N_Z - 1)], small_send.at[3])
    await_bytes(mean_all.at[pl.ds(0, N_DP - 1)], small_send.at[4])
    await_bytes(last_plane.at[pl.ds(0, 15)], last_send.at[0])
    await_bytes(last_z.at[pl.ds(0, N_Z - 1)], last_send.at[1])


def finish_kernel(pooled_in, proj_in, out_in, pooled_ref, proj_ref, out_ref):
    pooled_ref[...] = pooled_in[...]
    proj_ref[...] = proj_in[...]
    out_ref[...] = out_in[...]


def body(events, gain_in, gain_out, w_proj, w_out, target, segment, history, owners, pooled_cot):
    any_space, vmem = pl.BlockSpec(memory_space=pl.ANY), pl.BlockSpec(memory_space=pltpu.VMEM)
    smem = pl.BlockSpec(memory_space=pltpu.SMEM)
    dma = pltpu.SemaphoreType.DMA

    def bf16(*shape):
        return pltpu.VMEM(shape, BF16)

    def f32(*shape):
        return pltpu.VMEM(shape, F32)

    pooled, grad_proj, grad_out_t = pl.pallas_call(
        kernel,
        out_shape=(
            jax.ShapeDtypeStruct((4, FEATURES), F32),
            jax.ShapeDtypeStruct((128, 128), F32),
            jax.ShapeDtypeStruct((32, 128), F32),
        ),
        in_specs=[smem] * 4 + [vmem] * 3 + [any_space] * 3,
        out_specs=(vmem, vmem, vmem),
        scratch_shapes=[
            bf16(ROWS, FEATURES),
            bf16(128, FEATURES),
            bf16(N_DP, BLOCK, FEATURES),
            bf16(N_DP, BLOCK, FEATURES),
            f32(128, FEATURES),
            bf16(HEADS, N_Z, 128, 4 * HEAD),
            f32(16, 256),
            bf16(ROWS, FEATURES),
            bf16(FEATURES, ROWS),
            bf16(HEADS, ROWS, 4 * HEAD),
            f32(HEADS, ROWS, 4 * HEAD),
            bf16(HEADS, ROWS, ROWS),
            f32(HEADS, ROWS, ROWS),
            f32(HEADS, ROWS, HEAD),
            bf16(HEADS, ROWS, HEAD),
            f32(HEADS, ROWS, HEAD),
            bf16(ROWS, 128),
            bf16(BLOCK, ROWS),
            f32(ROWS, ROWS),
            bf16(16, 256),
            bf16(N_Z, 16, 256),
            bf16(N_Z, 16, 128),
            bf16(N_Z, 16, 128),
            f32(N_Z, 8, 128),
            f32(N_Z, 8, 128),
            bf16(N_Z, 16, 256),
            bf16(N_Z, 16, 256),
            bf16(16, 256),
            bf16(N_DP, 16, 256),
            bf16(4, 4, N_Z, 128, 128),
            bf16(4, 4, N_Z, 128, 128),
            bf16(4, 4, N_Z, STRIPE, 128),
            bf16(16, 2, 32, 128),
            bf16(16, 32, 128),
            bf16(2, 4, 4, 4, A_ROWS, 128),
            bf16(2, 2, 2, 4, 4, B_ROWS, 128),
            bf16(2, 2, 2, 4, B_ROWS, 128),
            bf16(N_Z, B_ROWS, 128),
            bf16(16, STRIPE - B_ROWS, 128),
            dma((3,)),
            dma,
            dma,
            dma,
            dma,
            dma((4, 2, 2)),
            dma((4, 2, 2)),
            dma((2, 2, 2, 2)),
            dma((2, 2, 2, 2)),
            dma,
            dma,
            dma((5,)),
            dma((5,)),
            dma((5,)),
            dma((5,)),
            dma((4, 2)),
            dma((4, 2)),
            dma((2, 2, 2, 2)),
            dma((2, 2, 2, 2)),
            dma((2,)),
            dma((2,)),
        ],
        compiler_params=pltpu.CompilerParams(
            collective_id=0, has_side_effects=True, vmem_limit_bytes=62 * 2**20
        ),
        name="step",
    )(
        target,
        owners,
        segment,
        history,
        gain_in.reshape(1, FEATURES),
        gain_out.reshape(1, FEATURES),
        pooled_cot,
        events,
        w_proj,
        w_out,
    )
    pooled, grad_proj, grad_out_t = pl.pallas_call(
        finish_kernel,
        out_shape=(
            jax.ShapeDtypeStruct((4, FEATURES), F32),
            jax.ShapeDtypeStruct((128, 128), F32),
            jax.ShapeDtypeStruct((32, 128), F32),
        ),
        in_specs=[vmem] * 3,
        out_specs=(vmem, vmem, vmem),
        name="finish",
    )(pooled, grad_proj, grad_out_t)
    return (pooled, grad_proj, grad_out_t.T)


def solution(mesh):
    in_specs = (
        P(("dp", "fsdp"), None),
        P(),
        P(),
        P("fsdp", None),
        P("fsdp", None),
        P(("dp", "fsdp")),
        P(("dp", "fsdp")),
        P(("dp", "fsdp")),
        P(("dp", "fsdp")),
        P(("dp", "fsdp"), None),
    )
    out_specs = (P(("dp", "fsdp"), None), P("fsdp", "dp"), P("fsdp", "dp"))
    return jax.shard_map(body, mesh=mesh, in_specs=in_specs, out_specs=out_specs, check_vma=False)
```

```python
import math

import jax
import jax.numpy as jnp
from jax import lax
from jax.experimental import pallas as pl
from jax.experimental.pallas import tpu as pltpu
from jax.sharding import PartitionSpec as P

MESH = pl.DeviceIdType.MESH
BF16, F32, I32 = jnp.bfloat16, jnp.float32, jnp.int32

N_DP, N_Z = 32, 8
HEADS, HEAD = 8, 128
TILE = 12
BLOCK = 16
ROWS = 384
FEATURES = 1024
B_ROWS = 80
A_ROWS = 48
STRIPE = 160


def dot(a, b, dims=((1,), (0,)), precision=None):
    return lax.dot_general(
        a, b, (dims, ((), ())), precision=precision, preferred_element_type=F32
    )


def sigmoid(v):
    return 0.5 * jnp.tanh(0.5 * v) + 0.5


def send(src, dst, send_sem, recv_sem, device):
    copy = pltpu.make_async_remote_copy(
        src_ref=src,
        dst_ref=dst,
        send_sem=send_sem,
        recv_sem=recv_sem,
        device_id=device,
        device_id_type=MESH,
    )
    copy.start()
    return copy


def await_bytes(ref, sem):
    pltpu.make_async_copy(ref, ref, sem).wait()


def kernel(
    target_ref,
    owners_ref,
    segment_ref,
    history_ref,
    gain_in_ref,
    gain_out_ref,
    cot_ref,
    events_hbm,
    proj_hbm,
    out_hbm,
    pooled_ref,
    proj_ref,
    out_ref,
    events,
    w_out,
    outgoing,
    incoming,
    padded_cot,
    weights,
    arrived_sum,
    normed,
    normed_t,
    act,
    act_slope,
    attend,
    attend_slope,
    mixed,
    mixed_slope,
    mixed_cot,
    gate_cot,
    users,
    users_t,
    mask,
    share,
    share_all,
    back,
    back_all,
    back_dev,
    stats,
    stats_other,
    pool_dev,
    pool,
    pool_all,
    part,
    part_all,
    mean,
    mean_all,
    held,
    grad_out_t,
    other_out,
    z_in,
    plane_in_0,
    plane_in_1,
    last_z,
    last_plane,
    load_sem,
    tile_send,
    tile_recv,
    piece_send,
    piece_recv,
    ring_send,
    ring_recv,
    plane_send,
    plane_recv,
    twin_send,
    twin_recv,
    small_send,
    small_recv,
    sum_z_send,
    sum_z_recv,
    sum_plane_send,
    sum_plane_recv,
    last_send,
    last_recv,
):
    i, z = lax.axis_index("dp"), lax.axis_index("fsdp")
    x, y, c = i // 8, (i // 2) % 4, i % 2
    twin = (i + 1 - 2 * c, z)
    scale = 1.0 / math.sqrt(HEAD)

    load_events = pltpu.make_async_copy(events_hbm, events, load_sem.at[0])
    load_events.start()
    for m in range(4):
        for b in range(4):
            column = pl.multiple_of(128 * (HEADS * b + 2 * m + c), 128)
            pltpu.make_async_copy(
                proj_hbm.at[:, pl.ds(column, 128)],
                weights.at[m, z, :, pl.ds(128 * b, 128)],
                load_sem.at[1],
            ).start()
    load_out = pltpu.make_async_copy(out_hbm, w_out, load_sem.at[2])
    load_out.start()

    lane = lax.broadcasted_iota(I32, (1, ROWS), 1)
    lane_slot, lane_row = lane // TILE, lane % TILE
    goes = jnp.zeros((1, ROWS), I32)
    comes = jnp.zeros((1, ROWS), I32)
    for b in range(N_DP):
        there = target_ref[b]
        goes = jnp.where(lane_slot == b, there, goes)
        comes = jnp.where(lane_slot == b, (2 * i - there + 2 * N_DP) % N_DP, comes)
    block_row = lax.broadcasted_iota(I32, (BLOCK * N_DP, ROWS), 0)
    place = (block_row == BLOCK * goes + lane_row).astype(BF16)
    user_lane = lax.broadcasted_iota(I32, (1, 128), 1)
    user_row = lax.broadcasted_iota(I32, (BLOCK, 1), 0)
    cot_goes = jnp.full((1, 128), -1, I32)
    cot_comes = jnp.full((BLOCK, 1), -1, I32)
    inverse = jnp.ones((BLOCK, 1), F32)
    for u in range(4):
        owner = owners_ref[u]
        origin = (2 * i - owner + 2 * N_DP) % N_DP
        cot_goes = jnp.where(user_lane == u, BLOCK * origin + TILE + u, cot_goes)
        cot_comes = jnp.where(user_row == u, BLOCK * owner + TILE + u, cot_comes)
        inverse = jnp.where(user_row % 4 == u, history_ref[u].astype(F32), inverse)
    inverse = 1.0 / inverse
    cot_row = lax.broadcasted_iota(I32, (BLOCK * N_DP, 128), 0)
    cot_place = (cot_row == cot_goes).astype(BF16)
    padded_cot[...] = jnp.zeros_like(padded_cot)
    padded_cot[0:4, :] = cot_ref[...]

    await_bytes(weights.at[:, z], load_sem.at[1])
    barrier = pltpu.get_barrier_semaphore()

    def greet_dp(k, carry):
        pl.semaphore_signal(barrier, inc=1, device_id=((i + k) % N_DP, z), device_id_type=MESH)
        return carry

    def greet_z(k, carry):
        pl.semaphore_signal(barrier, inc=1, device_id=(i, (z + k) % N_Z), device_id_type=MESH)
        return carry

    lax.fori_loop(1, N_DP, greet_dp, 0)
    lax.fori_loop(1, N_Z, greet_z, 0)

    load_events.wait()
    load_out.wait()
    packed = dot(place, events[...]) + dot(cot_place, padded_cot[...].astype(BF16))
    outgoing[...] = packed.astype(BF16).reshape(N_DP, BLOCK, FEATURES)
    pl.semaphore_wait(barrier, N_DP - 1 + N_Z - 1)

    sends = []

    def to_twin(src, dst, n):
        sends.append(send(src, dst, twin_send.at[n], twin_recv.at[n], twin))

    def along_z(make):
        def step(k, carry):
            make((z + 3 * k) % N_Z)
            return carry

        lax.fori_loop(1, N_Z, step, 0)

    half_of_z = z // 4
    p = (1 - half_of_z) * (4 * x + y) + half_of_z * (4 * y + x)
    piece = weights.at[p % 4, z, pl.ds(64 + 16 * (p // 4), 16)]
    along_z(lambda there: send(piece, piece, piece_send, piece_recv, (i, there)))

    def ring_part(step, way, group):
        shard = (z - way * step + 2 * N_Z) % N_Z
        rows = pl.ds(0, 64) if step < 4 else pl.ds(0 if way > 0 else 32, 32)
        return weights.at[pl.ds(2 * group, 2), shard, rows]

    def ring_step(step, group):
        for d, way in ((0, 1), (1, -1)):
            shard = (z - way * (step - 1) + 2 * N_Z) % N_Z
            rows = pl.ds(0, 64) if step < 4 else pl.ds(0 if way > 0 else 32, 32)
            ref = weights.at[pl.ds(2 * group, 2), shard, rows]
            sends.append(
                send(
                    ref,
                    ref,
                    ring_send.at[step - 1, group, d],
                    ring_recv.at[step - 1, group, d],
                    (i, (z + way + N_Z) % N_Z),
                )
            )

    def ring_arrive(step, group):
        for d, way in ((0, 1), (1, -1)):
            await_bytes(ring_part(step, way, group), ring_recv.at[step - 1, group, d])

    def ring_advance(step, group):
        ring_arrive(step, group)
        if step < 4:
            ring_step(step + 1, group)

    ring_step(1, 0)
    ring_step(1, 1)

    def send_tile(k, carry):
        there = (i + 13 * k) % N_DP
        send(outgoing.at[there], incoming.at[i], tile_send, tile_recv, (there, z))
        return carry

    lax.fori_loop(1, N_DP, send_tile, 0)
    incoming[i] = outgoing[i]

    def plane_chunk(half, phase, spot, only):
        slow = (x, y)[half]
        shards = pl.ds(4 * half + (2 if only == 1 else 0), 4 if only is None else 2)
        if phase == 0:
            return weights.at[spot, shards, pl.ds(64 + 16 * slow, 16)]
        return weights.at[:, shards, pl.ds(64 + 16 * spot, 16)]

    def plane_axis(along_y):
        here = y if along_y else x
        neighbours = []
        for way in (1, -1):
            there = (here + way + 4) % 4
            neighbours.append(8 * x + 2 * there + c if along_y else 8 * there + 2 * y + c)
        return here, neighbours

    def plane_step(phase, step):
        for half in range(2):
            here, neighbours = plane_axis((half == 0) == (phase == 0))
            for d, way in ((0, 1), (1, -1)):
                origin = (here - way * (step - 1) + 4) % 4
                ref = plane_chunk(half, phase, origin, None if step == 1 else d)
                sends.append(
                    send(
                        ref,
                        ref,
                        plane_send.at[phase, step - 1, half, d],
                        plane_recv.at[phase, step - 1, half, d],
                        (neighbours[d], z),
                    )
                )

    def plane_arrive(phase, step):
        for half in range(2):
            here, _ = plane_axis((half == 0) == (phase == 0))
            for d, way in ((0, 1), (1, -1)):
                origin = (here - way * step + 4) % 4
                ref = plane_chunk(half, phase, origin, None if step == 1 else d)
                await_bytes(ref, plane_recv.at[phase, step - 1, half, d])

    pieces = weights.at[0, pl.ds(0, N_Z - 1), pl.ds(0, 16)]
    await_bytes(pieces, piece_recv)
    plane_step(0, 1)
    ring_advance(1, 0)
    plane_arrive(0, 1)
    plane_step(0, 2)
    ring_advance(1, 1)
    plane_arrive(0, 2)
    plane_step(1, 1)
    ring_advance(2, 0)
    ring_advance(2, 1)
    plane_arrive(1, 1)
    plane_step(1, 2)
    ring_advance(3, 0)
    ring_advance(3, 1)

    await_bytes(incoming.at[pl.ds(0, N_DP - 1)], tile_recv)
    every = incoming[...].reshape(BLOCK * N_DP, FEATURES)
    fetch = (block_row == BLOCK * comes + lane_row).astype(BF16)
    arrived = dot(fetch, every, ((0,), (0,)))
    cot_lane = lax.broadcasted_iota(I32, (BLOCK, BLOCK * N_DP), 1)
    cot_mine = dot((cot_lane == cot_comes).astype(BF16), every)

    def pack(rows):
        return jnp.concatenate([rows[0:4, 256 * k : 256 * (k + 1)] for k in range(4)], axis=0)

    share[...] = (pack(cot_mine) * inverse).astype(BF16)
    share_all[z] = share[...]
    along_z(
        lambda there: send(share, share_all.at[z], small_send.at[0], small_recv.at[0], (i, there))
    )
    power = jnp.mean(arrived * arrived, axis=-1, keepdims=True)
    rows = (arrived * lax.rsqrt(power + 1e-06) * gain_in_ref[...]).astype(BF16)
    normed[c] = rows
    to_twin(normed.at[c], normed.at[c], 0)

    starts, ends = [], []
    for u in range(4):
        start = jnp.int32(0)
        for b in range(N_DP):
            start = start + jnp.where(segment_ref[b] < u, TILE, 0)
        starts.append(start)
        ends.append(start + history_ref[u])

    def members(event, user, stops):
        found = jnp.zeros(event.shape, jnp.bool_)
        for u in range(4):
            found = found | ((user == u) & (event >= starts[u]) & (event < stops[u]))
        return found.astype(F32).astype(BF16)

    event = lax.broadcasted_iota(I32, (ROWS, 128), 0)
    user = lax.broadcasted_iota(I32, (ROWS, 128), 1)
    users[c] = members(event, user, ends) + members(event, user - 16, starts[1:] + [ROWS])
    to_twin(users.at[c], users.at[c], 1)
    sum_t = members(
        lax.broadcasted_iota(I32, (BLOCK, ROWS), 1),
        lax.broadcasted_iota(I32, (BLOCK, ROWS), 0),
        ends,
    )
    arrived_sum[...] = pack(dot(sum_t, arrived.astype(BF16)))

    ring_advance(4, 0)
    plane_arrive(1, 2)
    ring_advance(4, 1)

    await_bytes(users.at[1 - c], twin_recv.at[1])
    await_bytes(normed.at[1 - c], twin_recv.at[0])
    shift_row = lax.broadcasted_iota(I32, (128, 128), 0)
    shift_column = lax.broadcasted_iota(I32, (128, 128), 1)
    shift = ((shift_row == shift_column + 16) & (shift_column < 4)).astype(F32).astype(BF16)
    keep = ((shift_row == shift_column) & (shift_column < 4)).astype(F32).astype(BF16)
    for dev in range(2):
        found = users[dev]
        owned = dot(found, shift).astype(BF16)
        valid = dot(found, keep).astype(BF16)
        same = dot(owned, valid, ((1,), (1,)))
        query_row = lax.broadcasted_iota(I32, (ROWS, ROWS), 0)
        key_row = lax.broadcasted_iota(I32, (ROWS, ROWS), 1)
        mask[dev] = jnp.where(key_row <= query_row, same, 0.0)
        users_t[dev] = dot(keep[0:BLOCK], found, ((1,), (1,))).astype(BF16)
        normed_t[:, ROWS * dev : ROWS * (dev + 1)] = normed[dev].T

    def forward(h, carry):
        dev = h % 2
        pre = dot(normed[dev], weights[h // 2].reshape(FEATURES, 4 * HEAD))
        sig = sigmoid(pre)
        silu = pre * sig
        act_slope[h] = sig + silu * (1.0 - sig)
        act[h] = silu.astype(BF16)
        value = act[h, :, 128:256]
        query = act[h, :, 256:384]
        key = act[h, :, 384:512]
        scores = dot(query, key, ((1,), (1,))) * scale
        sig = sigmoid(scores)
        silu = scores * sig
        attend_slope[h] = (sig + silu * (1.0 - sig)) * (mask[dev] * scale)
        attend[h] = (silu * mask[dev]).astype(BF16)
        mixed[h] = dot(attend[h], value)
        return carry

    lax.fori_loop(0, HEADS // 2, forward, 0)

    await_bytes(share_all.at[pl.ds(0, N_Z - 1)], small_recv.at[0])
    shares = share_all[...].reshape(16 * N_Z, 256)
    quarter = (lax.broadcasted_iota(I32, (16 * N_Z, 1), 0) % 16) // 4
    partial = jnp.zeros((16 * N_Z, 128), F32)
    for k in range(4):
        product = dot(shares, w_out[:, 256 * k : 256 * (k + 1)], ((1,), (1,)))
        partial = partial + jnp.where(quarter == k, product, 0.0)
    fold_row = lax.broadcasted_iota(I32, (16 * N_Z, 16 * N_Z), 0)
    fold_column = lax.broadcasted_iota(I32, (16 * N_Z, 16 * N_Z), 1)
    fold = (fold_row // 16 == fold_column // 16) & (fold_row % 4 == fold_column % 4)
    folded = dot(fold.astype(F32), partial, precision=lax.Precision.HIGHEST)
    back[...] = folded.astype(BF16).reshape(N_Z, 16, 128)
    back_all[z // 2, z % 2] = back[z]
    along_z(
        lambda there: send(
            back.at[there],
            back_all.at[z // 2, z % 2],
            small_send.at[1],
            small_recv.at[1],
            (i, there),
        )
    )

    lax.fori_loop(HEADS // 2, HEADS, forward, 0)

    await_bytes(back.at[pl.ds(0, N_Z - 1)], small_recv.at[1])
    back_dev[c] = back_all[:, c]
    to_twin(back_all.at[:, 1 - c], back_dev.at[c], 2)
    sums = []
    for dev in range(2):
        total = jnp.zeros((ROWS, 1), F32)
        for m in range(4):
            total = total + jnp.sum(mixed[2 * m + dev] * mixed[2 * m + dev], axis=-1, keepdims=True)
        sums.append(total)
    await_bytes(back_dev.at[1 - c], twin_recv.at[2])

    def gain_of(m):
        return gain_out_ref[:, pl.ds(pl.multiple_of(HEAD * (2 * m + c), HEAD), HEAD)]

    stat_lane = lax.broadcasted_iota(I32, (ROWS, 128), 1)
    for dev in range(2):
        total = jnp.zeros((ROWS, 1), F32)
        for m in range(4):
            n = 2 * m + dev
            cot_rows = dot(users[dev][:, 0:16], back_dev[dev, m])
            slope = cot_rows * act[n, :, 0:128].astype(F32) * gain_of(m)
            mixed_slope[n] = slope
            gate_cot[n] = cot_rows * gain_of(m) * mixed[n]
            total = total + jnp.sum(slope * mixed[n], axis=-1, keepdims=True)
        column = jnp.where(stat_lane == 0, sums[dev], jnp.where(stat_lane == 1, total, 0.0))
        stats[:, ROWS * dev : ROWS * (dev + 1)] = column.T[0:8]
    to_twin(stats, stats_other, 3)
    await_bytes(stats_other, twin_recv.at[3])
    both_stats = jnp.concatenate(
        [stats[...] + stats_other[...], jnp.zeros((120, 2 * ROWS), F32)], axis=0
    ).T
    for dev in range(2):
        total = both_stats[ROWS * dev : ROWS * (dev + 1), 0:1]
        slope_total = both_stats[ROWS * dev : ROWS * (dev + 1), 1:2]
        norm = lax.rsqrt(total * (1.0 / FEATURES) + 1e-06)
        shared = norm * norm * norm * slope_total * (1.0 / FEATURES)
        for m in range(4):
            n = 2 * m + dev
            gated = mixed[n] * norm * gain_of(m) * act[n, :, 0:128].astype(F32)
            pool_dev[dev, m] = dot(users_t[dev], gated.astype(BF16))[0:8]
            gate_cot[n] = gate_cot[n] * norm
            mixed_cot[n] = (norm * mixed_slope[n] - shared * mixed[n]).astype(BF16)
    pool[:, c] = pool_dev[c]
    to_twin(pool_dev.at[1 - c], pool.at[:, c], 4)

    def backward(k, carry):
        m = (y + 2 + 3 * k) % 4
        pre_cots = []
        for dev in range(2):
            n = 2 * m + dev
            value = act[n, :, 128:256]
            query = act[n, :, 256:384]
            key = act[n, :, 384:512]
            cot = mixed_cot[n]
            score_cot = (dot(cot, value, ((1,), (1,))) * attend_slope[n]).astype(BF16)
            value_cot = dot(attend[n], cot, ((0,), (0,)))
            query_cot = dot(score_cot, key)
            key_cot = dot(score_cot, query, ((0,), (0,)))
            act_cot = jnp.concatenate([gate_cot[n], value_cot, query_cot, key_cot], axis=1)
            pre_cots.append((act_cot * act_slope[n]).astype(BF16))
        grad = dot(normed_t[...], jnp.concatenate(pre_cots, axis=0)).astype(BF16)
        for b in range(4):
            held[b, m, :, 0:128, :] = grad[:, 128 * b : 128 * (b + 1)].reshape(N_Z, 128, 128)
        return carry

    lax.fori_loop(0, 1, backward, 0)
    await_bytes(pool.at[:, 1 - c], twin_recv.at[4])
    pool_all[z] = pool[z // 2, z % 2]
    along_z(
        lambda there: send(
            pool.at[there // 2, there % 2],
            pool_all.at[z],
            small_send.at[2],
            small_recv.at[2],
            (i, there),
        )
    )
    lax.fori_loop(1, 3, backward, 0)

    await_bytes(pool_all.at[pl.ds(0, N_Z - 1)], small_recv.at[2])
    pooled = pool_all[...]
    flat = pooled.reshape(8 * N_Z, 128)
    high = flat.astype(BF16).astype(F32)
    both = dot(jnp.concatenate([high, flat - high], axis=0).astype(BF16), w_out[...])
    products = (both[0 : 8 * N_Z] + both[8 * N_Z :]).reshape(N_Z, 8, FEATURES)
    part[...] = jnp.concatenate(
        [products[:, 0:4, 256 * k : 256 * (k + 1)] for k in range(4)], axis=1
    ).astype(BF16)
    part_all[z] = part[z]
    along_z(
        lambda there: send(
            part.at[there], part_all.at[z], small_send.at[3], small_recv.at[3], (i, there)
        )
    )
    spread = jnp.concatenate([pooled[:, 0:4]] * 4, axis=1).reshape(16 * N_Z, 128)
    for k in range(4):
        block = dot(
            share_all[...].reshape(16 * N_Z, 256),
            jnp.where(quarter == k, spread, 0.0).astype(BF16),
            ((0,), (0,)),
        )
        grad_out_t[4 * k : 4 * (k + 1)] = block.astype(BF16).reshape(4, 2, 32, 128)
    to_twin(grad_out_t.at[:, 1 - c], other_out, 5)

    lax.fori_loop(3, 4, backward, 0)

    first_rows, z_rows = pl.ds(0, B_ROWS), pl.ds(B_ROWS, A_ROWS)
    last_rows = pl.ds(B_ROWS, STRIPE - B_ROWS)

    def sum_z_chunk(away, d, half):
        if half:
            return held.at[pl.ds(2 * d, 2), :, (z + away + N_Z) % N_Z, z_rows]
        return held.at[:, :, (z + away + N_Z) % N_Z, z_rows]

    def sum_z_landing(step, d):
        if step == 1:
            return z_in.at[d, 0, pl.ds(2 * d, 2)]
        return z_in.at[d, step - 1]

    def sum_z_step(step):
        for d, way in ((0, 1), (1, -1)):
            sends.append(
                send(
                    sum_z_chunk(way * (5 - step), d, step == 1),
                    sum_z_landing(step, d),
                    sum_z_send.at[step - 1, d],
                    sum_z_recv.at[step - 1, d],
                    (i, (z + way + N_Z) % N_Z),
                )
            )

    def sum_z_arrive(step):
        for d, way in ((0, 1), (1, -1)):
            landing = sum_z_landing(step, d)
            await_bytes(landing, sum_z_recv.at[step - 1, d])
            chunk = sum_z_chunk(way * (4 - step), d, step == 1)
            chunk[...] = chunk[...] + landing[...]

    def sum_plane_chunk(half, phase, spot, d):
        if phase == 0:
            shards = pl.ds(4 * half, 4)
            among = pl.ds(0, 4) if d is None else pl.ds(2 * d, 2)
            if half == 0:
                return held.at[spot, among, shards, first_rows]
            return held.at[among, spot, shards, first_rows]
        shards = pl.ds(4 * half, 4) if d is None else pl.ds(4 * half + 2 * d, 2)
        if half == 0:
            return held.at[x, spot, shards, first_rows]
        return held.at[spot, y, shards, first_rows]

    def sum_plane_landing(half, phase, step, d):
        buffer = (plane_in_0, plane_in_1)[phase].at[half, step - 1, d]
        return buffer.at[pl.ds(2 * d, 2)] if step == 1 else buffer

    def sum_plane_step(phase, step):
        for half in range(2):
            here, neighbours = plane_axis((half == 1) == (phase == 0))
            for d, way in ((0, 1), (1, -1)):
                spot = (here + way * (3 - step) + 4) % 4
                sends.append(
                    send(
                        sum_plane_chunk(half, phase, spot, d if step == 1 else None),
                        sum_plane_landing(half, phase, step, d),
                        sum_plane_send.at[phase, step - 1, half, d],
                        sum_plane_recv.at[phase, step - 1, half, d],
                        (neighbours[d], z),
                    )
                )

    def sum_plane_arrive(phase, step):
        for half in range(2):
            here, _ = plane_axis((half == 1) == (phase == 0))
            for d, way in ((0, 1), (1, -1)):
                landing = sum_plane_landing(half, phase, step, d)
                await_bytes(landing, sum_plane_recv.at[phase, step - 1, half, d])
                spot = (here + way * (2 - step) + 4) % 4
                chunk = sum_plane_chunk(half, phase, spot, d if step == 1 else None)
                chunk[...] = chunk[...] + landing[...]

    sum_z_step(1)
    sum_plane_step(0, 1)

    await_bytes(part_all.at[pl.ds(0, N_Z - 1)], small_recv.at[3])
    mean[...] = (
        (jnp.sum(part_all[...].astype(F32), axis=0) + arrived_sum[...]) * inverse
    ).astype(BF16)
    mean_all[i] = mean[...]

    def send_mean(k, carry):
        send(mean, mean_all.at[i], small_send.at[4], small_recv.at[4], ((i + 13 * k) % N_DP, z))
        return carry

    lax.fori_loop(1, N_DP, send_mean, 0)
    await_bytes(other_out, twin_recv.at[5])
    held[:, :, z, 128:STRIPE, :] = (grad_out_t[:, c] + other_out[...]).reshape(4, 4, 32, 128)

    sum_z_arrive(1)
    sum_z_step(2)
    sum_plane_arrive(0, 1)
    sum_plane_step(0, 2)
    sum_z_arrive(2)
    sum_z_step(3)
    sum_z_arrive(3)
    sum_z_step(4)
    sum_plane_arrive(0, 2)
    sum_plane_step(1, 1)
    sum_z_arrive(4)

    def send_plane(k, carry):
        there = (i // 2 + 5 * k) % 16
        block = held.at[there // 4, there % 4, z, last_rows]
        send(block, last_plane.at[i // 2], last_send.at[0], last_recv.at[0], (2 * there + c, z))
        return carry

    lax.fori_loop(1, 16, send_plane, 0)
    last_plane[i // 2] = held[x, y, z, B_ROWS:STRIPE]

    sum_plane_arrive(1, 1)
    sum_plane_step(1, 2)

    await_bytes(mean_all.at[pl.ds(0, N_DP - 1)], small_recv.at[4])
    means = mean_all[...].reshape(16 * N_DP, 256)
    mean_lane = lax.broadcasted_iota(I32, (16, 16 * N_DP), 1)
    for k in range(4):
        wanted = jnp.full((16, 1), -1, I32)
        for u in range(4):
            source = (2 * i - owners_ref[u] + 2 * N_DP) % N_DP
            wanted = jnp.where(user_row == u, 16 * source + 4 * k + u, wanted)
        chosen = dot((mean_lane == wanted).astype(BF16), means)
        pooled_ref[:, 256 * k : 256 * (k + 1)] = chosen[0:4]

    sum_plane_arrive(1, 2)

    along_z(
        lambda there: send(
            held.at[x, y, there, first_rows],
            last_z.at[z],
            last_send.at[1],
            last_recv.at[1],
            (i, there),
        )
    )
    last_z[z] = held[x, y, z, 0:B_ROWS]

    await_bytes(last_plane.at[pl.ds(0, 15)], last_recv.at[0])
    rest = jnp.sum(last_plane[...].astype(F32), axis=0)
    proj_ref[B_ROWS:128, :] = rest[0:A_ROWS]
    out_ref[...] = rest[A_ROWS:]
    await_bytes(last_z.at[pl.ds(0, N_Z - 1)], last_recv.at[1])
    proj_ref[0:B_ROWS, :] = jnp.sum(last_z[...].astype(F32), axis=0)

    for copy in sends:
        copy.wait_send()
    await_bytes(pieces, piece_send)
    await_bytes(outgoing.at[pl.ds(0, N_DP - 1)], tile_send)
    await_bytes(share_all.at[pl.ds(0, N_Z - 1)], small_send.at[0])
    await_bytes(back.at[pl.ds(0, N_Z - 1)], small_send.at[1])
    await_bytes(pool_all.at[pl.ds(0, N_Z - 1)], small_send.at[2])
    await_bytes(part.at[pl.ds(0, N_Z - 1)], small_send.at[3])
    await_bytes(mean_all.at[pl.ds(0, N_DP - 1)], small_send.at[4])
    await_bytes(last_plane.at[pl.ds(0, 15)], last_send.at[0])
    await_bytes(last_z.at[pl.ds(0, N_Z - 1)], last_send.at[1])


def finish_kernel(pooled_in, proj_in, out_in, pooled_ref, proj_ref, out_ref):
    pooled_ref[...] = pooled_in[...]
    proj_ref[...] = proj_in[...]
    out_ref[...] = out_in[...]


def body(events, gain_in, gain_out, w_proj, w_out, target, segment, history, owners, pooled_cot):
    any_space, vmem = pl.BlockSpec(memory_space=pl.ANY), pl.BlockSpec(memory_space=pltpu.VMEM)
    smem = pl.BlockSpec(memory_space=pltpu.SMEM)
    dma = pltpu.SemaphoreType.DMA

    def bf16(*shape):
        return pltpu.VMEM(shape, BF16)

    def f32(*shape):
        return pltpu.VMEM(shape, F32)

    pooled, grad_proj, grad_out_t = pl.pallas_call(
        kernel,
        out_shape=(
            jax.ShapeDtypeStruct((4, FEATURES), F32),
            jax.ShapeDtypeStruct((128, 128), F32),
            jax.ShapeDtypeStruct((32, 128), F32),
        ),
        in_specs=[smem] * 4 + [vmem] * 3 + [any_space] * 3,
        out_specs=(vmem, vmem, vmem),
        scratch_shapes=[
            bf16(ROWS, FEATURES),
            bf16(128, FEATURES),
            bf16(N_DP, BLOCK, FEATURES),
            bf16(N_DP, BLOCK, FEATURES),
            f32(128, FEATURES),
            bf16(4, N_Z, 128, 4 * HEAD),
            f32(16, 256),
            bf16(2, ROWS, FEATURES),
            bf16(FEATURES, 2 * ROWS),
            bf16(HEADS, ROWS, 4 * HEAD),
            f32(HEADS, ROWS, 4 * HEAD),
            bf16(HEADS, ROWS, ROWS),
            f32(HEADS, ROWS, ROWS),
            f32(HEADS, ROWS, HEAD),
            f32(HEADS, ROWS, HEAD),
            bf16(HEADS, ROWS, HEAD),
            f32(HEADS, ROWS, HEAD),
            bf16(2, ROWS, 128),
            bf16(2, BLOCK, ROWS),
            f32(2, ROWS, ROWS),
            bf16(16, 256),
            bf16(N_Z, 16, 256),
            bf16(N_Z, 16, 128),
            bf16(4, 2, 16, 128),
            bf16(2, 4, 16, 128),
            f32(8, 2 * ROWS),
            f32(8, 2 * ROWS),
            f32(2, 4, 8, 128),
            f32(4, 2, 8, 128),
            f32(N_Z, 8, 128),
            bf16(N_Z, 16, 256),
            bf16(N_Z, 16, 256),
            bf16(16, 256),
            bf16(N_DP, 16, 256),
            bf16(4, 4, N_Z, STRIPE, 128),
            bf16(16, 2, 32, 128),
            bf16(16, 32, 128),
            bf16(2, 4, 4, 4, A_ROWS, 128),
            bf16(2, 2, 2, 4, 4, B_ROWS, 128),
            bf16(2, 2, 2, 4, B_ROWS, 128),
            bf16(N_Z, B_ROWS, 128),
            bf16(16, STRIPE - B_ROWS, 128),
            dma((3,)),
            dma,
            dma,
            dma,
            dma,
            dma((4, 2, 2)),
            dma((4, 2, 2)),
            dma((2, 2, 2, 2)),
            dma((2, 2, 2, 2)),
            dma((6,)),
            dma((6,)),
            dma((5,)),
            dma((5,)),
            dma((4, 2)),
            dma((4, 2)),
            dma((2, 2, 2, 2)),
            dma((2, 2, 2, 2)),
            dma((2,)),
            dma((2,)),
        ],
        compiler_params=pltpu.CompilerParams(
            collective_id=0, has_side_effects=True, vmem_limit_bytes=62 * 2**20
        ),
        name="step",
    )(
        target,
        owners,
        segment,
        history,
        gain_in.reshape(1, FEATURES),
        gain_out.reshape(1, FEATURES),
        pooled_cot,
        events,
        w_proj,
        w_out,
    )
    pooled, grad_proj, grad_out_t = pl.pallas_call(
        finish_kernel,
        out_shape=(
            jax.ShapeDtypeStruct((4, FEATURES), F32),
            jax.ShapeDtypeStruct((128, 128), F32),
            jax.ShapeDtypeStruct((32, 128), F32),
        ),
        in_specs=[vmem] * 3,
        out_specs=(vmem, vmem, vmem),
        name="finish",
    )(pooled, grad_proj, grad_out_t)
    return (pooled, grad_proj, grad_out_t.T)


def solution(mesh):
    in_specs = (
        P(("dp", "fsdp"), None),
        P(),
        P(),
        P("fsdp", None),
        P("fsdp", None),
        P(("dp", "fsdp")),
        P(("dp", "fsdp")),
        P(("dp", "fsdp")),
        P(("dp", "fsdp")),
        P(("dp", "fsdp"), None),
    )
    out_specs = (P(("dp", "fsdp"), None), P("fsdp", "dp"), P("fsdp", "dp"))
    return jax.shard_map(body, mesh=mesh, in_specs=in_specs, out_specs=out_specs, check_vma=False)
```

```python
import math

import jax
import jax.numpy as jnp
from jax import lax
from jax.experimental import pallas as pl
from jax.experimental.pallas import tpu as pltpu
from jax.sharding import PartitionSpec as P

MESH = pl.DeviceIdType.MESH
BF16, F32, I32 = jnp.bfloat16, jnp.float32, jnp.int32

N_DP, N_Z = 32, 8
HEADS, HEAD = 8, 128
TILE = 12
BLOCK = 16
ROWS = 384
FEATURES = 1024
B_ROWS = 80
A_ROWS = 48
STRIPE = 160


def dot(a, b, dims=((1,), (0,)), precision=None):
    return lax.dot_general(
        a, b, (dims, ((), ())), precision=precision, preferred_element_type=F32
    )


def sigmoid(v):
    return 0.5 * jnp.tanh(0.5 * v) + 0.5


def send(src, dst, send_sem, recv_sem, device):
    copy = pltpu.make_async_remote_copy(
        src_ref=src,
        dst_ref=dst,
        send_sem=send_sem,
        recv_sem=recv_sem,
        device_id=device,
        device_id_type=MESH,
    )
    copy.start()
    return copy


def await_bytes(ref, sem):
    pltpu.make_async_copy(ref, ref, sem).wait()


def kernel(
    target_ref,
    owners_ref,
    segment_ref,
    history_ref,
    gain_in_ref,
    gain_out_ref,
    cot_ref,
    events_hbm,
    proj_hbm,
    out_hbm,
    pooled_ref,
    proj_ref,
    out_ref,
    events,
    w_out,
    outgoing,
    incoming,
    padded_cot,
    weights,
    arrived_sum,
    normed,
    normed_t,
    act,
    act_slope,
    attend,
    attend_slope,
    mixed,
    mixed_slope,
    mixed_cot,
    gate_cot,
    users,
    users_t,
    mask,
    share,
    share_all,
    back,
    back_all,
    back_dev,
    stats,
    stats_other,
    pool_dev,
    pool,
    pool_all,
    part,
    part_all,
    mean,
    mean_all,
    held,
    grad_out_t,
    other_out,
    z_in,
    plane_in_0,
    plane_in_1,
    last_z,
    last_plane,
    load_sem,
    tile_send,
    tile_recv,
    piece_send,
    piece_recv,
    ring_send,
    ring_recv,
    plane_send,
    plane_recv,
    head_send,
    head_recv,
    twin_send,
    twin_recv,
    small_send,
    small_recv,
    sum_z_send,
    sum_z_recv,
    sum_x_send,
    sum_x_recv,
    sum_y_send,
    sum_y_recv,
    second_send,
    second_recv,
    last_send,
    last_recv,
):
    i, z = lax.axis_index("dp"), lax.axis_index("fsdp")
    x, y, c = i // 8, (i // 2) % 4, i % 2
    twin = (i + 1 - 2 * c, z)
    scale = 1.0 / math.sqrt(HEAD)

    load_events = pltpu.make_async_copy(events_hbm, events, load_sem.at[0])
    load_events.start()
    for m in range(4):
        for b in range(4):
            column = pl.multiple_of(128 * (HEADS * b + 2 * m + c), 128)
            pltpu.make_async_copy(
                proj_hbm.at[:, pl.ds(column, 128)],
                weights.at[m, z, :, pl.ds(128 * b, 128)],
                load_sem.at[1],
            ).start()
    load_out = pltpu.make_async_copy(out_hbm, w_out, load_sem.at[2])
    load_out.start()

    lane = lax.broadcasted_iota(I32, (1, ROWS), 1)
    lane_slot, lane_row = lane // TILE, lane % TILE
    goes = jnp.zeros((1, ROWS), I32)
    comes = jnp.zeros((1, ROWS), I32)
    for b in range(N_DP):
        there = target_ref[b]
        goes = jnp.where(lane_slot == b, there, goes)
        comes = jnp.where(lane_slot == b, (2 * i - there + 2 * N_DP) % N_DP, comes)
    block_row = lax.broadcasted_iota(I32, (BLOCK * N_DP, ROWS), 0)
    place = (block_row == BLOCK * goes + lane_row).astype(BF16)
    user_lane = lax.broadcasted_iota(I32, (1, 128), 1)
    user_row = lax.broadcasted_iota(I32, (BLOCK, 1), 0)
    cot_goes = jnp.full((1, 128), -1, I32)
    cot_comes = jnp.full((BLOCK, 1), -1, I32)
    inverse = jnp.ones((BLOCK, 1), F32)
    for u in range(4):
        owner = owners_ref[u]
        origin = (2 * i - owner + 2 * N_DP) % N_DP
        cot_goes = jnp.where(user_lane == u, BLOCK * origin + TILE + u, cot_goes)
        cot_comes = jnp.where(user_row == u, BLOCK * owner + TILE + u, cot_comes)
        inverse = jnp.where(user_row % 4 == u, history_ref[u].astype(F32), inverse)
    inverse = 1.0 / inverse
    cot_row = lax.broadcasted_iota(I32, (BLOCK * N_DP, 128), 0)
    cot_place = (cot_row == cot_goes).astype(BF16)
    padded_cot[...] = jnp.zeros_like(padded_cot)
    padded_cot[0:4, :] = cot_ref[...]

    await_bytes(weights.at[:, z], load_sem.at[1])
    barrier = pltpu.get_barrier_semaphore()

    def greet_dp(k, carry):
        pl.semaphore_signal(barrier, inc=1, device_id=((i + k) % N_DP, z), device_id_type=MESH)
        return carry

    def greet_z(k, carry):
        pl.semaphore_signal(barrier, inc=1, device_id=(i, (z + k) % N_Z), device_id_type=MESH)
        return carry

    lax.fori_loop(1, N_DP, greet_dp, 0)
    lax.fori_loop(1, N_Z, greet_z, 0)

    load_events.wait()
    load_out.wait()
    packed = dot(place, events[...]) + dot(cot_place, padded_cot[...].astype(BF16))
    outgoing[...] = packed.astype(BF16).reshape(N_DP, BLOCK, FEATURES)
    pl.semaphore_wait(barrier, N_DP - 1 + N_Z - 1)

    sends = []

    def to_twin(src, dst, n):
        sends.append(send(src, dst, twin_send.at[n], twin_recv.at[n], twin))

    def along_z(make):
        def step(k, carry):
            make((z + 3 * k) % N_Z)
            return carry

        lax.fori_loop(1, N_Z, step, 0)

    half_of_z = z // 4
    p = (1 - half_of_z) * (4 * x + y) + half_of_z * (4 * y + x)
    piece = weights.at[p % 4, z, pl.ds(64 + 16 * (p // 4), 16)]
    along_z(lambda there: send(piece, piece, piece_send, piece_recv, (i, there)))

    def ring_part(step, way, m):
        shard = (z - way * step + 2 * N_Z) % N_Z
        rows = pl.ds(0, 64) if step < 4 else pl.ds(0 if way > 0 else 32, 32)
        return weights.at[m, shard, rows]

    def ring_step(step, m):
        for d, way in ((0, 1), (1, -1)):
            shard = (z - way * (step - 1) + 2 * N_Z) % N_Z
            rows = pl.ds(0, 64) if step < 4 else pl.ds(0 if way > 0 else 32, 32)
            ref = weights.at[m, shard, rows]
            sends.append(
                send(
                    ref,
                    ref,
                    ring_send.at[step - 1, m, d],
                    ring_recv.at[step - 1, m, d],
                    (i, (z + way + N_Z) % N_Z),
                )
            )

    def ring_advance(step, m):
        for d, way in ((0, 1), (1, -1)):
            await_bytes(ring_part(step, way, m), ring_recv.at[step - 1, m, d])
        if step < 4:
            ring_step(step + 1, m)

    ring_step(1, 0)
    ring_step(1, 1)

    def send_tile(k, carry):
        there = (i + 13 * k) % N_DP
        send(outgoing.at[there], incoming.at[i], tile_send, tile_recv, (there, z))
        return carry

    lax.fori_loop(1, N_DP, send_tile, 0)
    incoming[i] = outgoing[i]

    def plane_axis(along_y):
        here = y if along_y else x
        neighbours = []
        for way in (1, -1):
            there = (here + way + 4) % 4
            neighbours.append(8 * x + 2 * there + c if along_y else 8 * there + 2 * y + c)
        return here, neighbours

    def plane_first(step, arrive):
        for half in range(2):
            here, neighbours = plane_axis(half == 0)
            slow = (x, y)[half]
            for d, way in ((0, 1), (1, -1)):
                origin = (here - way * (step if arrive else step - 1) + 4) % 4
                shards = pl.ds(4 * half, 4) if step == 1 else pl.ds(4 * half + 2 * d, 2)
                ref = weights.at[origin, shards, pl.ds(64 + 16 * slow, 16)]
                send_sem = plane_send.at[step - 1, half, d]
                recv_sem = plane_recv.at[step - 1, half, d]
                if arrive:
                    await_bytes(ref, recv_sem)
                else:
                    sends.append(send(ref, ref, send_sem, recv_sem, (neighbours[d], z)))

    def plane_head(step, m, arrive):
        for half in range(2):
            here, neighbours = plane_axis(half == 1)
            for d, way in ((0, 1), (1, -1)):
                origin = (here - way * (step if arrive else step - 1) + 4) % 4
                shards = pl.ds(4 * half, 4) if step == 1 else pl.ds(4 * half + 2 * d, 2)
                ref = weights.at[m, shards, pl.ds(64 + 16 * origin, 16)]
                send_sem = head_send.at[step - 1, m, half, d]
                recv_sem = head_recv.at[step - 1, m, half, d]
                if arrive:
                    await_bytes(ref, recv_sem)
                else:
                    sends.append(send(ref, ref, send_sem, recv_sem, (neighbours[d], z)))

    def plane_advance(m):
        plane_head(1, m, True)
        plane_head(2, m, False)

    pieces = weights.at[0, pl.ds(0, N_Z - 1), pl.ds(0, 16)]
    await_bytes(pieces, piece_recv)
    plane_first(1, False)
    ring_advance(1, 0)
    ring_step(1, 2)
    ring_advance(1, 1)
    ring_step(1, 3)
    plane_first(1, True)
    plane_first(2, False)
    ring_advance(2, 0)
    ring_advance(1, 2)
    plane_first(2, True)
    plane_head(1, 0, False)
    plane_head(1, 1, False)
    ring_advance(2, 1)
    ring_advance(1, 3)
    ring_advance(3, 0)
    ring_advance(2, 2)
    plane_advance(0)
    plane_head(1, 2, False)
    ring_advance(3, 1)
    ring_advance(2, 3)
    plane_advance(1)
    plane_head(1, 3, False)

    await_bytes(incoming.at[pl.ds(0, N_DP - 1)], tile_recv)
    every = incoming[...].reshape(BLOCK * N_DP, FEATURES)
    fetch = (block_row == BLOCK * comes + lane_row).astype(BF16)
    arrived = dot(fetch, every, ((0,), (0,)))
    cot_lane = lax.broadcasted_iota(I32, (BLOCK, BLOCK * N_DP), 1)
    cot_mine = dot((cot_lane == cot_comes).astype(BF16), every)

    def pack(rows):
        return jnp.concatenate([rows[0:4, 256 * k : 256 * (k + 1)] for k in range(4)], axis=0)

    share[...] = (pack(cot_mine) * inverse).astype(BF16)
    share_all[z] = share[...]
    along_z(
        lambda there: send(share, share_all.at[z], small_send.at[0], small_recv.at[0], (i, there))
    )
    power = jnp.mean(arrived * arrived, axis=-1, keepdims=True)
    rows = (arrived * lax.rsqrt(power + 1e-06) * gain_in_ref[...]).astype(BF16)
    normed[c] = rows
    to_twin(normed.at[c], normed.at[c], 0)

    starts, ends = [], []
    for u in range(4):
        start = jnp.int32(0)
        for b in range(N_DP):
            start = start + jnp.where(segment_ref[b] < u, TILE, 0)
        starts.append(start)
        ends.append(start + history_ref[u])

    def members(event, user, stops):
        found = jnp.zeros(event.shape, jnp.bool_)
        for u in range(4):
            found = found | ((user == u) & (event >= starts[u]) & (event < stops[u]))
        return found.astype(F32).astype(BF16)

    event = lax.broadcasted_iota(I32, (ROWS, 128), 0)
    user = lax.broadcasted_iota(I32, (ROWS, 128), 1)
    users[c] = members(event, user, ends) + members(event, user - 16, starts[1:] + [ROWS])
    to_twin(users.at[c], users.at[c], 1)
    sum_t = members(
        lax.broadcasted_iota(I32, (BLOCK, ROWS), 1),
        lax.broadcasted_iota(I32, (BLOCK, ROWS), 0),
        ends,
    )
    arrived_sum[...] = pack(dot(sum_t, arrived.astype(BF16)))

    ring_advance(3, 2)
    ring_advance(3, 3)
    plane_advance(2)
    plane_advance(3)

    await_bytes(users.at[1 - c], twin_recv.at[1])
    await_bytes(normed.at[1 - c], twin_recv.at[0])
    shift_row = lax.broadcasted_iota(I32, (128, 128), 0)
    shift_column = lax.broadcasted_iota(I32, (128, 128), 1)
    shift = ((shift_row == shift_column + 16) & (shift_column < 4)).astype(F32).astype(BF16)
    keep = ((shift_row == shift_column) & (shift_column < 4)).astype(F32).astype(BF16)
    for dev in range(2):
        found = users[dev]
        owned = dot(found, shift).astype(BF16)
        valid = dot(found, keep).astype(BF16)
        same = dot(owned, valid, ((1,), (1,)))
        query_row = lax.broadcasted_iota(I32, (ROWS, ROWS), 0)
        key_row = lax.broadcasted_iota(I32, (ROWS, ROWS), 1)
        mask[dev] = jnp.where(key_row <= query_row, same, 0.0)
        users_t[dev] = dot(keep[0:BLOCK], found, ((1,), (1,))).astype(BF16)
        normed_t[:, ROWS * dev : ROWS * (dev + 1)] = normed[dev].T

    def forward(m):
        ring_advance(4, m)
        plane_head(2, m, True)
        weight = weights[m].reshape(FEATURES, 4 * HEAD)
        for dev in range(2):
            n = 2 * m + dev
            pre = dot(normed[dev], weight)
            sig = sigmoid(pre)
            silu = pre * sig
            act_slope[n] = sig + silu * (1.0 - sig)
            act[n] = silu.astype(BF16)
        for dev in range(2):
            n = 2 * m + dev
            value = act[n, :, 128:256]
            query = act[n, :, 256:384]
            key = act[n, :, 384:512]
            scores = dot(query, key, ((1,), (1,))) * scale
            sig = sigmoid(scores)
            silu = scores * sig
            attend_slope[n] = (sig + silu * (1.0 - sig)) * (mask[dev] * scale)
            attend[n] = (silu * mask[dev]).astype(BF16)
            mixed[n] = dot(attend[n], value)

    forward(0)
    forward(1)

    await_bytes(share_all.at[pl.ds(0, N_Z - 1)], small_recv.at[0])
    shares = share_all[...].reshape(16 * N_Z, 256)
    quarter = (lax.broadcasted_iota(I32, (16 * N_Z, 1), 0) % 16) // 4
    partial = jnp.zeros((16 * N_Z, 128), F32)
    for k in range(4):
        product = dot(shares, w_out[:, 256 * k : 256 * (k + 1)], ((1,), (1,)))
        partial = partial + jnp.where(quarter == k, product, 0.0)
    fold_row = lax.broadcasted_iota(I32, (16 * N_Z, 16 * N_Z), 0)
    fold_column = lax.broadcasted_iota(I32, (16 * N_Z, 16 * N_Z), 1)
    fold = (fold_row // 16 == fold_column // 16) & (fold_row % 4 == fold_column % 4)
    folded = dot(fold.astype(F32), partial, precision=lax.Precision.HIGHEST)
    back[...] = folded.astype(BF16).reshape(N_Z, 16, 128)
    back_all[z // 2, z % 2] = back[z]
    along_z(
        lambda there: send(
            back.at[there],
            back_all.at[z // 2, z % 2],
            small_send.at[1],
            small_recv.at[1],
            (i, there),
        )
    )

    forward(2)
    forward(3)

    await_bytes(back.at[pl.ds(0, N_Z - 1)], small_recv.at[1])
    back_dev[c] = back_all[:, c]
    to_twin(back_all.at[:, 1 - c], back_dev.at[c], 2)
    sums = []
    for dev in range(2):
        total = jnp.zeros((ROWS, 1), F32)
        for m in range(4):
            total = total + jnp.sum(mixed[2 * m + dev] * mixed[2 * m + dev], axis=-1, keepdims=True)
        sums.append(total)
    await_bytes(back_dev.at[1 - c], twin_recv.at[2])

    def gain_of(m):
        return gain_out_ref[:, pl.ds(pl.multiple_of(HEAD * (2 * m + c), HEAD), HEAD)]

    stat_lane = lax.broadcasted_iota(I32, (ROWS, 128), 1)
    for dev in range(2):
        total = jnp.zeros((ROWS, 1), F32)
        for m in range(4):
            n = 2 * m + dev
            cot_rows = dot(users[dev][:, 0:16], back_dev[dev, m])
            slope = cot_rows * act[n, :, 0:128].astype(F32) * gain_of(m)
            mixed_slope[n] = slope
            gate_cot[n] = cot_rows * gain_of(m) * mixed[n]
            total = total + jnp.sum(slope * mixed[n], axis=-1, keepdims=True)
        column = jnp.where(stat_lane == 0, sums[dev], jnp.where(stat_lane == 1, total, 0.0))
        stats[:, ROWS * dev : ROWS * (dev + 1)] = column.T[0:8]
    to_twin(stats, stats_other, 3)
    await_bytes(stats_other, twin_recv.at[3])
    both_stats = jnp.concatenate(
        [stats[...] + stats_other[...], jnp.zeros((120, 2 * ROWS), F32)], axis=0
    ).T
    for dev in range(2):
        total = both_stats[ROWS * dev : ROWS * (dev + 1), 0:1]
        slope_total = both_stats[ROWS * dev : ROWS * (dev + 1), 1:2]
        norm = lax.rsqrt(total * (1.0 / FEATURES) + 1e-06)
        shared = norm * norm * norm * slope_total * (1.0 / FEATURES)
        for m in range(4):
            n = 2 * m + dev
            gated = mixed[n] * norm * gain_of(m) * act[n, :, 0:128].astype(F32)
            pool_dev[dev, m] = dot(users_t[dev], gated.astype(BF16))[0:8]
            gate_cot[n] = gate_cot[n] * norm
            mixed_cot[n] = (norm * mixed_slope[n] - shared * mixed[n]).astype(BF16)
    pool[:, c] = pool_dev[c]
    to_twin(pool_dev.at[1 - c], pool.at[:, c], 4)

    spots = [(y + away) % 4 for away in (2, 1, 3, 0)]

    def backward(k):
        m = spots[k]
        pre_cots = []
        for dev in range(2):
            n = 2 * m + dev
            value = act[n, :, 128:256]
            query = act[n, :, 256:384]
            key = act[n, :, 384:512]
            cot = mixed_cot[n]
            score_cot = (dot(cot, value, ((1,), (1,))) * attend_slope[n]).astype(BF16)
            value_cot = dot(attend[n], cot, ((0,), (0,)))
            query_cot = dot(score_cot, key)
            key_cot = dot(score_cot, query, ((0,), (0,)))
            act_cot = jnp.concatenate([gate_cot[n], value_cot, query_cot, key_cot], axis=1)
            pre_cots.append((act_cot * act_slope[n]).astype(BF16))
        grad = dot(normed_t[...], jnp.concatenate(pre_cots, axis=0)).astype(BF16)
        for b in range(4):
            held[b, m, :, 0:128, :] = grad[:, 128 * b : 128 * (b + 1)].reshape(N_Z, 128, 128)

    first_rows, z_rows = pl.ds(0, B_ROWS), pl.ds(B_ROWS, A_ROWS)
    last_rows = pl.ds(B_ROWS, STRIPE - B_ROWS)

    def exchange(src, landing, send_sem, recv_sem, device):
        sends.append(send(src, landing, send_sem, recv_sem, device))

    def collect(chunk, landing, recv_sem):
        await_bytes(landing, recv_sem)
        chunk[...] = chunk[...] + landing[...]

    def sum_z(step, k, arrive):
        for d, way in ((0, 1), (1, -1)):
            shard = (z + way * (4 - step if arrive else 5 - step) + N_Z) % N_Z
            among = pl.ds(2 * d, 2) if step == 1 else pl.ds(0, 4)
            chunk = held.at[among, spots[k], shard, z_rows]
            landing = z_in.at[d, step - 1, k, among]
            send_sem, recv_sem = sum_z_send.at[step - 1, k, d], sum_z_recv.at[step - 1, k, d]
            if arrive:
                collect(chunk, landing, recv_sem)
            else:
                exchange(chunk, landing, send_sem, recv_sem, (i, (z + way + N_Z) % N_Z))

    def sum_x(step, k, arrive):
        here, neighbours = plane_axis(False)
        for d, way in ((0, 1), (1, -1)):
            spot = (here + way * (2 - step if arrive else 3 - step) + 4) % 4
            shards = pl.ds(2 * d, 2) if step == 1 else pl.ds(0, 4)
            chunk = held.at[spot, spots[k], shards, first_rows]
            landing = plane_in_0.at[0, step - 1, d, k, shards]
            send_sem, recv_sem = sum_x_send.at[step - 1, k, d], sum_x_recv.at[step - 1, k, d]
            if arrive:
                collect(chunk, landing, recv_sem)
            else:
                exchange(chunk, landing, send_sem, recv_sem, (neighbours[d], z))

    def sum_y(step, arrive):
        here, neighbours = plane_axis(True)
        for d, way in ((0, 1), (1, -1)):
            spot = (here + way * (2 - step if arrive else 3 - step) + 4) % 4
            among = pl.ds(2 * d, 2) if step == 1 else pl.ds(0, 4)
            chunk = held.at[among, spot, pl.ds(4, 4), first_rows]
            landing = plane_in_0.at[1, step - 1, d, among]
            send_sem, recv_sem = sum_y_send.at[step - 1, d], sum_y_recv.at[step - 1, d]
            if arrive:
                collect(chunk, landing, recv_sem)
            else:
                exchange(chunk, landing, send_sem, recv_sem, (neighbours[d], z))

    def sum_second(half, step, arrive):
        here, neighbours = plane_axis(half == 0)
        for d, way in ((0, 1), (1, -1)):
            spot = (here + way * (2 - step if arrive else 3 - step) + 4) % 4
            first, count = (2 * d, 2) if step == 1 else (0, 4)
            shards = pl.ds(4 * half + first, count)
            chunk = held.at[(x, spot)[half], (spot, y)[half], shards, first_rows]
            landing = plane_in_1.at[half, step - 1, d, pl.ds(first, count)]
            send_sem = second_send.at[half, step - 1, d]
            recv_sem = second_recv.at[half, step - 1, d]
            if arrive:
                collect(chunk, landing, recv_sem)
            else:
                exchange(chunk, landing, send_sem, recv_sem, (neighbours[d], z))

    def sum_z_advance(step, k):
        sum_z(step, k, True)
        if step < 4:
            sum_z(step + 1, k, False)

    def sum_z_last(k):
        sum_z_advance(4, k)

        def send_block(n, carry):
            there = (x + n) % 4
            block = held.at[there, spots[k], z, last_rows]
            device = (8 * there + 2 * spots[k] + c, z)
            send(block, last_plane.at[i // 2], last_send.at[0], last_recv.at[0], device)
            return carry

        lax.fori_loop(0 if k < 3 else 1, 4, send_block, 0)

    def sum_x_advance(k):
        sum_x(1, k, True)
        sum_x(2, k, False)

    backward(0)
    sum_z(1, 0, False)
    sum_x(1, 0, False)
    sum_y(1, False)

    await_bytes(pool.at[:, 1 - c], twin_recv.at[4])
    pool_all[z] = pool[z // 2, z % 2]
    along_z(
        lambda there: send(
            pool.at[there // 2, there % 2],
            pool_all.at[z],
            small_send.at[2],
            small_recv.at[2],
            (i, there),
        )
    )
    backward(1)
    sum_z_advance(1, 0)
    sum_z(1, 1, False)
    sum_x_advance(0)
    sum_x(1, 1, False)

    backward(2)
    sum_z_advance(2, 0)
    sum_z_advance(1, 1)
    sum_z(1, 2, False)
    sum_x(2, 0, True)
    sum_second(0, 1, False)
    sum_x_advance(1)
    sum_x(1, 2, False)
    sum_y(1, True)
    sum_y(2, False)

    await_bytes(pool_all.at[pl.ds(0, N_Z - 1)], small_recv.at[2])
    pooled = pool_all[...]
    flat = pooled.reshape(8 * N_Z, 128)
    high = flat.astype(BF16).astype(F32)
    both = dot(jnp.concatenate([high, flat - high], axis=0).astype(BF16), w_out[...])
    products = (both[0 : 8 * N_Z] + both[8 * N_Z :]).reshape(N_Z, 8, FEATURES)
    part[...] = jnp.concatenate(
        [products[:, 0:4, 256 * k : 256 * (k + 1)] for k in range(4)], axis=1
    ).astype(BF16)
    part_all[z] = part[z]
    along_z(
        lambda there: send(
            part.at[there], part_all.at[z], small_send.at[3], small_recv.at[3], (i, there)
        )
    )
    spread = jnp.concatenate([pooled[:, 0:4]] * 4, axis=1).reshape(16 * N_Z, 128)
    for k in range(4):
        block = dot(
            share_all[...].reshape(16 * N_Z, 256),
            jnp.where(quarter == k, spread, 0.0).astype(BF16),
            ((0,), (0,)),
        )
        grad_out_t[4 * k : 4 * (k + 1)] = block.astype(BF16).reshape(4, 2, 32, 128)
    to_twin(grad_out_t.at[:, 1 - c], other_out, 5)

    backward(3)
    sum_z_advance(3, 0)
    sum_z_advance(2, 1)
    sum_z_advance(1, 2)
    sum_z(1, 3, False)
    sum_x(2, 1, True)
    sum_x_advance(2)
    sum_x(1, 3, False)
    sum_y(2, True)
    sum_second(1, 1, False)


    await_bytes(part_all.at[pl.ds(0, N_Z - 1)], small_recv.at[3])
    mean[...] = (
        (jnp.sum(part_all[...].astype(F32), axis=0) + arrived_sum[...]) * inverse
    ).astype(BF16)
    mean_all[x, y, c] = mean[...]

    def mean_along_y(k, carry):
        there = 8 * x + 2 * ((y + k) % 4) + c
        send(mean, mean_all.at[x, y, c], small_send.at[4], small_recv.at[4], (there, z))
        return carry

    def mean_along_x(k, carry):
        there = 8 * ((x + k) % 4) + 2 * y + c
        line = mean_all.at[x, :, c]
        send(line, line, small_send.at[5], small_recv.at[5], (there, z))
        return carry

    lax.fori_loop(1, 4, mean_along_y, 0)
    await_bytes(other_out, twin_recv.at[5])
    held[:, :, z, 128:STRIPE, :] = (grad_out_t[:, c] + other_out[...]).reshape(4, 4, 32, 128)

    sum_z_last(0)
    sum_z_advance(3, 1)
    sum_z_advance(2, 2)
    sum_z_advance(1, 3)
    await_bytes(mean_all.at[0, pl.ds(0, 3), 0], small_recv.at[4])
    lax.fori_loop(1, 4, mean_along_x, 0)
    sum_x(2, 2, True)
    sum_x_advance(3)
    sum_second(0, 1, True)
    sum_second(0, 2, False)
    sum_second(1, 1, True)
    sum_second(1, 2, False)
    sum_z_last(1)
    await_bytes(mean_all.at[pl.ds(0, 3), :, 0], small_recv.at[5])
    to_twin(mean_all.at[:, :, c], mean_all.at[:, :, c], 6)
    sum_z_advance(3, 2)
    sum_z_advance(2, 3)

    sum_x(2, 3, True)
    sum_second(0, 2, True)
    sum_second(1, 2, True)

    along_z(
        lambda there: send(
            held.at[x, y, there, first_rows],
            last_z.at[z],
            last_send.at[1],
            last_recv.at[1],
            (i, there),
        )
    )
    last_z[z] = held[x, y, z, 0:B_ROWS]
    sum_z_last(2)
    sum_z_advance(3, 3)
    sum_z_last(3)

    last_plane[i // 2] = held[x, y, z, B_ROWS:STRIPE]

    await_bytes(last_z.at[pl.ds(0, N_Z - 1)], last_recv.at[1])
    proj_ref[0:B_ROWS, :] = jnp.sum(last_z[...].astype(F32), axis=0)
    await_bytes(mean_all.at[:, :, 1 - c], twin_recv.at[6])
    means = mean_all[...].reshape(16 * N_DP, 256)
    mean_lane = lax.broadcasted_iota(I32, (16, 16 * N_DP), 1)
    for k in range(4):
        wanted = jnp.full((16, 1), -1, I32)
        for u in range(4):
            source = (2 * i - owners_ref[u] + 2 * N_DP) % N_DP
            wanted = jnp.where(user_row == u, 16 * source + 4 * k + u, wanted)
        chosen = dot((mean_lane == wanted).astype(BF16), means)
        pooled_ref[:, 256 * k : 256 * (k + 1)] = chosen[0:4]

    await_bytes(last_plane.at[pl.ds(0, 15)], last_recv.at[0])
    rest = jnp.sum(last_plane[...].astype(F32), axis=0)
    proj_ref[B_ROWS:128, :] = rest[0:A_ROWS]
    out_ref[...] = rest[A_ROWS:]

    for copy in sends:
        copy.wait_send()
    await_bytes(pieces, piece_send)
    await_bytes(outgoing.at[pl.ds(0, N_DP - 1)], tile_send)
    await_bytes(share_all.at[pl.ds(0, N_Z - 1)], small_send.at[0])
    await_bytes(back.at[pl.ds(0, N_Z - 1)], small_send.at[1])
    await_bytes(pool_all.at[pl.ds(0, N_Z - 1)], small_send.at[2])
    await_bytes(part.at[pl.ds(0, N_Z - 1)], small_send.at[3])
    await_bytes(mean_all.at[0, pl.ds(0, 3), 0], small_send.at[4])
    await_bytes(mean_all.at[pl.ds(0, 3), :, 0], small_send.at[5])
    await_bytes(last_plane.at[pl.ds(0, 15)], last_send.at[0])
    await_bytes(last_z.at[pl.ds(0, N_Z - 1)], last_send.at[1])


def finish_kernel(pooled_in, proj_in, out_in, pooled_ref, proj_ref, out_ref):
    pooled_ref[...] = pooled_in[...]
    proj_ref[...] = proj_in[...]
    out_ref[...] = out_in[...]


def body(events, gain_in, gain_out, w_proj, w_out, target, segment, history, owners, pooled_cot):
    any_space, vmem = pl.BlockSpec(memory_space=pl.ANY), pl.BlockSpec(memory_space=pltpu.VMEM)
    smem = pl.BlockSpec(memory_space=pltpu.SMEM)
    dma = pltpu.SemaphoreType.DMA

    def bf16(*shape):
        return pltpu.VMEM(shape, BF16)

    def f32(*shape):
        return pltpu.VMEM(shape, F32)

    pooled, grad_proj, grad_out_t = pl.pallas_call(
        kernel,
        out_shape=(
            jax.ShapeDtypeStruct((4, FEATURES), F32),
            jax.ShapeDtypeStruct((128, 128), F32),
            jax.ShapeDtypeStruct((32, 128), F32),
        ),
        in_specs=[smem] * 4 + [vmem] * 3 + [any_space] * 3,
        out_specs=(vmem, vmem, vmem),
        scratch_shapes=[
            bf16(ROWS, FEATURES),
            bf16(128, FEATURES),
            bf16(N_DP, BLOCK, FEATURES),
            bf16(N_DP, BLOCK, FEATURES),
            f32(128, FEATURES),
            bf16(4, N_Z, 128, 4 * HEAD),
            f32(16, 256),
            bf16(2, ROWS, FEATURES),
            bf16(FEATURES, 2 * ROWS),
            bf16(HEADS, ROWS, 4 * HEAD),
            f32(HEADS, ROWS, 4 * HEAD),
            bf16(HEADS, ROWS, ROWS),
            f32(HEADS, ROWS, ROWS),
            f32(HEADS, ROWS, HEAD),
            f32(HEADS, ROWS, HEAD),
            bf16(HEADS, ROWS, HEAD),
            f32(HEADS, ROWS, HEAD),
            bf16(2, ROWS, 128),
            bf16(2, BLOCK, ROWS),
            f32(2, ROWS, ROWS),
            bf16(16, 256),
            bf16(N_Z, 16, 256),
            bf16(N_Z, 16, 128),
            bf16(4, 2, 16, 128),
            bf16(2, 4, 16, 128),
            f32(8, 2 * ROWS),
            f32(8, 2 * ROWS),
            f32(2, 4, 8, 128),
            f32(4, 2, 8, 128),
            f32(N_Z, 8, 128),
            bf16(N_Z, 16, 256),
            bf16(N_Z, 16, 256),
            bf16(16, 256),
            bf16(4, 4, 2, 16, 256),
            bf16(4, 4, N_Z, STRIPE, 128),
            bf16(16, 2, 32, 128),
            bf16(16, 32, 128),
            bf16(2, 4, 4, 4, A_ROWS, 128),
            bf16(2, 2, 2, 4, 4, B_ROWS, 128),
            bf16(2, 2, 2, 4, B_ROWS, 128),
            bf16(N_Z, B_ROWS, 128),
            bf16(16, STRIPE - B_ROWS, 128),
            dma((3,)),
            dma,
            dma,
            dma,
            dma,
            dma((4, 4, 2)),
            dma((4, 4, 2)),
            dma((2, 2, 2)),
            dma((2, 2, 2)),
            dma((2, 4, 2, 2)),
            dma((2, 4, 2, 2)),
            dma((7,)),
            dma((7,)),
            dma((6,)),
            dma((6,)),
            dma((4, 4, 2)),
            dma((4, 4, 2)),
            dma((2, 4, 2)),
            dma((2, 4, 2)),
            dma((2, 2)),
            dma((2, 2)),
            dma((2, 2, 2)),
            dma((2, 2, 2)),
            dma((2,)),
            dma((2,)),
        ],
        compiler_params=pltpu.CompilerParams(
            collective_id=0, has_side_effects=True, vmem_limit_bytes=62 * 2**20
        ),
        name="step",
    )(
        target,
        owners,
        segment,
        history,
        gain_in.reshape(1, FEATURES),
        gain_out.reshape(1, FEATURES),
        pooled_cot,
        events,
        w_proj,
        w_out,
    )
    pooled, grad_proj, grad_out_t = pl.pallas_call(
        finish_kernel,
        out_shape=(
            jax.ShapeDtypeStruct((4, FEATURES), F32),
            jax.ShapeDtypeStruct((128, 128), F32),
            jax.ShapeDtypeStruct((32, 128), F32),
        ),
        in_specs=[vmem] * 3,
        out_specs=(vmem, vmem, vmem),
        name="finish",
    )(pooled, grad_proj, grad_out_t)
    return (pooled, grad_proj, grad_out_t.T)


def solution(mesh):
    in_specs = (
        P(("dp", "fsdp"), None),
        P(),
        P(),
        P("fsdp", None),
        P("fsdp", None),
        P(("dp", "fsdp")),
        P(("dp", "fsdp")),
        P(("dp", "fsdp")),
        P(("dp", "fsdp")),
        P(("dp", "fsdp"), None),
    )
    out_specs = (P(("dp", "fsdp"), None), P("fsdp", "dp"), P("fsdp", "dp"))
    return jax.shard_map(body, mesh=mesh, in_specs=in_specs, out_specs=out_specs, check_vma=False)
```

```python
import math

import jax
import jax.numpy as jnp
from jax import lax
from jax.experimental import pallas as pl
from jax.experimental.pallas import tpu as pltpu
from jax.sharding import PartitionSpec as P

MESH = pl.DeviceIdType.MESH
BF16, F32, I32 = jnp.bfloat16, jnp.float32, jnp.int32

N_DP, N_Z = 32, 8
HEADS, HEAD = 8, 128
TILE = 12
BLOCK = 16
ROWS = 384
FEATURES = 1024
B_ROWS = 80
A_ROWS = 48
STRIPE = 160


def dot(a, b, dims=((1,), (0,)), precision=None):
    return lax.dot_general(
        a, b, (dims, ((), ())), precision=precision, preferred_element_type=F32
    )


def sigmoid(v):
    return 0.5 * jnp.tanh(0.5 * v) + 0.5


def send(src, dst, send_sem, recv_sem, device):
    copy = pltpu.make_async_remote_copy(
        src_ref=src,
        dst_ref=dst,
        send_sem=send_sem,
        recv_sem=recv_sem,
        device_id=device,
        device_id_type=MESH,
    )
    copy.start()
    return copy


def await_bytes(ref, sem):
    pltpu.make_async_copy(ref, ref, sem).wait()


def kernel(
    target_ref,
    owners_ref,
    segment_ref,
    history_ref,
    gain_in_ref,
    gain_out_ref,
    cot_ref,
    events_hbm,
    proj_hbm,
    out_hbm,
    pooled_ref,
    proj_ref,
    out_ref,
    events,
    w_out,
    outgoing,
    incoming,
    padded_cot,
    weights,
    arrived_sum,
    normed,
    normed_t,
    act,
    act_slope,
    attend,
    attend_slope,
    mixed,
    mixed_slope,
    mixed_cot,
    gate_cot,
    users,
    users_t,
    mask,
    share,
    share_all,
    back,
    back_all,
    back_dev,
    stats,
    stats_other,
    pool_dev,
    pool,
    pool_all,
    part,
    part_all,
    mean,
    mean_all,
    held,
    grad_out_t,
    other_out,
    z_in,
    plane_in_0,
    plane_in_1,
    last_z,
    last_plane,
    load_sem,
    tile_send,
    tile_recv,
    piece_send,
    piece_recv,
    ring_send,
    ring_recv,
    plane_send,
    plane_recv,
    head_send,
    head_recv,
    twin_send,
    twin_recv,
    small_send,
    small_recv,
    sum_z_send,
    sum_z_recv,
    sum_x_send,
    sum_x_recv,
    sum_y_send,
    sum_y_recv,
    second_send,
    second_recv,
    last_send,
    last_recv,
):
    i, z = lax.axis_index("dp"), lax.axis_index("fsdp")
    x, y, c = i // 8, (i // 2) % 4, i % 2
    twin = (i + 1 - 2 * c, z)
    scale = 1.0 / math.sqrt(HEAD)

    load_events = pltpu.make_async_copy(events_hbm, events, load_sem.at[0])
    load_events.start()
    for m in range(4):
        for b in range(4):
            column = pl.multiple_of(128 * (HEADS * b + 2 * m + c), 128)
            pltpu.make_async_copy(
                proj_hbm.at[:, pl.ds(column, 128)],
                weights.at[m, z, :, pl.ds(128 * b, 128)],
                load_sem.at[1],
            ).start()
    load_out = pltpu.make_async_copy(out_hbm, w_out, load_sem.at[2])
    load_out.start()

    lane = lax.broadcasted_iota(I32, (1, ROWS), 1)
    lane_slot, lane_row = lane // TILE, lane % TILE
    goes = jnp.zeros((1, ROWS), I32)
    comes = jnp.zeros((1, ROWS), I32)
    for b in range(N_DP):
        there = target_ref[b]
        goes = jnp.where(lane_slot == b, there, goes)
        comes = jnp.where(lane_slot == b, (2 * i - there + 2 * N_DP) % N_DP, comes)
    block_row = lax.broadcasted_iota(I32, (BLOCK * N_DP, ROWS), 0)
    place = (block_row == BLOCK * goes + lane_row).astype(BF16)
    user_lane = lax.broadcasted_iota(I32, (1, 128), 1)
    user_row = lax.broadcasted_iota(I32, (BLOCK, 1), 0)
    cot_goes = jnp.full((1, 128), -1, I32)
    cot_comes = jnp.full((BLOCK, 1), -1, I32)
    inverse = jnp.ones((BLOCK, 1), F32)
    for u in range(4):
        owner = owners_ref[u]
        origin = (2 * i - owner + 2 * N_DP) % N_DP
        cot_goes = jnp.where(user_lane == u, BLOCK * origin + TILE + u, cot_goes)
        cot_comes = jnp.where(user_row == u, BLOCK * owner + TILE + u, cot_comes)
        inverse = jnp.where(user_row % 4 == u, history_ref[u].astype(F32), inverse)
    inverse = 1.0 / inverse
    cot_row = lax.broadcasted_iota(I32, (BLOCK * N_DP, 128), 0)
    cot_place = (cot_row == cot_goes).astype(BF16)
    padded_cot[...] = jnp.zeros_like(padded_cot)
    padded_cot[0:4, :] = cot_ref[...]

    await_bytes(weights.at[:, z], load_sem.at[1])
    barrier = pltpu.get_barrier_semaphore()

    def greet_dp(k, carry):
        pl.semaphore_signal(barrier, inc=1, device_id=((i + k) % N_DP, z), device_id_type=MESH)
        return carry

    def greet_z(k, carry):
        pl.semaphore_signal(barrier, inc=1, device_id=(i, (z + k) % N_Z), device_id_type=MESH)
        return carry

    lax.fori_loop(1, N_DP, greet_dp, 0)
    lax.fori_loop(1, N_Z, greet_z, 0)

    load_events.wait()
    load_out.wait()
    packed = dot(place, events[...]) + dot(cot_place, padded_cot[...].astype(BF16))
    outgoing[...] = packed.astype(BF16).reshape(N_DP, BLOCK, FEATURES)
    pl.semaphore_wait(barrier, N_DP - 1 + N_Z - 1)

    sends = []

    def to_twin(src, dst, n):
        sends.append(send(src, dst, twin_send.at[n], twin_recv.at[n], twin))

    def along_z(make):
        def step(k, carry):
            make((z + 3 * k) % N_Z)
            return carry

        lax.fori_loop(1, N_Z, step, 0)

    half_of_z = z // 4
    p = (1 - half_of_z) * (4 * x + y) + half_of_z * (4 * y + x)
    piece = weights.at[p % 4, z, pl.ds(64 + 16 * (p // 4), 16)]
    along_z(lambda there: send(piece, piece, piece_send, piece_recv, (i, there)))

    def ring_part(step, way, m):
        shard = (z - way * step + 2 * N_Z) % N_Z
        rows = pl.ds(0, 64) if step < 4 else pl.ds(0 if way > 0 else 32, 32)
        return weights.at[m, shard, rows]

    def ring_step(step, m):
        for d, way in ((0, 1), (1, -1)):
            shard = (z - way * (step - 1) + 2 * N_Z) % N_Z
            rows = pl.ds(0, 64) if step < 4 else pl.ds(0 if way > 0 else 32, 32)
            ref = weights.at[m, shard, rows]
            sends.append(
                send(
                    ref,
                    ref,
                    ring_send.at[step - 1, m, d],
                    ring_recv.at[step - 1, m, d],
                    (i, (z + way + N_Z) % N_Z),
                )
            )

    def ring_advance(step, m):
        for d, way in ((0, 1), (1, -1)):
            await_bytes(ring_part(step, way, m), ring_recv.at[step - 1, m, d])
        if step < 4:
            ring_step(step + 1, m)

    ring_step(1, 0)
    ring_step(1, 1)

    def send_tile(k, carry):
        there = (i + 13 * k) % N_DP
        send(outgoing.at[there], incoming.at[i], tile_send, tile_recv, (there, z))
        return carry

    lax.fori_loop(1, N_DP, send_tile, 0)
    incoming[i] = outgoing[i]

    def plane_axis(along_y):
        here = y if along_y else x
        neighbours = []
        for way in (1, -1):
            there = (here + way + 4) % 4
            neighbours.append(8 * x + 2 * there + c if along_y else 8 * there + 2 * y + c)
        return here, neighbours

    def plane_first(step, arrive):
        for half in range(2):
            here, neighbours = plane_axis(half == 0)
            slow = (x, y)[half]
            for d, way in ((0, 1), (1, -1)):
                origin = (here - way * (step if arrive else step - 1) + 4) % 4
                shards = pl.ds(4 * half, 4) if step == 1 else pl.ds(4 * half + 2 * d, 2)
                ref = weights.at[origin, shards, pl.ds(64 + 16 * slow, 16)]
                send_sem = plane_send.at[step - 1, half, d]
                recv_sem = plane_recv.at[step - 1, half, d]
                if arrive:
                    await_bytes(ref, recv_sem)
                else:
                    sends.append(send(ref, ref, send_sem, recv_sem, (neighbours[d], z)))

    def plane_head(step, m, arrive):
        for half in range(2):
            here, neighbours = plane_axis(half == 1)
            for d, way in ((0, 1), (1, -1)):
                origin = (here - way * (step if arrive else step - 1) + 4) % 4
                shards = pl.ds(4 * half, 4) if step == 1 else pl.ds(4 * half + 2 * d, 2)
                ref = weights.at[m, shards, pl.ds(64 + 16 * origin, 16)]
                send_sem = head_send.at[step - 1, m, half, d]
                recv_sem = head_recv.at[step - 1, m, half, d]
                if arrive:
                    await_bytes(ref, recv_sem)
                else:
                    sends.append(send(ref, ref, send_sem, recv_sem, (neighbours[d], z)))

    def plane_advance(m):
        plane_head(1, m, True)
        plane_head(2, m, False)

    pieces = weights.at[0, pl.ds(0, N_Z - 1), pl.ds(0, 16)]
    await_bytes(pieces, piece_recv)
    plane_first(1, False)
    ring_advance(1, 0)
    ring_step(1, 2)
    ring_advance(1, 1)
    ring_step(1, 3)
    plane_first(1, True)
    plane_first(2, False)
    ring_advance(2, 0)
    ring_advance(1, 2)
    plane_first(2, True)
    plane_head(1, 0, False)
    plane_head(1, 1, False)
    ring_advance(2, 1)
    ring_advance(1, 3)
    ring_advance(3, 0)
    ring_advance(2, 2)
    plane_advance(0)
    plane_head(1, 2, False)
    ring_advance(3, 1)
    ring_advance(2, 3)
    plane_advance(1)
    plane_head(1, 3, False)

    await_bytes(incoming.at[pl.ds(0, N_DP - 1)], tile_recv)
    every = incoming[...].reshape(BLOCK * N_DP, FEATURES)
    fetch = (block_row == BLOCK * comes + lane_row).astype(BF16)
    arrived = dot(fetch, every, ((0,), (0,)))
    cot_lane = lax.broadcasted_iota(I32, (BLOCK, BLOCK * N_DP), 1)
    cot_mine = dot((cot_lane == cot_comes).astype(BF16), every)

    def pack(rows):
        return jnp.concatenate([rows[0:4, 256 * k : 256 * (k + 1)] for k in range(4)], axis=0)

    share[...] = (pack(cot_mine) * inverse).astype(BF16)
    share_all[z] = share[...]
    along_z(
        lambda there: send(share, share_all.at[z], small_send.at[0], small_recv.at[0], (i, there))
    )
    power = jnp.mean(arrived * arrived, axis=-1, keepdims=True)
    rows = (arrived * lax.rsqrt(power + 1e-06) * gain_in_ref[...]).astype(BF16)
    normed[c] = rows
    to_twin(normed.at[c], normed.at[c], 0)

    starts, ends = [], []
    for u in range(4):
        start = jnp.int32(0)
        for b in range(N_DP):
            start = start + jnp.where(segment_ref[b] < u, TILE, 0)
        starts.append(start)
        ends.append(start + history_ref[u])

    def members(event, user, stops):
        found = jnp.zeros(event.shape, jnp.bool_)
        for u in range(4):
            found = found | ((user == u) & (event >= starts[u]) & (event < stops[u]))
        return found.astype(F32).astype(BF16)

    event = lax.broadcasted_iota(I32, (ROWS, 128), 0)
    user = lax.broadcasted_iota(I32, (ROWS, 128), 1)
    users[c] = members(event, user, ends) + members(event, user - 16, starts[1:] + [ROWS])
    to_twin(users.at[c], users.at[c], 1)
    sum_t = members(
        lax.broadcasted_iota(I32, (BLOCK, ROWS), 1),
        lax.broadcasted_iota(I32, (BLOCK, ROWS), 0),
        ends,
    )
    arrived_sum[...] = pack(dot(sum_t, arrived.astype(BF16)))

    ring_advance(3, 2)
    ring_advance(3, 3)
    plane_advance(2)
    plane_advance(3)

    await_bytes(users.at[1 - c], twin_recv.at[1])
    await_bytes(normed.at[1 - c], twin_recv.at[0])
    shift_row = lax.broadcasted_iota(I32, (128, 128), 0)
    shift_column = lax.broadcasted_iota(I32, (128, 128), 1)
    shift = ((shift_row == shift_column + 16) & (shift_column < 4)).astype(F32).astype(BF16)
    keep = ((shift_row == shift_column) & (shift_column < 4)).astype(F32).astype(BF16)
    for dev in range(2):
        found = users[dev]
        owned = dot(found, shift).astype(BF16)
        valid = dot(found, keep).astype(BF16)
        same = dot(owned, valid, ((1,), (1,)))
        query_row = lax.broadcasted_iota(I32, (ROWS, ROWS), 0)
        key_row = lax.broadcasted_iota(I32, (ROWS, ROWS), 1)
        mask[dev] = jnp.where(key_row <= query_row, same, 0.0)
        users_t[dev] = dot(keep[0:BLOCK], found, ((1,), (1,))).astype(BF16)
        normed_t[:, ROWS * dev : ROWS * (dev + 1)] = normed[dev].T

    def forward(m):
        ring_advance(4, m)
        plane_head(2, m, True)
        weight = weights[m].reshape(FEATURES, 4 * HEAD)
        for dev in range(2):
            n = 2 * m + dev
            pre = dot(normed[dev], weight)
            sig = sigmoid(pre)
            silu = pre * sig
            act_slope[n] = sig + silu * (1.0 - sig)
            act[n] = silu.astype(BF16)
        for dev in range(2):
            n = 2 * m + dev
            value = act[n, :, 128:256]
            query = act[n, :, 256:384]
            key = act[n, :, 384:512]
            scores = dot(query, key, ((1,), (1,))) * scale
            sig = sigmoid(scores)
            silu = scores * sig
            attend_slope[n] = (sig + silu * (1.0 - sig)) * (mask[dev] * scale)
            attend[n] = (silu * mask[dev]).astype(BF16)
            mixed[n] = dot(attend[n], value)

    forward(0)
    forward(1)

    await_bytes(share_all.at[pl.ds(0, N_Z - 1)], small_recv.at[0])
    shares = share_all[...].reshape(16 * N_Z, 256)
    quarter = (lax.broadcasted_iota(I32, (16 * N_Z, 1), 0) % 16) // 4
    partial = jnp.zeros((16 * N_Z, 128), F32)
    for k in range(4):
        product = dot(shares, w_out[:, 256 * k : 256 * (k + 1)], ((1,), (1,)))
        partial = partial + jnp.where(quarter == k, product, 0.0)
    fold_row = lax.broadcasted_iota(I32, (16 * N_Z, 16 * N_Z), 0)
    fold_column = lax.broadcasted_iota(I32, (16 * N_Z, 16 * N_Z), 1)
    fold = (fold_row // 16 == fold_column // 16) & (fold_row % 4 == fold_column % 4)
    folded = dot(fold.astype(F32), partial, precision=lax.Precision.HIGHEST)
    back[...] = folded.astype(BF16).reshape(N_Z, 16, 128)
    back_all[z // 2, z % 2] = back[z]
    along_z(
        lambda there: send(
            back.at[there],
            back_all.at[z // 2, z % 2],
            small_send.at[1],
            small_recv.at[1],
            (i, there),
        )
    )

    forward(2)
    forward(3)

    await_bytes(back.at[pl.ds(0, N_Z - 1)], small_recv.at[1])
    back_dev[c] = back_all[:, c]
    to_twin(back_all.at[:, 1 - c], back_dev.at[c], 2)
    sums = []
    for dev in range(2):
        total = jnp.zeros((ROWS, 1), F32)
        for m in range(4):
            total = total + jnp.sum(mixed[2 * m + dev] * mixed[2 * m + dev], axis=-1, keepdims=True)
        sums.append(total)
    await_bytes(back_dev.at[1 - c], twin_recv.at[2])

    def gain_of(m):
        return gain_out_ref[:, pl.ds(pl.multiple_of(HEAD * (2 * m + c), HEAD), HEAD)]

    stat_lane = lax.broadcasted_iota(I32, (ROWS, 128), 1)
    for dev in range(2):
        total = jnp.zeros((ROWS, 1), F32)
        for m in range(4):
            n = 2 * m + dev
            cot_rows = dot(users[dev][:, 0:16], back_dev[dev, m])
            slope = cot_rows * act[n, :, 0:128].astype(F32) * gain_of(m)
            mixed_slope[n] = slope
            gate_cot[n] = cot_rows * gain_of(m) * mixed[n]
            total = total + jnp.sum(slope * mixed[n], axis=-1, keepdims=True)
        column = jnp.where(stat_lane == 0, sums[dev], jnp.where(stat_lane == 1, total, 0.0))
        stats[:, ROWS * dev : ROWS * (dev + 1)] = column.T[0:8]
    to_twin(stats, stats_other, 3)
    await_bytes(stats_other, twin_recv.at[3])
    both_stats = jnp.concatenate(
        [stats[...] + stats_other[...], jnp.zeros((120, 2 * ROWS), F32)], axis=0
    ).T
    for dev in range(2):
        total = both_stats[ROWS * dev : ROWS * (dev + 1), 0:1]
        slope_total = both_stats[ROWS * dev : ROWS * (dev + 1), 1:2]
        norm = lax.rsqrt(total * (1.0 / FEATURES) + 1e-06)
        shared = norm * norm * norm * slope_total * (1.0 / FEATURES)
        for m in range(4):
            n = 2 * m + dev
            gated = mixed[n] * norm * gain_of(m) * act[n, :, 0:128].astype(F32)
            pool_dev[dev, m] = dot(users_t[dev], gated.astype(BF16))[0:8]
            gate_cot[n] = gate_cot[n] * norm
            mixed_cot[n] = (norm * mixed_slope[n] - shared * mixed[n]).astype(BF16)
    pool[:, c] = pool_dev[c]
    to_twin(pool_dev.at[1 - c], pool.at[:, c], 4)

    spots = [(y + away) % 4 for away in (2, 1, 3, 0)]

    def backward(k):
        m = spots[k]
        pre_cots = []
        for dev in range(2):
            n = 2 * m + dev
            value = act[n, :, 128:256]
            query = act[n, :, 256:384]
            key = act[n, :, 384:512]
            cot = mixed_cot[n]
            score_cot = (dot(cot, value, ((1,), (1,))) * attend_slope[n]).astype(BF16)
            value_cot = dot(attend[n], cot, ((0,), (0,)))
            query_cot = dot(score_cot, key)
            key_cot = dot(score_cot, query, ((0,), (0,)))
            act_cot = jnp.concatenate([gate_cot[n], value_cot, query_cot, key_cot], axis=1)
            pre_cots.append((act_cot * act_slope[n]).astype(BF16))
        grad = dot(normed_t[...], jnp.concatenate(pre_cots, axis=0)).astype(BF16)
        for b in range(4):
            held[b, m, :, 0:128, :] = grad[:, 128 * b : 128 * (b + 1)].reshape(N_Z, 128, 128)

    first_rows, z_rows = pl.ds(0, B_ROWS), pl.ds(B_ROWS, A_ROWS)
    last_rows = pl.ds(B_ROWS, STRIPE - B_ROWS)

    def exchange(src, landing, send_sem, recv_sem, device):
        sends.append(send(src, landing, send_sem, recv_sem, device))

    def collect(chunk, landing, recv_sem):
        await_bytes(landing, recv_sem)
        chunk[...] = chunk[...] + landing[...]

    def sum_z(step, k, arrive):
        for d, way in ((0, 1), (1, -1)):
            shard = (z + way * (4 - step if arrive else 5 - step) + N_Z) % N_Z
            among = pl.ds(2 * d, 2) if step == 1 else pl.ds(0, 4)
            chunk = held.at[among, spots[k], shard, z_rows]
            landing = z_in.at[d, step - 1, k, among]
            send_sem, recv_sem = sum_z_send.at[step - 1, k, d], sum_z_recv.at[step - 1, k, d]
            if arrive:
                collect(chunk, landing, recv_sem)
            else:
                exchange(chunk, landing, send_sem, recv_sem, (i, (z + way + N_Z) % N_Z))

    def sum_x(step, k, arrive):
        here, neighbours = plane_axis(False)
        for d, way in ((0, 1), (1, -1)):
            spot = (here + way * (2 - step if arrive else 3 - step) + 4) % 4
            shards = pl.ds(2 * d, 2) if step == 1 else pl.ds(0, 4)
            chunk = held.at[spot, spots[k], shards, first_rows]
            landing = plane_in_0.at[0, step - 1, d, k, shards]
            send_sem, recv_sem = sum_x_send.at[step - 1, k, d], sum_x_recv.at[step - 1, k, d]
            if arrive:
                collect(chunk, landing, recv_sem)
            else:
                exchange(chunk, landing, send_sem, recv_sem, (neighbours[d], z))

    def sum_y(step, arrive):
        here, neighbours = plane_axis(True)
        for d, way in ((0, 1), (1, -1)):
            spot = (here + way * (2 - step if arrive else 3 - step) + 4) % 4
            among = pl.ds(2 * d, 2) if step == 1 else pl.ds(0, 4)
            chunk = held.at[among, spot, pl.ds(4, 4), first_rows]
            landing = plane_in_0.at[1, step - 1, d, among]
            send_sem, recv_sem = sum_y_send.at[step - 1, d], sum_y_recv.at[step - 1, d]
            if arrive:
                collect(chunk, landing, recv_sem)
            else:
                exchange(chunk, landing, send_sem, recv_sem, (neighbours[d], z))

    def sum_second(half, step, arrive):
        here, neighbours = plane_axis(half == 0)
        for d, way in ((0, 1), (1, -1)):
            spot = (here + way * (2 - step if arrive else 3 - step) + 4) % 4
            first, count = (2 * d, 2) if step == 1 else (0, 4)
            shards = pl.ds(4 * half + first, count)
            chunk = held.at[(x, spot)[half], (spot, y)[half], shards, first_rows]
            landing = plane_in_1.at[half, step - 1, d, pl.ds(first, count)]
            send_sem = second_send.at[half, step - 1, d]
            recv_sem = second_recv.at[half, step - 1, d]
            if arrive:
                collect(chunk, landing, recv_sem)
            else:
                exchange(chunk, landing, send_sem, recv_sem, (neighbours[d], z))

    def sum_z_advance(step, k):
        sum_z(step, k, True)
        if step < 4:
            sum_z(step + 1, k, False)

    def sum_z_last(k):
        sum_z_advance(4, k)

        def send_block(n, carry):
            there = (x + n) % 4
            block = held.at[there, spots[k], z, last_rows]
            device = (8 * there + 2 * spots[k] + c, z)
            send(block, last_plane.at[i // 2], last_send.at[0], last_recv.at[0], device)
            return carry

        lax.fori_loop(0 if k < 3 else 1, 4, send_block, 0)

    def sum_x_advance(k):
        sum_x(1, k, True)
        sum_x(2, k, False)

    backward(0)
    sum_z(1, 0, False)
    sum_x(1, 0, False)
    sum_y(1, False)

    await_bytes(pool.at[:, 1 - c], twin_recv.at[4])
    pool_all[z] = pool[z // 2, z % 2]
    along_z(
        lambda there: send(
            pool.at[there // 2, there % 2],
            pool_all.at[z],
            small_send.at[2],
            small_recv.at[2],
            (i, there),
        )
    )
    backward(1)
    sum_z_advance(1, 0)
    sum_z(1, 1, False)
    sum_x_advance(0)
    sum_x(1, 1, False)

    backward(2)
    sum_z_advance(2, 0)
    sum_z_advance(1, 1)
    sum_z(1, 2, False)
    sum_x(2, 0, True)
    sum_second(0, 1, False)
    sum_x_advance(1)
    sum_x(1, 2, False)
    sum_y(1, True)
    sum_y(2, False)

    await_bytes(pool_all.at[pl.ds(0, N_Z - 1)], small_recv.at[2])
    pooled = pool_all[...]
    flat = pooled.reshape(8 * N_Z, 128)
    high = flat.astype(BF16).astype(F32)
    both = dot(jnp.concatenate([high, flat - high], axis=0).astype(BF16), w_out[...])
    products = (both[0 : 8 * N_Z] + both[8 * N_Z :]).reshape(N_Z, 8, FEATURES)
    part[...] = jnp.concatenate(
        [products[:, 0:4, 256 * k : 256 * (k + 1)] for k in range(4)], axis=1
    ).astype(BF16)
    part_all[z] = part[z]
    along_z(
        lambda there: send(
            part.at[there], part_all.at[z], small_send.at[3], small_recv.at[3], (i, there)
        )
    )
    spread = jnp.concatenate([pooled[:, 0:4]] * 4, axis=1).reshape(16 * N_Z, 128)
    for k in range(4):
        block = dot(
            share_all[...].reshape(16 * N_Z, 256),
            jnp.where(quarter == k, spread, 0.0).astype(BF16),
            ((0,), (0,)),
        )
        grad_out_t[4 * k : 4 * (k + 1)] = block.astype(BF16).reshape(4, 2, 32, 128)
    to_twin(grad_out_t.at[:, 1 - c], other_out, 5)

    backward(3)
    sum_z_advance(3, 0)
    sum_z_advance(2, 1)
    sum_z_advance(1, 2)
    sum_z(1, 3, False)
    sum_x(2, 1, True)
    sum_x_advance(2)
    sum_x(1, 3, False)
    sum_y(2, True)
    sum_second(1, 1, False)


    await_bytes(part_all.at[pl.ds(0, N_Z - 1)], small_recv.at[3])
    mean[...] = (
        (jnp.sum(part_all[...].astype(F32), axis=0) + arrived_sum[...]) * inverse
    ).astype(BF16)
    mean_all[x, y, c] = mean[...]

    def mean_along_y(k, carry):
        there = 8 * x + 2 * ((y + k) % 4) + c
        send(mean, mean_all.at[x, y, c], small_send.at[4], small_recv.at[4], (there, z))
        return carry

    def mean_along_x(k, carry):
        there = 8 * ((x + k) % 4) + 2 * y + c
        line = mean_all.at[x, :, c]
        send(line, line, small_send.at[5], small_recv.at[5], (there, z))
        return carry

    lax.fori_loop(1, 4, mean_along_y, 0)
    await_bytes(other_out, twin_recv.at[5])
    held[:, :, z, 128:STRIPE, :] = (grad_out_t[:, c] + other_out[...]).reshape(4, 4, 32, 128)

    sum_z_last(0)
    sum_z_advance(1, 3)
    sum_z_advance(3, 1)
    sum_z_advance(2, 2)
    sum_x_advance(3)
    await_bytes(mean_all.at[0, pl.ds(0, 3), 0], small_recv.at[4])
    lax.fori_loop(1, 4, mean_along_x, 0)
    sum_x(2, 2, True)
    sum_second(0, 1, True)
    sum_second(0, 2, False)
    sum_z_advance(2, 3)
    sum_second(1, 1, True)
    sum_second(1, 2, False)
    sum_z_last(1)
    sum_z_advance(3, 2)
    sum_z_advance(3, 3)
    await_bytes(mean_all.at[pl.ds(0, 3), :, 0], small_recv.at[5])
    to_twin(mean_all.at[:, :, c], mean_all.at[:, :, c], 6)
    sum_x(2, 3, True)
    sum_second(0, 2, True)
    sum_second(1, 2, True)

    along_z(
        lambda there: send(
            held.at[x, y, there, first_rows],
            last_z.at[z],
            last_send.at[1],
            last_recv.at[1],
            (i, there),
        )
    )
    last_z[z] = held[x, y, z, 0:B_ROWS]
    sum_z_last(2)
    sum_z_last(3)

    last_plane[i // 2] = held[x, y, z, B_ROWS:STRIPE]

    await_bytes(last_z.at[pl.ds(0, N_Z - 1)], last_recv.at[1])
    proj_ref[0:B_ROWS, :] = jnp.sum(last_z[...].astype(F32), axis=0)
    await_bytes(mean_all.at[:, :, 1 - c], twin_recv.at[6])
    means = mean_all[...].reshape(16 * N_DP, 256)
    mean_lane = lax.broadcasted_iota(I32, (16, 16 * N_DP), 1)
    for k in range(4):
        wanted = jnp.full((16, 1), -1, I32)
        for u in range(4):
            source = (2 * i - owners_ref[u] + 2 * N_DP) % N_DP
            wanted = jnp.where(user_row == u, 16 * source + 4 * k + u, wanted)
        chosen = dot((mean_lane == wanted).astype(BF16), means)
        pooled_ref[:, 256 * k : 256 * (k + 1)] = chosen[0:4]

    await_bytes(last_plane.at[pl.ds(0, 15)], last_recv.at[0])
    rest = jnp.sum(last_plane[...].astype(F32), axis=0)
    proj_ref[B_ROWS:128, :] = rest[0:A_ROWS]
    out_ref[...] = rest[A_ROWS:]

    for copy in sends:
        copy.wait_send()
    await_bytes(pieces, piece_send)
    await_bytes(outgoing.at[pl.ds(0, N_DP - 1)], tile_send)
    await_bytes(share_all.at[pl.ds(0, N_Z - 1)], small_send.at[0])
    await_bytes(back.at[pl.ds(0, N_Z - 1)], small_send.at[1])
    await_bytes(pool_all.at[pl.ds(0, N_Z - 1)], small_send.at[2])
    await_bytes(part.at[pl.ds(0, N_Z - 1)], small_send.at[3])
    await_bytes(mean_all.at[0, pl.ds(0, 3), 0], small_send.at[4])
    await_bytes(mean_all.at[pl.ds(0, 3), :, 0], small_send.at[5])
    await_bytes(last_plane.at[pl.ds(0, 15)], last_send.at[0])
    await_bytes(last_z.at[pl.ds(0, N_Z - 1)], last_send.at[1])


def finish_kernel(pooled_in, proj_in, out_in, pooled_ref, proj_ref, out_ref):
    pooled_ref[...] = pooled_in[...]
    proj_ref[...] = proj_in[...]
    out_ref[...] = out_in[...]


def body(events, gain_in, gain_out, w_proj, w_out, target, segment, history, owners, pooled_cot):
    any_space, vmem = pl.BlockSpec(memory_space=pl.ANY), pl.BlockSpec(memory_space=pltpu.VMEM)
    smem = pl.BlockSpec(memory_space=pltpu.SMEM)
    dma = pltpu.SemaphoreType.DMA

    def bf16(*shape):
        return pltpu.VMEM(shape, BF16)

    def f32(*shape):
        return pltpu.VMEM(shape, F32)

    pooled, grad_proj, grad_out_t = pl.pallas_call(
        kernel,
        out_shape=(
            jax.ShapeDtypeStruct((4, FEATURES), F32),
            jax.ShapeDtypeStruct((128, 128), F32),
            jax.ShapeDtypeStruct((32, 128), F32),
        ),
        in_specs=[smem] * 4 + [vmem] * 3 + [any_space] * 3,
        out_specs=(vmem, vmem, vmem),
        scratch_shapes=[
            bf16(ROWS, FEATURES),
            bf16(128, FEATURES),
            bf16(N_DP, BLOCK, FEATURES),
            bf16(N_DP, BLOCK, FEATURES),
            f32(128, FEATURES),
            bf16(4, N_Z, 128, 4 * HEAD),
            f32(16, 256),
            bf16(2, ROWS, FEATURES),
            bf16(FEATURES, 2 * ROWS),
            bf16(HEADS, ROWS, 4 * HEAD),
            f32(HEADS, ROWS, 4 * HEAD),
            bf16(HEADS, ROWS, ROWS),
            f32(HEADS, ROWS, ROWS),
            f32(HEADS, ROWS, HEAD),
            f32(HEADS, ROWS, HEAD),
            bf16(HEADS, ROWS, HEAD),
            f32(HEADS, ROWS, HEAD),
            bf16(2, ROWS, 128),
            bf16(2, BLOCK, ROWS),
            f32(2, ROWS, ROWS),
            bf16(16, 256),
            bf16(N_Z, 16, 256),
            bf16(N_Z, 16, 128),
            bf16(4, 2, 16, 128),
            bf16(2, 4, 16, 128),
            f32(8, 2 * ROWS),
            f32(8, 2 * ROWS),
            f32(2, 4, 8, 128),
            f32(4, 2, 8, 128),
            f32(N_Z, 8, 128),
            bf16(N_Z, 16, 256),
            bf16(N_Z, 16, 256),
            bf16(16, 256),
            bf16(4, 4, 2, 16, 256),
            bf16(4, 4, N_Z, STRIPE, 128),
            bf16(16, 2, 32, 128),
            bf16(16, 32, 128),
            bf16(2, 4, 4, 4, A_ROWS, 128),
            bf16(2, 2, 2, 4, 4, B_ROWS, 128),
            bf16(2, 2, 2, 4, B_ROWS, 128),
            bf16(N_Z, B_ROWS, 128),
            bf16(16, STRIPE - B_ROWS, 128),
            dma((3,)),
            dma,
            dma,
            dma,
            dma,
            dma((4, 4, 2)),
            dma((4, 4, 2)),
            dma((2, 2, 2)),
            dma((2, 2, 2)),
            dma((2, 4, 2, 2)),
            dma((2, 4, 2, 2)),
            dma((7,)),
            dma((7,)),
            dma((6,)),
            dma((6,)),
            dma((4, 4, 2)),
            dma((4, 4, 2)),
            dma((2, 4, 2)),
            dma((2, 4, 2)),
            dma((2, 2)),
            dma((2, 2)),
            dma((2, 2, 2)),
            dma((2, 2, 2)),
            dma((2,)),
            dma((2,)),
        ],
        compiler_params=pltpu.CompilerParams(
            collective_id=0, has_side_effects=True, vmem_limit_bytes=62 * 2**20
        ),
        name="step",
    )(
        target,
        owners,
        segment,
        history,
        gain_in.reshape(1, FEATURES),
        gain_out.reshape(1, FEATURES),
        pooled_cot,
        events,
        w_proj,
        w_out,
    )
    pooled, grad_proj, grad_out_t = pl.pallas_call(
        finish_kernel,
        out_shape=(
            jax.ShapeDtypeStruct((4, FEATURES), F32),
            jax.ShapeDtypeStruct((128, 128), F32),
            jax.ShapeDtypeStruct((32, 128), F32),
        ),
        in_specs=[vmem] * 3,
        out_specs=(vmem, vmem, vmem),
        name="finish",
    )(pooled, grad_proj, grad_out_t)
    return (pooled, grad_proj, grad_out_t.T)


def solution(mesh):
    in_specs = (
        P(("dp", "fsdp"), None),
        P(),
        P(),
        P("fsdp", None),
        P("fsdp", None),
        P(("dp", "fsdp")),
        P(("dp", "fsdp")),
        P(("dp", "fsdp")),
        P(("dp", "fsdp")),
        P(("dp", "fsdp"), None),
    )
    out_specs = (P(("dp", "fsdp"), None), P("fsdp", "dp"), P("fsdp", "dp"))
    return jax.shard_map(body, mesh=mesh, in_specs=in_specs, out_specs=out_specs, check_vma=False)
```

```python
import math

import jax
import jax.numpy as jnp
from jax import lax
from jax.experimental import pallas as pl
from jax.experimental.pallas import tpu as pltpu
from jax.sharding import PartitionSpec as P

MESH = pl.DeviceIdType.MESH
BF16, F32, I32 = jnp.bfloat16, jnp.float32, jnp.int32

N_DP, N_Z = 32, 8
HEADS, HEAD = 8, 128
TILE = 12
BLOCK = 16
ROWS = 384
FEATURES = 1024
B_ROWS = 80
A_ROWS = 48
STRIPE = 160


def dot(a, b, dims=((1,), (0,)), precision=None):
    return lax.dot_general(
        a, b, (dims, ((), ())), precision=precision, preferred_element_type=F32
    )


def sigmoid(v):
    return 0.5 * jnp.tanh(0.5 * v) + 0.5


def send(src, dst, send_sem, recv_sem, device):
    copy = pltpu.make_async_remote_copy(
        src_ref=src,
        dst_ref=dst,
        send_sem=send_sem,
        recv_sem=recv_sem,
        device_id=device,
        device_id_type=MESH,
    )
    copy.start()
    return copy


def await_bytes(ref, sem):
    pltpu.make_async_copy(ref, ref, sem).wait()


def kernel(
    target_ref,
    owners_ref,
    segment_ref,
    history_ref,
    gain_in_ref,
    gain_out_ref,
    cot_ref,
    events_hbm,
    proj_hbm,
    out_hbm,
    pooled_ref,
    proj_ref,
    out_ref,
    events,
    w_out,
    outgoing,
    incoming,
    padded_cot,
    weights,
    arrived_sum,
    normed,
    normed_t,
    act,
    act_slope,
    attend,
    attend_slope,
    mixed,
    mixed_slope,
    mixed_cot,
    gate_cot,
    users,
    users_t,
    mask,
    share,
    share_all,
    back,
    back_all,
    back_dev,
    stats,
    stats_other,
    pool_dev,
    pool,
    pool_all,
    part,
    part_all,
    mean,
    mean_all,
    held,
    grad_out_t,
    other_out,
    z_in,
    plane_in_0,
    plane_in_1,
    last_z,
    last_plane,
    load_sem,
    tile_send,
    tile_recv,
    piece_send,
    piece_recv,
    ring_send,
    ring_recv,
    plane_send,
    plane_recv,
    head_send,
    head_recv,
    twin_send,
    twin_recv,
    small_send,
    small_recv,
    sum_z_send,
    sum_z_recv,
    sum_x_send,
    sum_x_recv,
    sum_y_send,
    sum_y_recv,
    second_send,
    second_recv,
    last_send,
    last_recv,
):
    i, z = lax.axis_index("dp"), lax.axis_index("fsdp")
    x, y, c = i // 8, (i // 2) % 4, i % 2
    twin = (i + 1 - 2 * c, z)
    scale = 1.0 / math.sqrt(HEAD)

    load_events = pltpu.make_async_copy(events_hbm, events, load_sem.at[0])
    load_events.start()
    for m in range(4):
        for b in range(4):
            column = pl.multiple_of(128 * (HEADS * b + 2 * m + c), 128)
            pltpu.make_async_copy(
                proj_hbm.at[:, pl.ds(column, 128)],
                weights.at[m, z, :, pl.ds(128 * b, 128)],
                load_sem.at[1],
            ).start()
    load_out = pltpu.make_async_copy(out_hbm, w_out, load_sem.at[2])
    load_out.start()

    lane = lax.broadcasted_iota(I32, (1, ROWS), 1)
    lane_slot, lane_row = lane // TILE, lane % TILE
    goes = jnp.zeros((1, ROWS), I32)
    comes = jnp.zeros((1, ROWS), I32)
    for b in range(N_DP):
        there = target_ref[b]
        goes = jnp.where(lane_slot == b, there, goes)
        comes = jnp.where(lane_slot == b, (2 * i - there + 2 * N_DP) % N_DP, comes)
    block_row = lax.broadcasted_iota(I32, (BLOCK * N_DP, ROWS), 0)
    place = (block_row == BLOCK * goes + lane_row).astype(BF16)
    user_lane = lax.broadcasted_iota(I32, (1, 128), 1)
    user_row = lax.broadcasted_iota(I32, (BLOCK, 1), 0)
    cot_goes = jnp.full((1, 128), -1, I32)
    cot_comes = jnp.full((BLOCK, 1), -1, I32)
    inverse = jnp.ones((BLOCK, 1), F32)
    for u in range(4):
        owner = owners_ref[u]
        origin = (2 * i - owner + 2 * N_DP) % N_DP
        cot_goes = jnp.where(user_lane == u, BLOCK * origin + TILE + u, cot_goes)
        cot_comes = jnp.where(user_row == u, BLOCK * owner + TILE + u, cot_comes)
        inverse = jnp.where(user_row % 4 == u, history_ref[u].astype(F32), inverse)
    inverse = 1.0 / inverse
    cot_row = lax.broadcasted_iota(I32, (BLOCK * N_DP, 128), 0)
    cot_place = (cot_row == cot_goes).astype(BF16)
    padded_cot[...] = jnp.zeros_like(padded_cot)
    padded_cot[0:4, :] = cot_ref[...]

    await_bytes(weights.at[:, z], load_sem.at[1])
    barrier = pltpu.get_barrier_semaphore()

    def greet_dp(k, carry):
        pl.semaphore_signal(barrier, inc=1, device_id=((i + k) % N_DP, z), device_id_type=MESH)
        return carry

    def greet_z(k, carry):
        pl.semaphore_signal(barrier, inc=1, device_id=(i, (z + k) % N_Z), device_id_type=MESH)
        return carry

    lax.fori_loop(1, N_DP, greet_dp, 0)
    lax.fori_loop(1, N_Z, greet_z, 0)

    load_events.wait()
    load_out.wait()
    packed = dot(place, events[...]) + dot(cot_place, padded_cot[...].astype(BF16))
    outgoing[...] = packed.astype(BF16).reshape(N_DP, BLOCK, FEATURES)
    pl.semaphore_wait(barrier, N_DP - 1 + N_Z - 1)

    sends = []

    def to_twin(src, dst, n):
        sends.append(send(src, dst, twin_send.at[n], twin_recv.at[n], twin))

    def along_z(make):
        def step(k, carry):
            make((z + 3 * k) % N_Z)
            return carry

        lax.fori_loop(1, N_Z, step, 0)

    half_of_z = z // 4
    p = (1 - half_of_z) * (4 * x + y) + half_of_z * (4 * y + x)
    piece = weights.at[p % 4, z, pl.ds(64 + 16 * (p // 4), 16)]
    along_z(lambda there: send(piece, piece, piece_send, piece_recv, (i, there)))

    def ring_part(step, way, m):
        shard = (z - way * step + 2 * N_Z) % N_Z
        rows = pl.ds(0, 64) if step < 4 else pl.ds(0 if way > 0 else 32, 32)
        return weights.at[m, shard, rows]

    def ring_step(step, m):
        for d, way in ((0, 1), (1, -1)):
            shard = (z - way * (step - 1) + 2 * N_Z) % N_Z
            rows = pl.ds(0, 64) if step < 4 else pl.ds(0 if way > 0 else 32, 32)
            ref = weights.at[m, shard, rows]
            sends.append(
                send(
                    ref,
                    ref,
                    ring_send.at[step - 1, m, d],
                    ring_recv.at[step - 1, m, d],
                    (i, (z + way + N_Z) % N_Z),
                )
            )

    def ring_advance(step, m):
        for d, way in ((0, 1), (1, -1)):
            await_bytes(ring_part(step, way, m), ring_recv.at[step - 1, m, d])
        if step < 4:
            ring_step(step + 1, m)

    ring_step(1, 0)
    ring_step(1, 1)

    def send_tile(k, carry):
        there = (i + 13 * k) % N_DP
        send(outgoing.at[there], incoming.at[i], tile_send, tile_recv, (there, z))
        return carry

    lax.fori_loop(1, N_DP, send_tile, 0)
    incoming[i] = outgoing[i]

    def plane_axis(along_y):
        here = y if along_y else x
        neighbours = []
        for way in (1, -1):
            there = (here + way + 4) % 4
            neighbours.append(8 * x + 2 * there + c if along_y else 8 * there + 2 * y + c)
        return here, neighbours

    def plane_first(step, arrive):
        for half in range(2):
            here, neighbours = plane_axis(half == 0)
            slow = (x, y)[half]
            for d, way in ((0, 1), (1, -1)):
                origin = (here - way * (step if arrive else step - 1) + 4) % 4
                shards = pl.ds(4 * half, 4) if step == 1 else pl.ds(4 * half + 2 * d, 2)
                ref = weights.at[origin, shards, pl.ds(64 + 16 * slow, 16)]
                send_sem = plane_send.at[step - 1, half, d]
                recv_sem = plane_recv.at[step - 1, half, d]
                if arrive:
                    await_bytes(ref, recv_sem)
                else:
                    sends.append(send(ref, ref, send_sem, recv_sem, (neighbours[d], z)))

    def plane_head(step, m, arrive):
        for half in range(2):
            here, neighbours = plane_axis(half == 1)
            for d, way in ((0, 1), (1, -1)):
                origin = (here - way * (step if arrive else step - 1) + 4) % 4
                shards = pl.ds(4 * half, 4) if step == 1 else pl.ds(4 * half + 2 * d, 2)
                ref = weights.at[m, shards, pl.ds(64 + 16 * origin, 16)]
                send_sem = head_send.at[step - 1, m, half, d]
                recv_sem = head_recv.at[step - 1, m, half, d]
                if arrive:
                    await_bytes(ref, recv_sem)
                else:
                    sends.append(send(ref, ref, send_sem, recv_sem, (neighbours[d], z)))

    def plane_advance(m):
        plane_head(1, m, True)
        plane_head(2, m, False)

    pieces = weights.at[0, pl.ds(0, N_Z - 1), pl.ds(0, 16)]
    await_bytes(pieces, piece_recv)
    plane_first(1, False)
    ring_advance(1, 0)
    ring_step(1, 2)
    ring_advance(1, 1)
    ring_step(1, 3)
    plane_first(1, True)
    plane_first(2, False)
    ring_advance(2, 0)
    ring_advance(1, 2)
    plane_first(2, True)
    plane_head(1, 0, False)
    plane_head(1, 1, False)
    ring_advance(2, 1)
    ring_advance(1, 3)
    ring_advance(3, 0)
    ring_advance(2, 2)
    plane_advance(0)
    plane_head(1, 2, False)
    ring_advance(3, 1)
    ring_advance(2, 3)
    plane_advance(1)
    plane_head(1, 3, False)

    await_bytes(incoming.at[pl.ds(0, N_DP - 1)], tile_recv)
    every = incoming[...].reshape(BLOCK * N_DP, FEATURES)
    fetch = (block_row == BLOCK * comes + lane_row).astype(BF16)
    arrived = dot(fetch, every, ((0,), (0,)))
    cot_lane = lax.broadcasted_iota(I32, (BLOCK, BLOCK * N_DP), 1)
    cot_mine = dot((cot_lane == cot_comes).astype(BF16), every)

    def pack(rows):
        return jnp.concatenate([rows[0:4, 256 * k : 256 * (k + 1)] for k in range(4)], axis=0)

    share[...] = (pack(cot_mine) * inverse).astype(BF16)
    share_all[z] = share[...]
    along_z(
        lambda there: send(share, share_all.at[z], small_send.at[0], small_recv.at[0], (i, there))
    )
    power = jnp.mean(arrived * arrived, axis=-1, keepdims=True)
    rows = (arrived * lax.rsqrt(power + 1e-06) * gain_in_ref[...]).astype(BF16)
    normed[c] = rows
    to_twin(normed.at[c], normed.at[c], 0)

    starts, ends = [], []
    for u in range(4):
        start = jnp.int32(0)
        for b in range(N_DP):
            start = start + jnp.where(segment_ref[b] < u, TILE, 0)
        starts.append(start)
        ends.append(start + history_ref[u])

    def members(event, user, stops):
        found = jnp.zeros(event.shape, jnp.bool_)
        for u in range(4):
            found = found | ((user == u) & (event >= starts[u]) & (event < stops[u]))
        return found.astype(F32).astype(BF16)

    event = lax.broadcasted_iota(I32, (ROWS, 128), 0)
    user = lax.broadcasted_iota(I32, (ROWS, 128), 1)
    users[c] = members(event, user, ends) + members(event, user - 16, starts[1:] + [ROWS])
    to_twin(users.at[c], users.at[c], 1)
    sum_t = members(
        lax.broadcasted_iota(I32, (BLOCK, ROWS), 1),
        lax.broadcasted_iota(I32, (BLOCK, ROWS), 0),
        ends,
    )
    arrived_sum[...] = pack(dot(sum_t, arrived.astype(BF16)))

    ring_advance(3, 2)
    plane_advance(2)

    await_bytes(users.at[1 - c], twin_recv.at[1])
    await_bytes(normed.at[1 - c], twin_recv.at[0])
    shift_row = lax.broadcasted_iota(I32, (128, 128), 0)
    shift_column = lax.broadcasted_iota(I32, (128, 128), 1)
    shift = ((shift_row == shift_column + 16) & (shift_column < 4)).astype(F32).astype(BF16)
    keep = ((shift_row == shift_column) & (shift_column < 4)).astype(F32).astype(BF16)
    for dev in range(2):
        found = users[dev]
        owned = dot(found, shift).astype(BF16)
        valid = dot(found, keep).astype(BF16)
        same = dot(owned, valid, ((1,), (1,)))
        query_row = lax.broadcasted_iota(I32, (ROWS, ROWS), 0)
        key_row = lax.broadcasted_iota(I32, (ROWS, ROWS), 1)
        mask[dev] = jnp.where(key_row <= query_row, same, 0.0)
        users_t[dev] = dot(keep[0:BLOCK], found, ((1,), (1,))).astype(BF16)
        normed_t[:, ROWS * dev : ROWS * (dev + 1)] = normed[dev].T

    ring_advance(3, 3)
    plane_advance(3)

    def forward(m):
        ring_advance(4, m)
        plane_head(2, m, True)
        weight = weights[m].reshape(FEATURES, 4 * HEAD)
        for dev in range(2):
            n = 2 * m + dev
            pre = dot(normed[dev], weight)
            sig = sigmoid(pre)
            silu = pre * sig
            act_slope[n] = sig + silu * (1.0 - sig)
            act[n] = silu.astype(BF16)
        for dev in range(2):
            n = 2 * m + dev
            value = act[n, :, 128:256]
            query = act[n, :, 256:384]
            key = act[n, :, 384:512]
            scores = dot(query, key, ((1,), (1,))) * scale
            sig = sigmoid(scores)
            silu = scores * sig
            attend_slope[n] = (sig + silu * (1.0 - sig)) * (mask[dev] * scale)
            attend[n] = (silu * mask[dev]).astype(BF16)
            mixed[n] = dot(attend[n], value)

    forward(0)
    forward(1)

    await_bytes(share_all.at[pl.ds(0, N_Z - 1)], small_recv.at[0])
    shares = share_all[...].reshape(16 * N_Z, 256)
    quarter = (lax.broadcasted_iota(I32, (16 * N_Z, 1), 0) % 16) // 4
    partial = jnp.zeros((16 * N_Z, 128), F32)
    for k in range(4):
        product = dot(shares, w_out[:, 256 * k : 256 * (k + 1)], ((1,), (1,)))
        partial = partial + jnp.where(quarter == k, product, 0.0)
    fold_row = lax.broadcasted_iota(I32, (16 * N_Z, 16 * N_Z), 0)
    fold_column = lax.broadcasted_iota(I32, (16 * N_Z, 16 * N_Z), 1)
    fold = (fold_row // 16 == fold_column // 16) & (fold_row % 4 == fold_column % 4)
    folded = dot(fold.astype(F32), partial, precision=lax.Precision.HIGHEST)
    back[...] = folded.astype(BF16).reshape(N_Z, 16, 128)
    back_all[z // 2, z % 2] = back[z]
    along_z(
        lambda there: send(
            back.at[there],
            back_all.at[z // 2, z % 2],
            small_send.at[1],
            small_recv.at[1],
            (i, there),
        )
    )

    forward(2)
    forward(3)

    await_bytes(back.at[pl.ds(0, N_Z - 1)], small_recv.at[1])
    back_dev[c] = back_all[:, c]
    to_twin(back_all.at[:, 1 - c], back_dev.at[c], 2)
    sums = []
    for dev in range(2):
        total = jnp.zeros((ROWS, 1), F32)
        for m in range(4):
            total = total + jnp.sum(mixed[2 * m + dev] * mixed[2 * m + dev], axis=-1, keepdims=True)
        sums.append(total)
    await_bytes(back_dev.at[1 - c], twin_recv.at[2])

    def gain_of(m):
        return gain_out_ref[:, pl.ds(pl.multiple_of(HEAD * (2 * m + c), HEAD), HEAD)]

    stat_lane = lax.broadcasted_iota(I32, (ROWS, 128), 1)
    for dev in range(2):
        total = jnp.zeros((ROWS, 1), F32)
        for m in range(4):
            n = 2 * m + dev
            cot_rows = dot(users[dev][:, 0:16], back_dev[dev, m])
            slope = cot_rows * act[n, :, 0:128].astype(F32) * gain_of(m)
            mixed_slope[n] = slope
            gate_cot[n] = cot_rows * gain_of(m) * mixed[n]
            total = total + jnp.sum(slope * mixed[n], axis=-1, keepdims=True)
        column = jnp.where(stat_lane == 0, sums[dev], jnp.where(stat_lane == 1, total, 0.0))
        stats[:, ROWS * dev : ROWS * (dev + 1)] = column.T[0:8]
    to_twin(stats, stats_other, 3)
    await_bytes(stats_other, twin_recv.at[3])
    both_stats = jnp.concatenate(
        [stats[...] + stats_other[...], jnp.zeros((120, 2 * ROWS), F32)], axis=0
    ).T
    for dev in range(2):
        total = both_stats[ROWS * dev : ROWS * (dev + 1), 0:1]
        slope_total = both_stats[ROWS * dev : ROWS * (dev + 1), 1:2]
        norm = lax.rsqrt(total * (1.0 / FEATURES) + 1e-06)
        shared = norm * norm * norm * slope_total * (1.0 / FEATURES)
        for m in range(4):
            n = 2 * m + dev
            gated = mixed[n] * norm * gain_of(m) * act[n, :, 0:128].astype(F32)
            pool_dev[dev, m] = dot(users_t[dev], gated.astype(BF16))[0:8]
            gate_cot[n] = gate_cot[n] * norm
            mixed_cot[n] = (norm * mixed_slope[n] - shared * mixed[n]).astype(BF16)
    pool[:, c] = pool_dev[c]
    to_twin(pool_dev.at[1 - c], pool.at[:, c], 4)

    spots = [(y + away) % 4 for away in (2, 1, 3, 0)]

    def backward(k):
        m = spots[k]
        pre_cots = []
        for dev in range(2):
            n = 2 * m + dev
            value = act[n, :, 128:256]
            query = act[n, :, 256:384]
            key = act[n, :, 384:512]
            cot = mixed_cot[n]
            score_cot = (dot(cot, value, ((1,), (1,))) * attend_slope[n]).astype(BF16)
            value_cot = dot(attend[n], cot, ((0,), (0,)))
            query_cot = dot(score_cot, key)
            key_cot = dot(score_cot, query, ((0,), (0,)))
            act_cot = jnp.concatenate([gate_cot[n], value_cot, query_cot, key_cot], axis=1)
            pre_cots.append((act_cot * act_slope[n]).astype(BF16))
        grad = dot(normed_t[...], jnp.concatenate(pre_cots, axis=0)).astype(BF16)
        for b in range(4):
            held[b, m, :, 0:128, :] = grad[:, 128 * b : 128 * (b + 1)].reshape(N_Z, 128, 128)

    first_rows, z_rows = pl.ds(0, B_ROWS), pl.ds(B_ROWS, A_ROWS)
    last_rows = pl.ds(B_ROWS, STRIPE - B_ROWS)

    def exchange(src, landing, send_sem, recv_sem, device):
        sends.append(send(src, landing, send_sem, recv_sem, device))

    def collect(chunk, landing, recv_sem):
        await_bytes(landing, recv_sem)
        chunk[...] = chunk[...] + landing[...]

    def sum_z(step, k, arrive):
        for d, way in ((0, 1), (1, -1)):
            shard = (z + way * (4 - step if arrive else 5 - step) + N_Z) % N_Z
            among = pl.ds(2 * d, 2) if step == 1 else pl.ds(0, 4)
            chunk = held.at[among, spots[k], shard, z_rows]
            landing = z_in.at[d, step - 1, k, among]
            send_sem, recv_sem = sum_z_send.at[step - 1, k, d], sum_z_recv.at[step - 1, k, d]
            if arrive:
                collect(chunk, landing, recv_sem)
            else:
                exchange(chunk, landing, send_sem, recv_sem, (i, (z + way + N_Z) % N_Z))

    def sum_x(step, k, arrive):
        here, neighbours = plane_axis(False)
        for d, way in ((0, 1), (1, -1)):
            spot = (here + way * (2 - step if arrive else 3 - step) + 4) % 4
            shards = pl.ds(2 * d, 2) if step == 1 else pl.ds(0, 4)
            chunk = held.at[spot, spots[k], shards, first_rows]
            landing = plane_in_0.at[0, step - 1, d, k, shards]
            send_sem, recv_sem = sum_x_send.at[step - 1, k, d], sum_x_recv.at[step - 1, k, d]
            if arrive:
                collect(chunk, landing, recv_sem)
            else:
                exchange(chunk, landing, send_sem, recv_sem, (neighbours[d], z))

    def sum_y(step, arrive):
        here, neighbours = plane_axis(True)
        for d, way in ((0, 1), (1, -1)):
            spot = (here + way * (2 - step if arrive else 3 - step) + 4) % 4
            among = pl.ds(2 * d, 2) if step == 1 else pl.ds(0, 4)
            chunk = held.at[among, spot, pl.ds(4, 4), first_rows]
            landing = plane_in_0.at[1, step - 1, d, among]
            send_sem, recv_sem = sum_y_send.at[step - 1, d], sum_y_recv.at[step - 1, d]
            if arrive:
                collect(chunk, landing, recv_sem)
            else:
                exchange(chunk, landing, send_sem, recv_sem, (neighbours[d], z))

    def sum_second(half, step, arrive):
        here, neighbours = plane_axis(half == 0)
        for d, way in ((0, 1), (1, -1)):
            spot = (here + way * (2 - step if arrive else 3 - step) + 4) % 4
            first, count = (2 * d, 2) if step == 1 else (0, 4)
            shards = pl.ds(4 * half + first, count)
            chunk = held.at[(x, spot)[half], (spot, y)[half], shards, first_rows]
            landing = plane_in_1.at[half, step - 1, d, pl.ds(first, count)]
            send_sem = second_send.at[half, step - 1, d]
            recv_sem = second_recv.at[half, step - 1, d]
            if arrive:
                collect(chunk, landing, recv_sem)
            else:
                exchange(chunk, landing, send_sem, recv_sem, (neighbours[d], z))

    def sum_z_advance(step, k):
        sum_z(step, k, True)
        if step < 4:
            sum_z(step + 1, k, False)

    def sum_z_last(k):
        sum_z_advance(4, k)

        def send_block(n, carry):
            there = (x + n) % 4
            block = held.at[there, spots[k], z, last_rows]
            device = (8 * there + 2 * spots[k] + c, z)
            send(block, last_plane.at[i // 2], last_send.at[0], last_recv.at[0], device)
            return carry

        lax.fori_loop(0 if k < 3 else 1, 4, send_block, 0)

    def sum_x_advance(k):
        sum_x(1, k, True)
        sum_x(2, k, False)

    backward(0)
    sum_z(1, 0, False)
    sum_x(1, 0, False)
    sum_y(1, False)

    await_bytes(pool.at[:, 1 - c], twin_recv.at[4])
    pool_all[z] = pool[z // 2, z % 2]
    along_z(
        lambda there: send(
            pool.at[there // 2, there % 2],
            pool_all.at[z],
            small_send.at[2],
            small_recv.at[2],
            (i, there),
        )
    )
    backward(1)
    sum_z_advance(1, 0)
    sum_z(1, 1, False)
    sum_x_advance(0)
    sum_x(1, 1, False)

    backward(2)
    sum_z_advance(2, 0)
    sum_z_advance(1, 1)
    sum_z(1, 2, False)
    sum_x(2, 0, True)
    sum_second(0, 1, False)
    sum_x_advance(1)
    sum_x(1, 2, False)
    sum_y(1, True)
    sum_y(2, False)

    await_bytes(pool_all.at[pl.ds(0, N_Z - 1)], small_recv.at[2])
    pooled = pool_all[...]
    flat = pooled.reshape(8 * N_Z, 128)
    high = flat.astype(BF16).astype(F32)
    both = dot(jnp.concatenate([high, flat - high], axis=0).astype(BF16), w_out[...])
    products = (both[0 : 8 * N_Z] + both[8 * N_Z :]).reshape(N_Z, 8, FEATURES)
    part[...] = jnp.concatenate(
        [products[:, 0:4, 256 * k : 256 * (k + 1)] for k in range(4)], axis=1
    ).astype(BF16)
    part_all[z] = part[z]
    along_z(
        lambda there: send(
            part.at[there], part_all.at[z], small_send.at[3], small_recv.at[3], (i, there)
        )
    )
    spread = jnp.concatenate([pooled[:, 0:4]] * 4, axis=1).reshape(16 * N_Z, 128)
    for k in range(4):
        block = dot(
            share_all[...].reshape(16 * N_Z, 256),
            jnp.where(quarter == k, spread, 0.0).astype(BF16),
            ((0,), (0,)),
        )
        grad_out_t[4 * k : 4 * (k + 1)] = block.astype(BF16).reshape(4, 2, 32, 128)
    to_twin(grad_out_t.at[:, 1 - c], other_out, 5)

    backward(3)
    sum_z(1, 3, False)
    sum_x(1, 3, False)
    sum_z_advance(3, 0)
    sum_z_advance(2, 1)
    sum_z_advance(1, 2)
    sum_x(2, 1, True)
    sum_x_advance(2)
    sum_y(2, True)
    sum_second(1, 1, False)

    await_bytes(part_all.at[pl.ds(0, N_Z - 1)], small_recv.at[3])
    mean[...] = (
        (jnp.sum(part_all[...].astype(F32), axis=0) + arrived_sum[...]) * inverse
    ).astype(BF16)
    mean_all[x, y, c] = mean[...]

    def mean_along_y(k, carry):
        there = 8 * x + 2 * ((y + k) % 4) + c
        send(mean, mean_all.at[x, y, c], small_send.at[4], small_recv.at[4], (there, z))
        return carry

    def mean_along_x(k, carry):
        there = 8 * ((x + k) % 4) + 2 * y + c
        line = mean_all.at[x, :, c]
        send(line, line, small_send.at[5], small_recv.at[5], (there, z))
        return carry

    lax.fori_loop(1, 4, mean_along_y, 0)
    await_bytes(other_out, twin_recv.at[5])
    held[:, :, z, 128:STRIPE, :] = (grad_out_t[:, c] + other_out[...]).reshape(4, 4, 32, 128)

    sum_z_last(0)
    sum_z_advance(1, 3)
    sum_z_advance(3, 1)
    sum_z_advance(2, 2)
    sum_x_advance(3)
    await_bytes(mean_all.at[0, pl.ds(0, 3), 0], small_recv.at[4])
    lax.fori_loop(1, 4, mean_along_x, 0)
    sum_x(2, 2, True)
    sum_second(0, 1, True)
    sum_second(0, 2, False)
    sum_z_advance(2, 3)
    sum_second(1, 1, True)
    sum_second(1, 2, False)
    sum_z_last(1)
    sum_z_advance(3, 2)
    sum_z_advance(3, 3)
    await_bytes(mean_all.at[pl.ds(0, 3), :, 0], small_recv.at[5])
    to_twin(mean_all.at[:, :, c], mean_all.at[:, :, c], 6)
    sum_x(2, 3, True)
    sum_second(0, 2, True)
    sum_second(1, 2, True)

    along_z(
        lambda there: send(
            held.at[x, y, there, first_rows],
            last_z.at[z],
            last_send.at[1],
            last_recv.at[1],
            (i, there),
        )
    )
    last_z[z] = held[x, y, z, 0:B_ROWS]
    sum_z_last(2)
    sum_z_last(3)

    last_plane[i // 2] = held[x, y, z, B_ROWS:STRIPE]

    await_bytes(last_z.at[pl.ds(0, N_Z - 1)], last_recv.at[1])
    proj_ref[0:B_ROWS, :] = jnp.sum(last_z[...].astype(F32), axis=0)
    await_bytes(mean_all.at[:, :, 1 - c], twin_recv.at[6])
    means = mean_all[...].reshape(16 * N_DP, 256)
    mean_lane = lax.broadcasted_iota(I32, (16, 16 * N_DP), 1)
    for k in range(4):
        wanted = jnp.full((16, 1), -1, I32)
        for u in range(4):
            source = (2 * i - owners_ref[u] + 2 * N_DP) % N_DP
            wanted = jnp.where(user_row == u, 16 * source + 4 * k + u, wanted)
        chosen = dot((mean_lane == wanted).astype(BF16), means)
        pooled_ref[:, 256 * k : 256 * (k + 1)] = chosen[0:4]

    await_bytes(last_plane.at[pl.ds(0, 15)], last_recv.at[0])
    rest = jnp.sum(last_plane[...].astype(F32), axis=0)
    proj_ref[B_ROWS:128, :] = rest[0:A_ROWS]
    out_ref[...] = rest[A_ROWS:]

    for copy in sends:
        copy.wait_send()
    await_bytes(pieces, piece_send)
    await_bytes(outgoing.at[pl.ds(0, N_DP - 1)], tile_send)
    await_bytes(share_all.at[pl.ds(0, N_Z - 1)], small_send.at[0])
    await_bytes(back.at[pl.ds(0, N_Z - 1)], small_send.at[1])
    await_bytes(pool_all.at[pl.ds(0, N_Z - 1)], small_send.at[2])
    await_bytes(part.at[pl.ds(0, N_Z - 1)], small_send.at[3])
    await_bytes(mean_all.at[0, pl.ds(0, 3), 0], small_send.at[4])
    await_bytes(mean_all.at[pl.ds(0, 3), :, 0], small_send.at[5])
    await_bytes(last_plane.at[pl.ds(0, 15)], last_send.at[0])
    await_bytes(last_z.at[pl.ds(0, N_Z - 1)], last_send.at[1])


def finish_kernel(pooled_in, proj_in, out_in, pooled_ref, proj_ref, out_ref):
    pooled_ref[...] = pooled_in[...]
    proj_ref[...] = proj_in[...]
    out_ref[...] = out_in[...]


def body(events, gain_in, gain_out, w_proj, w_out, target, segment, history, owners, pooled_cot):
    any_space, vmem = pl.BlockSpec(memory_space=pl.ANY), pl.BlockSpec(memory_space=pltpu.VMEM)
    smem = pl.BlockSpec(memory_space=pltpu.SMEM)
    dma = pltpu.SemaphoreType.DMA

    def bf16(*shape):
        return pltpu.VMEM(shape, BF16)

    def f32(*shape):
        return pltpu.VMEM(shape, F32)

    pooled, grad_proj, grad_out_t = pl.pallas_call(
        kernel,
        out_shape=(
            jax.ShapeDtypeStruct((4, FEATURES), F32),
            jax.ShapeDtypeStruct((128, 128), F32),
            jax.ShapeDtypeStruct((32, 128), F32),
        ),
        in_specs=[smem] * 4 + [vmem] * 3 + [any_space] * 3,
        out_specs=(vmem, vmem, vmem),
        scratch_shapes=[
            bf16(ROWS, FEATURES),
            bf16(128, FEATURES),
            bf16(N_DP, BLOCK, FEATURES),
            bf16(N_DP, BLOCK, FEATURES),
            f32(128, FEATURES),
            bf16(4, N_Z, 128, 4 * HEAD),
            f32(16, 256),
            bf16(2, ROWS, FEATURES),
            bf16(FEATURES, 2 * ROWS),
            bf16(HEADS, ROWS, 4 * HEAD),
            f32(HEADS, ROWS, 4 * HEAD),
            bf16(HEADS, ROWS, ROWS),
            f32(HEADS, ROWS, ROWS),
            f32(HEADS, ROWS, HEAD),
            f32(HEADS, ROWS, HEAD),
            bf16(HEADS, ROWS, HEAD),
            f32(HEADS, ROWS, HEAD),
            bf16(2, ROWS, 128),
            bf16(2, BLOCK, ROWS),
            f32(2, ROWS, ROWS),
            bf16(16, 256),
            bf16(N_Z, 16, 256),
            bf16(N_Z, 16, 128),
            bf16(4, 2, 16, 128),
            bf16(2, 4, 16, 128),
            f32(8, 2 * ROWS),
            f32(8, 2 * ROWS),
            f32(2, 4, 8, 128),
            f32(4, 2, 8, 128),
            f32(N_Z, 8, 128),
            bf16(N_Z, 16, 256),
            bf16(N_Z, 16, 256),
            bf16(16, 256),
            bf16(4, 4, 2, 16, 256),
            bf16(4, 4, N_Z, STRIPE, 128),
            bf16(16, 2, 32, 128),
            bf16(16, 32, 128),
            bf16(2, 4, 4, 4, A_ROWS, 128),
            bf16(2, 2, 2, 4, 4, B_ROWS, 128),
            bf16(2, 2, 2, 4, B_ROWS, 128),
            bf16(N_Z, B_ROWS, 128),
            bf16(16, STRIPE - B_ROWS, 128),
            dma((3,)),
            dma,
            dma,
            dma,
            dma,
            dma((4, 4, 2)),
            dma((4, 4, 2)),
            dma((2, 2, 2)),
            dma((2, 2, 2)),
            dma((2, 4, 2, 2)),
            dma((2, 4, 2, 2)),
            dma((7,)),
            dma((7,)),
            dma((6,)),
            dma((6,)),
            dma((4, 4, 2)),
            dma((4, 4, 2)),
            dma((2, 4, 2)),
            dma((2, 4, 2)),
            dma((2, 2)),
            dma((2, 2)),
            dma((2, 2, 2)),
            dma((2, 2, 2)),
            dma((2,)),
            dma((2,)),
        ],
        compiler_params=pltpu.CompilerParams(
            collective_id=0, has_side_effects=True, vmem_limit_bytes=62 * 2**20
        ),
        name="step",
    )(
        target,
        owners,
        segment,
        history,
        gain_in.reshape(1, FEATURES),
        gain_out.reshape(1, FEATURES),
        pooled_cot,
        events,
        w_proj,
        w_out,
    )
    pooled, grad_proj, grad_out_t = pl.pallas_call(
        finish_kernel,
        out_shape=(
            jax.ShapeDtypeStruct((4, FEATURES), F32),
            jax.ShapeDtypeStruct((128, 128), F32),
            jax.ShapeDtypeStruct((32, 128), F32),
        ),
        in_specs=[vmem] * 3,
        out_specs=(vmem, vmem, vmem),
        name="finish",
    )(pooled, grad_proj, grad_out_t)
    return (pooled, grad_proj, grad_out_t.T)


def solution(mesh):
    in_specs = (
        P(("dp", "fsdp"), None),
        P(),
        P(),
        P("fsdp", None),
        P("fsdp", None),
        P(("dp", "fsdp")),
        P(("dp", "fsdp")),
        P(("dp", "fsdp")),
        P(("dp", "fsdp")),
        P(("dp", "fsdp"), None),
    )
    out_specs = (P(("dp", "fsdp"), None), P("fsdp", "dp"), P("fsdp", "dp"))
    return jax.shard_map(body, mesh=mesh, in_specs=in_specs, out_specs=out_specs, check_vma=False)
```
